32 devices in a mesh: lon: 4 (over y, x), batch: 8 (over z, core).
Axes of the slice: x: 2, y: 2, z: 4, core: 2. Of those that a mesh axis runs over, the one named last changes fastest.
Arguments:
- frames: bfloat16 [32, 32, 32, 256], P('batch', None, 'lon'), may hold values from -6 to 6
- latent_init: bfloat16 [32, 32, 32, 32], P('batch', None, 'lon'), may hold values from -0.8984375 to 0.8984375
- crop_band: int32 [32, 2], P('batch'), may hold values from 0 to 32, as said below
- cotangent: bfloat16 [32, 32, 32, 256], P('batch', None, 'lon'), may hold values from -6 to 6
- triple_weight: float32 [2, 256, 768], replicated, may hold values from -0.375 to 0.375
- triple_moment: float32 [2, 256, 768], replicated, may hold values from -0.75 to 0.75
- triple_average: float32 [2, 256, 768], replicated, may hold values from -0.375 to 0.375
- output_weight: float32 [2, 256, 256], replicated, may hold values from -1 to 1
- output_moment: float32 [2, 256, 256], replicated, may hold values from -0.75 to 0.75
- output_average: float32 [2, 256, 256], replicated, may hold values from -1 to 1
- expand_weight: float32 [2, 256, 1024], replicated, may hold values from -0.375 to 0.375
- expand_moment: float32 [2, 256, 1024], replicated, may hold values from -0.75 to 0.75
- expand_average: float32 [2, 256, 1024], replicated, may hold values from -0.375 to 0.375
- shrink_weight: float32 [2, 1024, 256], replicated, may hold values from -0.1875 to 0.1875
- shrink_moment: float32 [2, 1024, 256], replicated, may hold values from -0.75 to 0.75
- shrink_average: float32 [2, 1024, 256], replicated, may hold values from -0.1875 to 0.1875
- recurrent_weight: float32 [2, 288, 32], replicated, may hold values from -0.375 to 0.375
- recurrent_moment: float32 [2, 288, 32], replicated, may hold values from -0.75 to 0.75
- recurrent_average: float32 [2, 288, 32], replicated, may hold values from -0.375 to 0.375
- readout_weight: float32 [2, 32, 256], replicated, may hold values from -1 to 1
- readout_moment: float32 [2, 32, 256], replicated, may hold values from -0.75 to 0.75
- readout_average: float32 [2, 32, 256], replicated, may hold values from -1 to 1
- gains_weight: float32 [2, 3, 256], replicated, may hold values from 0.5 to 1.5
- gains_moment: float32 [2, 3, 256], replicated, may hold values from -1.5 to 1.5
- gains_average: float32 [2, 3, 256], replicated, may hold values from 0.5 to 1.5
- table_weight: float32 [2, 8, 225], replicated, may hold values from -3 to 3
- table_moment: float32 [2, 8, 225], replicated, may hold values from -1.5 to 1.5
- table_average: float32 [2, 8, 225], replicated, may hold values from -3 to 3
Outputs:
- activations: bfloat16 [32, 32, 32, 256], P('batch', None, 'lon')
- input_grad: float32 [32, 32, 32, 256], P('batch', None, 'lon')
- triple_updated: float32 [2, 256, 768], replicated
- triple_velocity: float32 [2, 256, 768], replicated
- triple_smoothed: float32 [2, 256, 768], replicated
- output_updated: float32 [2, 256, 256], replicated
- output_velocity: float32 [2, 256, 256], replicated
- output_smoothed: float32 [2, 256, 256], replicated
- expand_updated: float32 [2, 256, 1024], replicated
- expand_velocity: float32 [2, 256, 1024], replicated
- expand_smoothed: float32 [2, 256, 1024], replicated
- shrink_updated: float32 [2, 1024, 256], replicated
- shrink_velocity: float32 [2, 1024, 256], replicated
- shrink_smoothed: float32 [2, 1024, 256], replicated
- recurrent_updated: float32 [2, 288, 32], replicated
- recurrent_velocity: float32 [2, 288, 32], replicated
- recurrent_smoothed: float32 [2, 288, 32], replicated
- readout_updated: float32 [2, 32, 256], replicated
- readout_velocity: float32 [2, 32, 256], replicated
- readout_smoothed: float32 [2, 32, 256], replicated
- gains_updated: float32 [2, 3, 256], replicated
- gains_velocity: float32 [2, 3, 256], replicated
- gains_smoothed: float32 [2, 3, 256], replicated
- table_updated: float32 [2, 8, 225], replicated
- table_velocity: float32 [2, 8, 225], replicated
- table_smoothed: float32 [2, 8, 225], replicated
The draws below stay inside these ranges and needn't reach their ends.
Inputs may be any that keep to these rules, and one draw needn't show every extreme that they name: Frames of even index are whole: crop_band is 0 and 32. For the others the first valid row is at most 8 and the end at least 24.
All inputs are finite; a program needn't handle non-finite values.
Results may differ from the reference program's by a relative error of at most 0.018.
Values may be sent and summed in bfloat16 or wider, within the bound.
A program may use at most 192 MiB of HBM per device.

```python
import jax
import jax.numpy as jnp
from jax import lax

WIDTH = 256
HEADS = 8
HIDDEN_SIZE = 1024
LATENT = 32
WINDOW = 8
LAYERS = 2
ROWS = 32
PAIRS = 225
FRAMES = 32
COLS = 32
TOKENS = 32768


def draw_crop_band(key, part):
    key = jax.random.fold_in(key, 7)
    start_key, final_key = jax.random.split(key)
    starts = jax.random.randint(start_key, (FRAMES,), 0, ROWS // 4 + 1)
    finals = jax.random.randint(final_key, (FRAMES,), 3 * ROWS // 4, ROWS + 1)
    entire = jnp.arange(FRAMES) % 2 == 0
    starts = jnp.where(entire, 0, starts)
    finals = jnp.where(entire, ROWS, finals)
    return jnp.stack([starts, finals], axis=1).astype(jnp.int32)


def block_levels(own_key, shape, cuts, smallest, high):
    gain = 1.0
    for position, blocks in cuts:
        draws = jax.random.uniform(jax.random.fold_in(jax.random.fold_in(own_key, 6), position), (blocks,), jnp.float32, smallest / len(cuts), high / len(cuts))
        gain = gain * jnp.repeat(jnp.exp(draws), shape[position] // blocks).reshape((-1,) + (1,) * (len(shape) - 1 - position))
    return gain


def centred(rng, dims, width, bound, cuts=(), kind=jnp.bfloat16):
    values = jax.random.normal(rng, dims, jnp.float32) * width
    if len(cuts) > 0:
        values = block_levels(rng, dims, cuts, -0.22, 0.18) * values
    return jnp.clip(values, min=-bound, max=bound).astype(kind)


def setup_inputs(seed: int = 0) -> dict:
    streams_of = jax.random.split(jax.random.key(seed), 29)
    frames = centred(streams_of[0], (FRAMES, ROWS, COLS, WIDTH), 1.0, 6.0, ((0, 8), (2, 4)))
    latent_init = jnp.clip(jax.random.uniform(streams_of[1], (FRAMES, ROWS, COLS, LATENT), jnp.float32, -0.8984375, 0.8984375) * block_levels(streams_of[1], (FRAMES, ROWS, COLS, LATENT), ((0, 8), (2, 4)), -0.4, 0.0), -0.8984375, 0.8984375).astype(jnp.bfloat16)
    crop_band = draw_crop_band(jax.random.fold_in(streams_of[28], 71), 0)
    cotangent = centred(streams_of[3], (FRAMES, ROWS, COLS, WIDTH), 1.0, 6.0, ((0, 8), (2, 4)))
    triple_weight = centred(streams_of[4], (LAYERS, WIDTH, 3 * WIDTH), WIDTH ** -0.5, 0.375, (), jnp.float32)
    triple_moment = centred(streams_of[5], (LAYERS, WIDTH, 3 * WIDTH), 0.05, 0.75, (), jnp.float32)
    triple_average = centred(streams_of[6], (LAYERS, WIDTH, 3 * WIDTH), WIDTH ** -0.5, 0.375, (), jnp.float32)
    output_weight = centred(streams_of[7], (LAYERS, WIDTH, WIDTH), (WIDTH // 8) ** -0.5, 1.0, (), jnp.float32)
    output_moment = centred(streams_of[8], (LAYERS, WIDTH, WIDTH), 0.05, 0.75, (), jnp.float32)
    output_average = centred(streams_of[9], (LAYERS, WIDTH, WIDTH), (WIDTH // 8) ** -0.5, 1.0, (), jnp.float32)
    expand_weight = centred(streams_of[10], (LAYERS, WIDTH, HIDDEN_SIZE), WIDTH ** -0.5, 0.375, (), jnp.float32)
    expand_moment = centred(streams_of[11], (LAYERS, WIDTH, HIDDEN_SIZE), 0.05, 0.75, (), jnp.float32)
    expand_average = centred(streams_of[12], (LAYERS, WIDTH, HIDDEN_SIZE), WIDTH ** -0.5, 0.375, (), jnp.float32)
    shrink_weight = centred(streams_of[13], (LAYERS, HIDDEN_SIZE, WIDTH), HIDDEN_SIZE ** -0.5, 0.1875, (), jnp.float32)
    shrink_moment = centred(streams_of[14], (LAYERS, HIDDEN_SIZE, WIDTH), 0.05, 0.75, (), jnp.float32)
    shrink_average = centred(streams_of[15], (LAYERS, HIDDEN_SIZE, WIDTH), HIDDEN_SIZE ** -0.5, 0.1875, (), jnp.float32)
    recurrent_weight = centred(streams_of[16], (LAYERS, WIDTH + LATENT, LATENT), (WIDTH + LATENT) ** -0.5, 0.375, (), jnp.float32)
    recurrent_moment = centred(streams_of[17], (LAYERS, WIDTH + LATENT, LATENT), 0.05, 0.75, (), jnp.float32)
    recurrent_average = centred(streams_of[18], (LAYERS, WIDTH + LATENT, LATENT), (WIDTH + LATENT) ** -0.5, 0.375, (), jnp.float32)
    readout_weight = centred(streams_of[19], (LAYERS, LATENT, WIDTH), LATENT ** -0.5, 1.0, (), jnp.float32)
    readout_moment = centred(streams_of[20], (LAYERS, LATENT, WIDTH), 0.05, 0.75, (), jnp.float32)
    readout_average = centred(streams_of[21], (LAYERS, LATENT, WIDTH), LATENT ** -0.5, 1.0, (), jnp.float32)
    gains_weight = jnp.clip(1.0 + 0.1 * jax.random.normal(streams_of[22], (LAYERS, 3, WIDTH), jnp.float32), 0.5, 1.5)
    gains_moment = centred(streams_of[23], (LAYERS, 3, WIDTH), 0.1, 1.5, (), jnp.float32)
    gains_average = jnp.clip(1.0 + 0.1 * jax.random.normal(streams_of[24], (LAYERS, 3, WIDTH), jnp.float32), 0.5, 1.5)
    table_weight = centred(streams_of[25], (LAYERS, HEADS, PAIRS), 0.5, 3.0, (), jnp.float32)
    table_moment = centred(streams_of[26], (LAYERS, HEADS, PAIRS), 0.1, 1.5, (), jnp.float32)
    table_average = centred(streams_of[27], (LAYERS, HEADS, PAIRS), 0.5, 3.0, (), jnp.float32)
    return {"frames": frames, "latent_init": latent_init, "crop_band": crop_band, "cotangent": cotangent, "triple_weight": triple_weight, "triple_moment": triple_moment, "triple_average": triple_average, "output_weight": output_weight, "output_moment": output_moment, "output_average": output_average, "expand_weight": expand_weight, "expand_moment": expand_moment, "expand_average": expand_average, "shrink_weight": shrink_weight, "shrink_moment": shrink_moment, "shrink_average": shrink_average, "recurrent_weight": recurrent_weight, "recurrent_moment": recurrent_moment, "recurrent_average": recurrent_average, "readout_weight": readout_weight, "readout_moment": readout_moment, "readout_average": readout_average, "gains_weight": gains_weight, "gains_moment": gains_moment, "gains_average": gains_average, "table_weight": table_weight, "table_moment": table_moment, "table_average": table_average}


@jax.custom_vjp
def low(v):
    return lax.optimization_barrier(v.astype(jnp.bfloat16)).astype(jnp.float32)

@jax.custom_vjp
def low_back(v):
    return v

def low_keep(v):
    return (low(v), None)

def low_pass(kept, grad):
    return (grad,)

def back_keep(v):
    return (v, None)

def back_low(kept, grad):
    return (low(grad),)
low.defvjp(low_keep, low_pass)
low_back.defvjp(back_keep, back_low)
learn_rate = 0.2
momentum_rate = 0.9
average_decay = 0.5
norm_eps = 1e-05
mask_fill = -100.0
highest = lax.Precision.HIGHEST

def layer_norm(stream, gain_row):
    center = stream - lax.optimization_barrier(jnp.mean(stream, axis=-1, keepdims=True))
    inverse = lax.rsqrt(lax.optimization_barrier(jnp.mean(center * center, axis=-1, keepdims=True)) + norm_eps)
    return center * inverse * gain_row

def gelu_tanh(preact):
    return jax.nn.gelu(preact, approximate=True)

def windowize(tensor):
    row_count, col_count, channels = tensor.shape
    tensor = tensor.reshape(row_count // WINDOW, WINDOW, col_count // WINDOW, WINDOW, channels)
    return tensor.transpose(0, 2, 1, 3, 4).reshape(-1, WINDOW * WINDOW, channels)

def unwindowize(tensor, row_count, col_count):
    channels = tensor.shape[-1]
    tensor = tensor.reshape(row_count // WINDOW, col_count // WINDOW, WINDOW, WINDOW, channels)
    return tensor.transpose(0, 2, 1, 3, 4).reshape(row_count, col_count, channels)

def offset_index():
    coords = jnp.arange(WINDOW * WINDOW, dtype=jnp.int32)
    row_of = coords // WINDOW
    col_of = coords % WINDOW
    return (row_of[:, None] - row_of[None, :] + WINDOW - 1) * (2 * WINDOW - 1) + col_of[:, None] - col_of[None, :] + WINDOW - 1

def attention_mask(crop_rows, shifted, row_count, col_count):
    row_ids = jnp.arange(row_count, dtype=jnp.int32)
    half_window = WINDOW // 2
    if shifted:
        source = (row_ids + half_window) % row_count
        region = (row_ids >= row_count - WINDOW).astype(jnp.int32) + (row_ids >= row_count - half_window).astype(jnp.int32)
    else:
        source = row_ids
        region = jnp.zeros_like(row_ids)
    in_crop = ((source >= crop_rows[0]) & (source < crop_rows[1])).astype(jnp.int32)
    crop_grid = jnp.broadcast_to(in_crop[:, None, None], (row_count, col_count, 1))
    region_grid = jnp.broadcast_to(region[:, None, None], (row_count, col_count, 1))
    crop_win = windowize(crop_grid)[:, :, 0]
    region_win = windowize(region_grid)[:, :, 0]
    allowed = (crop_win[:, None, :] > 0) & (region_win[:, :, None] == region_win[:, None, :])
    return jnp.where(allowed, 0.0, mask_fill).astype(jnp.float32)

def swin_layer(stream, latent, weights, crop_rows, shifted):
    triple, output, expand, shrink, recurrent, readout, gain_rows, bias_table = weights
    row_count, col_count, features = stream.shape
    head_count = bias_table.shape[0]
    head_width = features // head_count
    half_window = WINDOW // 2
    normed = layer_norm(stream, gain_rows[0])
    if shifted:
        normed = jnp.roll(normed, (-half_window, -half_window), axis=(0, 1))
        normed = low_back(low(normed))
    else:
        normed = low(normed)
    packed = low_back(low(jnp.dot(normed, low(triple), precision=highest)))
    windows = windowize(packed)
    window_count = windows.shape[0]
    split_heads = windows.reshape(window_count, WINDOW * WINDOW, 3, head_count, head_width)
    queries = split_heads[:, :, 0]
    key_heads = split_heads[:, :, 1]
    value_heads = split_heads[:, :, 2]
    scores = jnp.einsum('wqhd,wkhd->whqk', queries, key_heads, precision=highest) * head_width ** (-0.5)
    scores = scores + bias_table[:, offset_index()][None] + attention_mask(crop_rows, shifted, row_count, col_count)[:, None]
    scores = low_back(scores)
    row_max = lax.optimization_barrier(jnp.max(scores, axis=-1, keepdims=True))
    exponent = jnp.exp(scores - row_max)
    attn_probs = low(exponent / lax.optimization_barrier(jnp.sum(exponent, axis=-1, keepdims=True)))
    context = jnp.einsum('whqk,wkhd->wqhd', attn_probs, value_heads, precision=highest)
    context = unwindowize(low(context.reshape(window_count, WINDOW * WINDOW, features)), row_count, col_count)
    if shifted:
        context = jnp.roll(context, (half_window, half_window), axis=(0, 1))
    context = low_back(context)
    stream = stream + low_back(jnp.dot(context, low(output), precision=highest))
    cell_in = jnp.concatenate([low(layer_norm(stream, gain_rows[2])), latent], axis=-1)
    preact = low_back(jnp.dot(cell_in, low(recurrent), precision=highest))
    latent = low(jnp.tanh(preact))
    stream = stream + low_back(jnp.dot(latent, low(readout), precision=highest))
    hidden = low(layer_norm(stream, gain_rows[1]))
    inner_pre = low_back(jnp.dot(hidden, low(expand), precision=highest))
    activated = low(gelu_tanh(inner_pre))
    stream = stream + low_back(jnp.dot(activated, low(shrink), precision=highest))
    return (stream, latent)

def frame_pass(params, frame, latent, crop_rows):
    stream = frame
    for layer_index in range(LAYERS):
        layer_weights = tuple((parameter[layer_index] for parameter in params))
        stream, latent = swin_layer(stream, latent, layer_weights, crop_rows, layer_index % 2 == 1)
    return stream

def update(weight, moment, average, gradient):
    gradient = gradient * TOKENS ** (-0.5)
    velocity = momentum_rate * moment + gradient
    updated = weight - learn_rate * (gradient + momentum_rate * velocity)
    smoothed = average_decay * average + (1.0 - average_decay) * updated
    return (updated, velocity, smoothed)

def reference(frames, latent_init, crop_band, cotangent, triple_weight, triple_moment, triple_average, output_weight, output_moment, output_average, expand_weight, expand_moment, expand_average, shrink_weight, shrink_moment, shrink_average, recurrent_weight, recurrent_moment, recurrent_average, readout_weight, readout_moment, readout_average, gains_weight, gains_moment, gains_average, table_weight, table_moment, table_average):
    params = (triple_weight, output_weight, expand_weight, shrink_weight, recurrent_weight, readout_weight, gains_weight, table_weight)
    stream = frames.astype(jnp.float32)
    latent = latent_init.astype(jnp.float32)

    def forward(params, stream):
        frame_step = jax.checkpoint(lambda member: frame_pass(params, member[0], member[1], member[2]))
        return lax.map(frame_step, (stream, latent, crop_band))
    result, pullback = jax.vjp(forward, params, stream)
    grads, input_grad = pullback(cotangent.astype(jnp.float32))
    triple_updated, triple_velocity, triple_smoothed = update(triple_weight, triple_moment, triple_average, grads[0])
    output_updated, output_velocity, output_smoothed = update(output_weight, output_moment, output_average, grads[1])
    expand_updated, expand_velocity, expand_smoothed = update(expand_weight, expand_moment, expand_average, grads[2])
    shrink_updated, shrink_velocity, shrink_smoothed = update(shrink_weight, shrink_moment, shrink_average, grads[3])
    recurrent_updated, recurrent_velocity, recurrent_smoothed = update(recurrent_weight, recurrent_moment, recurrent_average, grads[4])
    readout_updated, readout_velocity, readout_smoothed = update(readout_weight, readout_moment, readout_average, grads[5])
    gains_updated, gains_velocity, gains_smoothed = update(gains_weight, gains_moment, gains_average, grads[6])
    table_updated, table_velocity, table_smoothed = update(table_weight, table_moment, table_average, grads[7])
    return (result.astype(jnp.bfloat16), input_grad, triple_updated, triple_velocity, triple_smoothed, output_updated, output_velocity, output_smoothed, expand_updated, expand_velocity, expand_smoothed, shrink_updated, shrink_velocity, shrink_smoothed, recurrent_updated, recurrent_velocity, recurrent_smoothed, readout_updated, readout_velocity, readout_smoothed, gains_updated, gains_velocity, gains_smoothed, table_updated, table_velocity, table_smoothed)
```

```python
import functools

import jax
import jax.numpy as jnp
from jax import lax
from jax.experimental import pallas as pl
from jax.experimental.pallas import tpu as pltpu
from jax.sharding import PartitionSpec as P

WINDOW = 8
HALF = WINDOW // 2
SPAN = WINDOW * WINDOW
HEADS = 8
LANES = 128
LAYERS = 2
WIDTH = 256
HIDDEN = 1024
LATENT = 32
OFFSETS = 2 * WINDOW - 1
PAIRS = OFFSETS * OFFSETS

LEARN_RATE = 0.2
MOMENTUM_RATE = 0.9
AVERAGE_DECAY = 0.5
NORM_EPS = 1e-05
MASK_FILL = -100.0
HEAD_WIDTH = WIDTH // HEADS
HEADS_A_HALF = LANES // HEAD_WIDTH
SCALE = HEAD_WIDTH ** (-0.5)
GELU_C = 0.7978845608028654
GELU_A = 0.044715

F32 = jnp.float32
BF16 = jnp.bfloat16
MESH = pl.DeviceIdType.MESH

SMALL_ROWS = 256
SHRINK_AT, EXPAND_AT, OUTPUT_AT, TRIPLE_AT, SMALL_AT, GRAD_ROWS = (
    (4096 + 2048, 0),
    (4096 + 2048 + 2048, 2048),
    (4096 + 2048 + 4096, 4096),
    (4096 + 2048 + 4096 + 512, 4096 + 512),
    (4096 + 2048 + 4096 + 2048, 4096 + 2048 + 4096 + 2048 + SMALL_ROWS),
    4096 + 2048 + 4096 + 2048 + 2 * SMALL_ROWS,
)


def dot(a, b):
    return jnp.dot(a, b, preferred_element_type=F32)


def dot_nt(a, b):
    return lax.dot_general(a, b, (((1,), (1,)), ((), ())), preferred_element_type=F32)


def dot_tn(a, b):
    return lax.dot_general(a, b, (((0,), (0,)), ((), ())), preferred_element_type=F32)


def norm_parts(stream):
    center = stream - jnp.mean(stream, axis=-1, keepdims=True)
    inverse = lax.rsqrt(jnp.mean(center * center, axis=-1, keepdims=True) + NORM_EPS)
    return center * inverse, inverse


def norm_back(upstream, gain_row, scaled, inverse):
    product = upstream * scaled
    rows, features = product.shape
    gain_part = jnp.sum(product.reshape(rows // 8, 8, features), axis=0)
    weighted = upstream * gain_row
    along = jnp.mean(product * gain_row, axis=-1, keepdims=True)
    inner = weighted - jnp.mean(weighted, axis=-1, keepdims=True) - scaled * along
    return gain_part, inverse * inner


def lower_slots(shape):
    return lax.broadcasted_iota(jnp.int32, shape, 1) < HALF


def pack_half(own):
    tokens, features = own.shape
    rows = own.reshape(tokens // WINDOW, WINDOW, features)
    count = tokens // WINDOW // 2
    moved = pltpu.roll(rows[count:], HALF, axis=1)
    return jnp.where(lower_slots(moved.shape), rows[:count], moved).reshape(tokens // 2, features)


def unpack_half(packed, own):
    tokens, features = own.shape
    pairs = packed.reshape(tokens // WINDOW // 2, WINDOW, features)
    full = jnp.concatenate([pairs, pltpu.roll(pairs, HALF, axis=1)], axis=0)
    rows = own.reshape(tokens // WINDOW, WINDOW, features)
    return jnp.where(lower_slots(full.shape), full, rows).reshape(tokens, features)


def rows_ahead(value):
    cut = HALF * WINDOW
    return jnp.concatenate([value[cut:], value[:cut]], axis=0)


def rows_behind(value):
    cut = value.shape[0] - HALF * WINDOW
    return jnp.concatenate([value[cut:], value[:cut]], axis=0)


def head_of_lane(shape):
    return lax.broadcasted_iota(jnp.int32, shape, 1) // HEAD_WIDTH


def spread_heads(block):
    lane_head = head_of_lane(block.shape)
    zero = jnp.zeros_like(block)
    return jnp.concatenate(
        [jnp.where(lane_head == head, block, zero) for head in range(HEADS_A_HALF)], axis=0
    )


def gather_heads(stacked):
    count = stacked.shape[0] // HEADS_A_HALF
    lane_head = head_of_lane((count, LANES))
    out = stacked[:count]
    for head in range(1, HEADS_A_HALF):
        out = jnp.where(lane_head == head, stacked[head * count : (head + 1) * count], out)
    return out


def half_lanes(half):
    return slice(half * LANES, (half + 1) * LANES)


def half_scores(half):
    return slice(half * HEADS_A_HALF * SPAN, (half + 1) * HEADS_A_HALF * SPAN)


def score_mask(crop_start, crop_end, shifted, window, row_count):
    shape = (SPAN, HEADS_A_HALF * SPAN)
    key_row = lax.broadcasted_iota(jnp.int32, shape, 0) // WINDOW
    source = key_row + window * WINDOW
    if shifted:
        source = source + HALF
        if window == row_count // WINDOW - 1:
            source = jnp.where(source >= row_count, source - row_count, source)
    allowed = (source >= crop_start) & (source < crop_end)
    if shifted and window == row_count // WINDOW - 1:
        query_row = lax.broadcasted_iota(jnp.int32, shape, 1) % SPAN // WINDOW
        allowed = allowed & ((key_row < HALF) == (query_row < HALF))
    return jnp.where(allowed, 0.0, MASK_FILL).astype(F32)


def offset_onehot(shifted):
    shape = (WIDTH, WINDOW * LANES)
    lane = lax.broadcasted_iota(jnp.int32, shape, 1)
    key_col = lane // LANES
    row_offset = lane % LANES // WINDOW
    query_col = lane % WINDOW
    if shifted:
        key_col = (key_col + HALF) % WINDOW
        query_col = (query_col + HALF) % WINDOW
    target = row_offset * OFFSETS + query_col - key_col + WINDOW - 1
    target = jnp.where(row_offset < OFFSETS, target, -1)
    pair = lax.broadcasted_iota(jnp.int32, shape, 0)
    return jnp.where(pair == target, 1.0, 0.0).astype(BF16)


def three_parts(value):
    high = value.astype(BF16)
    rest = value - high.astype(F32)
    middle = rest.astype(BF16)
    low = (rest - middle.astype(F32)).astype(BF16)
    return jnp.concatenate([high.astype(F32), middle.astype(F32), low.astype(F32)], axis=0).astype(BF16)


def swap_groups(tiles):
    return [jnp.concatenate([tile[b : b + 1] for tile in tiles], axis=0) for b in range(8)]


def bias_of_table(table, onehot):
    spread = dot(three_parts(table), onehot)
    spread = spread[:HEADS] + (spread[HEADS : 2 * HEADS] + spread[2 * HEADS :])
    tiles = swap_groups([spread[:, col * LANES : (col + 1) * LANES] for col in range(WINDOW)])
    lane = lax.broadcasted_iota(jnp.int32, (WINDOW, LANES), 1)
    blocks = []
    for key_row in range(WINDOW):
        back = (WINDOW - 1 - key_row) * WINDOW
        pieces = []
        for pair in range(HEADS // 2):
            even = pltpu.roll(tiles[2 * pair], (LANES - back) % LANES, axis=1)
            odd = pltpu.roll(tiles[2 * pair + 1], (LANES + SPAN - back) % LANES, axis=1)
            pieces.append(jnp.where(lane < SPAN, even, odd))
        blocks.append(jnp.concatenate(pieces, axis=1))
    return jnp.concatenate(blocks, axis=0)


def table_of_bias(gathered, onehot):
    lane = lax.broadcasted_iota(jnp.int32, (WINDOW, LANES), 1)
    zero = jnp.zeros((WINDOW, LANES), F32)
    tiles = []
    for head in range(HEADS):
        total = None
        for key_row in range(WINDOW):
            forth = (WINDOW - 1 - key_row) * WINDOW
            block = gathered[key_row * WINDOW : (key_row + 1) * WINDOW, half_lanes(head // 2)]
            if head % 2 == 0:
                moved = pltpu.roll(jnp.where(lane < SPAN, block, zero), forth, axis=1)
            else:
                moved = pltpu.roll(jnp.where(lane < SPAN, zero, block), (forth + SPAN) % LANES, axis=1)
            total = moved if total is None else total + moved
        tiles.append(total)
    spread = jnp.concatenate(swap_groups(tiles), axis=1)
    parts = dot_nt(three_parts(spread), onehot)
    return parts[:HEADS] + (parts[HEADS : 2 * HEADS] + parts[2 * HEADS :])


def attend_forward(qkv, bias_ref, layer, crop, probs_ref, frame, row_count):
    shifted = layer % 2 == 1
    windows = []
    for window in range(row_count // WINDOW):
        rows = slice(window * SPAN, (window + 1) * SPAN)
        mask = score_mask(crop[0], crop[1], shifted, window, row_count)
        halves = []
        for half in range(2):
            queries = qkv[rows, half * LANES : (half + 1) * LANES]
            keys = qkv[rows, WIDTH + half * LANES : WIDTH + (half + 1) * LANES]
            values = qkv[rows, 2 * WIDTH + half * LANES : 2 * WIDTH + (half + 1) * LANES]
            scores = dot_nt(keys, spread_heads(queries)) * SCALE
            scores = scores + bias_ref[layer, :, half_scores(half)] + mask
            exponent = jnp.exp(scores - jnp.max(scores, axis=0, keepdims=True))
            probs = exponent * (1.0 / jnp.sum(exponent, axis=0, keepdims=True))
            probs = probs.astype(BF16)
            at = (frame * (row_count // WINDOW) + window) * SPAN
            probs_ref[layer, pl.ds(pl.multiple_of(at, SPAN), SPAN), half_scores(half)] = probs
            halves.append(gather_heads(dot_tn(probs, values)))
        windows.append(jnp.concatenate(halves, axis=1))
    return jnp.concatenate(windows, axis=0)


def attend_backward(qkv, dcontext, layer, probs_ref, frame, gathered_ref, row_count):
    parts = []
    for window in range(row_count // WINDOW):
        rows = slice(window * SPAN, (window + 1) * SPAN)
        dqs, dks, dvs = [], [], []
        for half in range(2):
            queries = qkv[rows, half * LANES : (half + 1) * LANES]
            keys = qkv[rows, WIDTH + half * LANES : WIDTH + (half + 1) * LANES]
            values = qkv[rows, 2 * WIDTH + half * LANES : 2 * WIDTH + (half + 1) * LANES]
            dcs = spread_heads(dcontext[rows, half_lanes(half)])
            at = (frame * (row_count // WINDOW) + window) * SPAN
            low = probs_ref[layer, pl.ds(pl.multiple_of(at, SPAN), SPAN), half_scores(half)]
            probs = low.astype(F32)
            dvs.append(dot(low, dcs))
            dprobs = dot_nt(values, dcs)
            dscores = probs * (dprobs - jnp.sum(probs * dprobs, axis=0, keepdims=True))
            gathered_ref[layer, :, half_scores(half)] += dscores
            dscores = dscores.astype(BF16)
            dks.append(dot(dscores, spread_heads(queries)) * SCALE)
            dqs.append(gather_heads(dot_tn(dscores, keys)) * SCALE)
        parts.append([jnp.concatenate(d, axis=1) for d in (dqs, dks, dvs)])
    return [
        jnp.concatenate([part[i] for part in parts], axis=0).astype(BF16) for i in range(3)
    ]


def kernel(
    lon_count,
    crop_ref,
    frames_ref,
    latent_ref,
    cotangent_ref,
    triple_ref,
    output_ref,
    expand_ref,
    shrink_ref,
    recurrent_ref,
    readout_ref,
    gains_ref,
    table_ref,
    act_out_ref,
    input_grad_ref,
    grads_ref,
    triple_low,
    output_low,
    expand_low,
    shrink_low,
    recurrent_low,
    readout_low,
    table_pad,
    bias_ref,
    onehot_ref,
    gathered_ref,
    gain_sums,
    stream_in,
    stream_one,
    stream_two,
    normed_ref,
    qkv_ref,
    probs_ref,
    context_ref,
    cell_ref,
    tangent_ref,
    state_ref,
    hidden_ref,
    active_ref,
    slope_ref,
    g_ref,
    gm_ref,
    gl_ref,
    gc_ref,
    gpre_ref,
    gstate_ref,
    dcontext_ref,
    dpacked_ref,
    out_halo,
    in_halo,
    send_sem,
    recv_sem,
):
    frame_count = crop_ref.shape[0]
    tokens = frames_ref.shape[0] // frame_count
    row_count = tokens // WINDOW
    me_lon = lax.axis_index("lon")
    ahead = lax.rem(me_lon + 1, lon_count)
    behind = lax.rem(me_lon + lon_count - 1, lon_count)

    barrier = pltpu.get_barrier_semaphore()
    for peer in (ahead, behind):
        pl.semaphore_signal(barrier, inc=1, device_id={"lon": peer}, device_id_type=MESH)
    pl.semaphore_wait(barrier, 2)

    def halo(exchange, frame):
        return pltpu.make_async_remote_copy(
            src_ref=out_halo.at[exchange, frame],
            dst_ref=in_halo.at[exchange, frame],
            send_sem=send_sem.at[exchange, frame],
            recv_sem=recv_sem.at[exchange, frame],
            device_id={"lon": behind if exchange % 2 == 0 else ahead},
            device_id_type=MESH,
        )

    def send_halo(exchange, frame, value):
        out_halo[exchange, frame] = pack_half(value).astype(BF16)
        halo(exchange, frame).start()

    def take_halo(exchange, frame, own):
        halo(exchange, frame).wait_recv()
        return unpack_half(in_halo[exchange, frame].astype(F32), own)

    for layer in range(LAYERS):
        triple_low[layer] = triple_ref[layer].astype(BF16)
        output_low[layer] = output_ref[layer].astype(BF16)
        expand_low[layer] = expand_ref[layer].astype(BF16)
        shrink_low[layer] = shrink_ref[layer].astype(BF16)
        recurrent_low[layer] = recurrent_ref[layer].astype(BF16)
        readout_low[layer] = readout_ref[layer].astype(BF16)
        table_pad[...] = jnp.zeros_like(table_pad)
        table_pad[:, :PAIRS] = table_ref[layer]
        onehot_ref[layer] = offset_onehot(layer % 2 == 1)
        bias_ref[layer] = bias_of_table(table_pad[...], onehot_ref[layer])
    gathered_ref[...] = jnp.zeros_like(gathered_ref)
    gain_sums[...] = jnp.zeros_like(gain_sums)

    def span(frame):
        return pl.ds(pl.multiple_of(frame * tokens, tokens), tokens)

    def gain(layer, which):
        return gains_ref[layer, which : which + 1, :]

    def attention_part(layer, frame, normed):
        at = span(frame)
        normed_ref[layer, at] = normed
        qkv = dot(normed, triple_low[layer]).astype(BF16)
        qkv_ref[layer, at] = qkv
        crop = (crop_ref[frame, 0], crop_ref[frame, 1])
        return attend_forward(qkv, bias_ref, layer, crop, probs_ref, frame, row_count)

    def middle(layer, frame, stream, context, latent):
        at = span(frame)
        context_ref[layer, at] = context
        one = stream + dot(context, output_low[layer])
        stream_one[layer, at] = one
        scaled, _ = norm_parts(one)
        cell = (scaled * gain(layer, 2)).astype(BF16)
        cell_ref[layer, at] = cell
        preact = dot(cell, recurrent_low[layer, :WIDTH]) + dot(latent, recurrent_low[layer, WIDTH:])
        tangent = jnp.tanh(preact)
        tangent_ref[layer, at] = tangent
        state = tangent.astype(BF16)
        state_ref[layer, at] = state
        two = one + dot(state, readout_low[layer])
        stream_two[layer, at] = two
        scaled, _ = norm_parts(two)
        hidden = (scaled * gain(layer, 1)).astype(BF16)
        hidden_ref[layer, at] = hidden
        for block in range(HIDDEN // WIDTH):
            cols = slice(block * WIDTH, (block + 1) * WIDTH)
            inner = dot(hidden, expand_low[layer, :, cols])
            square = inner * inner
            bend = GELU_C * (1.0 + GELU_A * square)
            gate = 0.5 * (1.0 + jnp.tanh(inner * bend))
            active = inner * gate
            slope = gate + active * (1.0 - gate) * (2.0 * GELU_C + 6.0 * GELU_C * GELU_A * square)
            active_ref[layer, at, cols] = active.astype(BF16)
            slope_ref[layer, at, cols] = slope.astype(BF16)
        return two + dot(active_ref[layer, at], shrink_low[layer])

    def middle_back(layer, frame, g, gstate):
        at = span(frame)
        gm = g.astype(BF16)
        gm_ref[at] = gm
        for block in range(HIDDEN // WIDTH):
            cols = slice(block * WIDTH, (block + 1) * WIDTH)
            dactive = dot_nt(gm, shrink_low[layer, cols])
            slope_ref[layer, at, cols] = (dactive * slope_ref[layer, at, cols].astype(F32)).astype(BF16)
        dhidden = dot_nt(slope_ref[layer, at], expand_low[layer])
        scaled, inverse = norm_parts(stream_two[layer, at])
        part, change = norm_back(dhidden, gain(layer, 1), scaled, inverse)
        gain_sums[layer, 1] += part
        g = g + change
        gl = g.astype(BF16)
        gl_ref[at] = gl
        dstate = dot_nt(gl, readout_low[layer])
        if gstate is not None:
            dstate = dstate + gstate
        tangent = tangent_ref[layer, at]
        gpre = (dstate * (1.0 - tangent * tangent)).astype(BF16)
        gpre_ref[at] = gpre
        if layer > 0:
            gstate_ref[at] = dot_nt(gpre, recurrent_low[layer, WIDTH:])
        scaled, inverse = norm_parts(stream_one[layer, at])
        dcell = dot_nt(gpre, recurrent_low[layer, :WIDTH])
        part, change = norm_back(dcell, gain(layer, 2), scaled, inverse)
        gain_sums[layer, 2] += part
        g = g + change
        gc = g.astype(BF16)
        gc_ref[at] = gc
        g_ref[at] = g
        return dot_nt(gc, output_low[layer])

    def attention_back(layer, frame, dcontext):
        at = span(frame)
        pieces = attend_backward(
            qkv_ref[layer, at], dcontext, layer, probs_ref, frame, gathered_ref, row_count
        )
        for which in range(3):
            dpacked_ref[at, which * WIDTH : (which + 1) * WIDTH] = pieces[which]
        return dot_nt(dpacked_ref[at], triple_low[layer])

    def stream_back(layer, frame, g, stream, dnormed):
        scaled, inverse = norm_parts(stream)
        part, change = norm_back(dnormed, gain(layer, 0), scaled, inverse)
        gain_sums[layer, 0] += part
        return g + change

    def put_blocks(start, value):
        rows = value.shape[0]
        for block in range(value.shape[1] // LANES):
            grads_ref[start + block * rows : start + (block + 1) * rows] = value[
                :, half_lanes(block)
            ].astype(BF16)

    def put_rows(start, total_rows, row, value):
        rows = value.shape[0]
        for block in range(value.shape[1] // LANES):
            at = start + block * total_rows + row
            grads_ref[at : at + rows] = value[:, half_lanes(block)].astype(BF16)

    def feed_grads(layer):
        for block in range(HIDDEN // WIDTH):
            cols = slice(block * WIDTH, (block + 1) * WIDTH)
            put_rows(
                SHRINK_AT[layer], HIDDEN, block * WIDTH, dot_tn(active_ref[layer, :, cols], gm_ref[...])
            )
        for block in range(HIDDEN // WIDTH):
            cols = slice(block * WIDTH, (block + 1) * WIDTH)
            put_blocks(
                EXPAND_AT[layer] + 2 * block * WIDTH, dot_tn(hidden_ref[layer], slope_ref[layer, :, cols])
            )

    def small_grads(layer, latent):
        low = dot_tn(cell_ref[layer], gpre_ref[...])
        high = dot_tn(latent, gpre_ref[...])
        recurrent = jnp.concatenate([low, high], axis=0)
        quarter = recurrent.shape[0] // 4
        recurrent = jnp.concatenate(
            [recurrent[i * quarter : (i + 1) * quarter] for i in range(4)], axis=1
        )
        readout = dot_tn(state_ref[layer], gl_ref[...])
        return [recurrent, readout[:, :LANES], readout[:, LANES:]]

    def put_small(layer, pieces):
        table = table_of_bias(gathered_ref[layer], onehot_ref[layer])
        gains = jnp.concatenate(
            [jnp.sum(gain_sums[layer, i], axis=0, keepdims=True) for i in range(3)]
            + [jnp.zeros((5, WIDTH), F32)],
            axis=0,
        )
        pieces = pieces + [table[:, :LANES], table[:, LANES:], gains[:, :LANES], gains[:, LANES:]]
        used = sum(piece.shape[0] for piece in pieces)
        pieces = pieces + [jnp.zeros((SMALL_ROWS - used, LANES), F32)]
        grads_ref[SMALL_AT[layer] : SMALL_AT[layer] + SMALL_ROWS] = jnp.concatenate(
            pieces, axis=0
        ).astype(BF16)

    def output_grads(layer):
        put_blocks(OUTPUT_AT[layer], dot_tn(context_ref[layer], gc_ref[...]))

    def triple_grads(layer):
        for block in range(3):
            cols = slice(block * WIDTH, (block + 1) * WIDTH)
            put_blocks(
                TRIPLE_AT[layer] + 2 * block * WIDTH, dot_tn(normed_ref[layer], dpacked_ref[:, cols])
            )

    def loop(body):
        lax.fori_loop(0, frame_count, lambda frame, unused: body(frame), None)

    def first_layer(frame):
        at = span(frame)
        stream = frames_ref[at].astype(F32)
        scaled, _ = norm_parts(stream)
        normed = (scaled * gain(0, 0)).astype(BF16)
        context = attention_part(0, frame, normed).astype(BF16)
        stream = middle(0, frame, stream, context, latent_ref[at])
        stream_in[at] = stream
        scaled, _ = norm_parts(stream)
        normed = scaled * gain(1, 0)
        normed_ref[1, at] = normed.astype(BF16)
        send_halo(0, frame, normed)

    loop(first_layer)

    def second_attention(frame):
        at = span(frame)
        normed = take_halo(0, frame, normed_ref[1, at].astype(F32))
        context = attention_part(1, frame, rows_ahead(normed).astype(BF16))
        context = rows_behind(context)
        context_ref[1, at] = context.astype(BF16)
        send_halo(1, frame, context)

    loop(second_attention)

    def second_middle(frame):
        at = span(frame)
        context = take_halo(1, frame, context_ref[1, at].astype(F32)).astype(BF16)
        stream = middle(1, frame, stream_in[at], context, state_ref[0, at])
        act_out_ref[at] = stream.astype(BF16)
        dcontext = middle_back(1, frame, cotangent_ref[at].astype(F32), None)
        dcontext_ref[at] = dcontext.astype(BF16)
        send_halo(2, frame, dcontext)

    loop(second_middle)
    feed_grads(1)
    output_grads(1)
    small_one = small_grads(1, state_ref[0])

    def second_back(frame):
        at = span(frame)
        dcontext = take_halo(2, frame, dcontext_ref[at].astype(F32))
        dnormed = attention_back(1, frame, rows_ahead(dcontext).astype(BF16))
        dnormed = rows_behind(dnormed)
        dcontext_ref[at] = dnormed.astype(BF16)
        send_halo(3, frame, dnormed)

    loop(second_back)
    triple_grads(1)

    def first_middle_back(frame):
        at = span(frame)
        dnormed = take_halo(3, frame, dcontext_ref[at].astype(F32))
        g = stream_back(1, frame, g_ref[at], stream_in[at], dnormed)
        dcontext_ref[at] = middle_back(0, frame, g, gstate_ref[at]).astype(BF16)

    loop(first_middle_back)
    put_small(1, small_one)
    feed_grads(0)
    output_grads(0)
    small_zero = small_grads(0, latent_ref[...])

    def first_back(frame):
        at = span(frame)
        dnormed = attention_back(0, frame, dcontext_ref[at])
        stream = frames_ref[at].astype(F32)
        input_grad_ref[at] = stream_back(0, frame, g_ref[at], stream, dnormed)

    loop(first_back)
    triple_grads(0)
    put_small(0, small_zero)

    def drain(frame, unused):
        for exchange in range(4):
            halo(exchange, frame).wait_send()

    lax.fori_loop(0, frame_count, drain, None)


def layers_step(frames, latent, crop_band, cotangent, weights, lon_count):
    frame_count, row_count, col_count, features = frames.shape
    count = frame_count * row_count * col_count
    tokens = row_count * col_count
    flat = lambda a: a.reshape(count, a.shape[-1])
    vmem = pl.BlockSpec(memory_space=pltpu.VMEM)
    both = lambda *shape: pltpu.VMEM((LAYERS,) + shape, BF16)
    one = lambda *shape: pltpu.VMEM(shape, BF16)
    wide = lambda *shape: pltpu.VMEM(shape, F32)
    scratch = [
        both(WIDTH, 3 * WIDTH),
        both(WIDTH, WIDTH),
        both(WIDTH, HIDDEN),
        both(HIDDEN, WIDTH),
        both(WIDTH + LATENT, LATENT),
        both(LATENT, WIDTH),
        wide(HEADS, WIDTH),
        wide(LAYERS, SPAN, HEADS * SPAN),
        both(WIDTH, WINDOW * LANES),
        wide(LAYERS, SPAN, HEADS * SPAN),
        wide(LAYERS, 3, 8, WIDTH),
        wide(count, WIDTH),
        wide(LAYERS, count, WIDTH),
        wide(LAYERS, count, WIDTH),
        both(count, WIDTH),
        both(count, 3 * WIDTH),
        both(count, HEADS * SPAN),
        both(count, WIDTH),
        both(count, WIDTH),
        wide(LAYERS, count, LATENT),
        both(count, LATENT),
        both(count, WIDTH),
        both(count, HIDDEN),
        both(count, HIDDEN),
        wide(count, WIDTH),
        one(count, WIDTH),
        one(count, WIDTH),
        one(count, WIDTH),
        one(count, LATENT),
        wide(count, LATENT),
        one(count, WIDTH),
        one(count, 3 * WIDTH),
        one(4, frame_count, tokens // 2, WIDTH),
        one(4, frame_count, tokens // 2, WIDTH),
        pltpu.SemaphoreType.DMA((4, frame_count)),
        pltpu.SemaphoreType.DMA((4, frame_count)),
    ]
    return pl.pallas_call(
        functools.partial(kernel, lon_count),
        out_shape=(
            jax.ShapeDtypeStruct((count, WIDTH), BF16),
            jax.ShapeDtypeStruct((count, WIDTH), F32),
            jax.ShapeDtypeStruct((GRAD_ROWS, LANES), BF16),
        ),
        in_specs=[pl.BlockSpec(memory_space=pltpu.SMEM)] + [vmem] * (3 + len(weights)),
        out_specs=(vmem, vmem, vmem),
        scratch_shapes=scratch,
        compiler_params=pltpu.CompilerParams(
            collective_id=0, has_side_effects=True, vmem_limit_bytes=60 * 1024 * 1024
        ),
        name="swin_step",
    )(crop_band, flat(frames), flat(latent), flat(cotangent), *weights)


def update(weight, moment, average, gradient):
    velocity = MOMENTUM_RATE * moment + gradient
    updated = weight - LEARN_RATE * (gradient + MOMENTUM_RATE * velocity)
    smoothed = AVERAGE_DECAY * average + (1.0 - AVERAGE_DECAY) * updated
    return (updated, velocity, smoothed)


def unblock(rows, shape):
    height, width = shape
    return rows.reshape(width // LANES, height, LANES).transpose(1, 0, 2).reshape(shape)


def split_grads(grads):
    def at(start, shape):
        count = shape[0] * shape[1] // LANES
        return unblock(grads[start : start + count], shape)

    def expand_at(start, blocks):
        return jnp.concatenate([at(start + 512 * i, (WIDTH, WIDTH)) for i in range(blocks)], axis=1)

    out = []
    for layer in range(LAYERS):
        small = grads[SMALL_AT[layer] : SMALL_AT[layer] + SMALL_ROWS]
        recurrent = jnp.concatenate(
            [small[:72, i * LATENT : (i + 1) * LATENT] for i in range(4)], axis=0
        )
        out.append(
            (
                expand_at(TRIPLE_AT[layer], 3),
                at(OUTPUT_AT[layer], (WIDTH, WIDTH)),
                expand_at(EXPAND_AT[layer], 4),
                at(SHRINK_AT[layer], (HIDDEN, WIDTH)),
                recurrent,
                unblock(small[72:136], (LATENT, WIDTH)),
                unblock(small[152:168], (8, WIDTH))[:3],
                unblock(small[136:152], (HEADS, WIDTH))[:, :PAIRS],
            )
        )
    return [jnp.stack(pair) for pair in zip(*out)]


def per_device(frames, latent_init, crop_band, cotangent, *parameters):
    weights, moments, averages = parameters[0::3], parameters[1::3], parameters[2::3]
    shape = frames.shape
    result, input_grad, grads = layers_step(
        frames, latent_init, crop_band, cotangent, weights, lax.axis_size("lon")
    )
    grads = lax.psum(grads, ("lon", "batch")).astype(F32)
    tokens = shape[0] * shape[1] * shape[2] * lax.axis_size("lon") * lax.axis_size("batch")
    scale = float(tokens) ** (-0.5)
    outs = [result.reshape(shape), input_grad.reshape(shape)]
    for weight, moment, average, gradient in zip(weights, moments, averages, split_grads(grads)):
        outs.extend(update(weight, moment, average, gradient * scale))
    return tuple(outs)


def solution(mesh):
    split = P("batch", None, "lon", None)
    return jax.shard_map(
        per_device,
        mesh=mesh,
        in_specs=(split, split, P("batch", None), split) + (P(),) * 24,
        out_specs=(split, split) + (P(),) * 24,
        check_vma=False,
    )
```

```python
import functools
import math

import jax
import jax.numpy as jnp
from jax import lax
from jax.experimental import pallas as pl
from jax.experimental.pallas import tpu as pltpu
from jax.sharding import PartitionSpec as P

WINDOW = 8
HALF = WINDOW // 2
SPAN = WINDOW * WINDOW
HEADS = 8
LANES = 128
LAYERS = 2
WIDTH = 256
HIDDEN = 1024
LATENT = 32
OFFSETS = 2 * WINDOW - 1
PAIRS = OFFSETS * OFFSETS

LEARN_RATE = 0.2
MOMENTUM_RATE = 0.9
AVERAGE_DECAY = 0.5
NORM_EPS = 1e-05
MASK_FILL = -100.0
HEAD_WIDTH = WIDTH // HEADS
HEADS_A_HALF = LANES // HEAD_WIDTH
SCALE = HEAD_WIDTH ** (-0.5)
GELU_C = 0.7978845608028654
GELU_A = 0.044715

F32 = jnp.float32
BF16 = jnp.bfloat16
MESH = pl.DeviceIdType.MESH

SMALL_ROWS = 256
FEED_ROWS = 2 * HIDDEN * WIDTH // LANES
OUTPUT_ROWS = WIDTH * WIDTH // LANES
TRIPLE_ROWS = 3 * OUTPUT_ROWS
FEED_ONE, ATTEND_ONE, FEED_ZERO, ATTEND_ZERO = range(4)
SECTION_ROWS = (
    FEED_ROWS,
    OUTPUT_ROWS + TRIPLE_ROWS,
    FEED_ROWS,
    OUTPUT_ROWS + TRIPLE_ROWS + LAYERS * SMALL_ROWS,
)
ROW_TILE = 16


class Places:
    def __init__(self, device_count):
        unit = ROW_TILE * device_count
        self.rows = [-(-rows // unit) * unit for rows in SECTION_ROWS]
        self.starts = [sum(self.rows[:i]) for i in range(len(self.rows))]
        self.total = sum(self.rows)
        feed = (self.starts[FEED_ZERO], self.starts[FEED_ONE])
        attend = (self.starts[ATTEND_ZERO], self.starts[ATTEND_ONE])
        self.shrink = feed
        self.expand = tuple(at + FEED_ROWS // 2 for at in feed)
        self.output = attend
        self.triple = tuple(at + OUTPUT_ROWS for at in attend)
        small = attend[0] + OUTPUT_ROWS + TRIPLE_ROWS
        self.small = tuple(small + i * SMALL_ROWS for i in range(LAYERS))


def dot(a, b):
    return jnp.dot(a, b, preferred_element_type=F32)


def dot_nt(a, b):
    return lax.dot_general(a, b, (((1,), (1,)), ((), ())), preferred_element_type=F32)


def dot_tn(a, b):
    return lax.dot_general(a, b, (((0,), (0,)), ((), ())), preferred_element_type=F32)


def norm_parts(stream):
    center = stream - jnp.mean(stream, axis=-1, keepdims=True)
    inverse = lax.rsqrt(jnp.mean(center * center, axis=-1, keepdims=True) + NORM_EPS)
    return center * inverse, inverse


def norm_back(upstream, gain_row, scaled, inverse):
    product = upstream * scaled
    rows, features = product.shape
    gain_part = jnp.sum(product.reshape(rows // 8, 8, features), axis=0)
    weighted = upstream * gain_row
    along = jnp.mean(product * gain_row, axis=-1, keepdims=True)
    inner = weighted - jnp.mean(weighted, axis=-1, keepdims=True) - scaled * along
    return gain_part, inverse * inner


def lower_slots(shape):
    return lax.broadcasted_iota(jnp.int32, shape, 1) < HALF


def pack_half(own):
    tokens, features = own.shape
    rows = own.reshape(tokens // WINDOW, WINDOW, features)
    count = tokens // WINDOW // 2
    moved = pltpu.roll(rows[count:], HALF, axis=1)
    return jnp.where(lower_slots(moved.shape), rows[:count], moved).reshape(tokens // 2, features)


def unpack_half(packed, own):
    tokens, features = own.shape
    pairs = packed.reshape(tokens // WINDOW // 2, WINDOW, features)
    full = jnp.concatenate([pairs, pltpu.roll(pairs, HALF, axis=1)], axis=0)
    rows = own.reshape(tokens // WINDOW, WINDOW, features)
    return jnp.where(lower_slots(full.shape), full, rows).reshape(tokens, features)


def rows_ahead(value):
    cut = HALF * WINDOW
    return jnp.concatenate([value[cut:], value[:cut]], axis=0)


def rows_behind(value):
    cut = value.shape[0] - HALF * WINDOW
    return jnp.concatenate([value[cut:], value[:cut]], axis=0)


def head_of_lane(shape):
    return lax.broadcasted_iota(jnp.int32, shape, 1) // HEAD_WIDTH


def spread_heads(block):
    lane_head = head_of_lane(block.shape)
    zero = jnp.zeros_like(block)
    return jnp.concatenate(
        [jnp.where(lane_head == head, block, zero) for head in range(HEADS_A_HALF)], axis=0
    )


def gather_heads(stacked):
    count = stacked.shape[0] // HEADS_A_HALF
    lane_head = head_of_lane((count, LANES))
    out = stacked[:count]
    for head in range(1, HEADS_A_HALF):
        out = jnp.where(lane_head == head, stacked[head * count : (head + 1) * count], out)
    return out


def half_lanes(half):
    return slice(half * LANES, (half + 1) * LANES)


def half_scores(half):
    return slice(half * HEADS_A_HALF * SPAN, (half + 1) * HEADS_A_HALF * SPAN)


def score_mask(crop_start, crop_end, shifted, window, row_count):
    shape = (SPAN, HEADS_A_HALF * SPAN)
    key_row = lax.broadcasted_iota(jnp.int32, shape, 0) // WINDOW
    source = key_row + window * WINDOW
    if shifted:
        source = source + HALF
        if window == row_count // WINDOW - 1:
            source = jnp.where(source >= row_count, source - row_count, source)
    allowed = (source >= crop_start) & (source < crop_end)
    if shifted and window == row_count // WINDOW - 1:
        query_row = lax.broadcasted_iota(jnp.int32, shape, 1) % SPAN // WINDOW
        allowed = allowed & ((key_row < HALF) == (query_row < HALF))
    return jnp.where(allowed, 0.0, MASK_FILL).astype(F32)


def offset_onehot(shifted):
    shape = (WIDTH, WINDOW * LANES)
    lane = lax.broadcasted_iota(jnp.int32, shape, 1)
    key_col = lane // LANES
    row_offset = lane % LANES // WINDOW
    query_col = lane % WINDOW
    if shifted:
        key_col = (key_col + HALF) % WINDOW
        query_col = (query_col + HALF) % WINDOW
    target = row_offset * OFFSETS + query_col - key_col + WINDOW - 1
    target = jnp.where(row_offset < OFFSETS, target, -1)
    pair = lax.broadcasted_iota(jnp.int32, shape, 0)
    return jnp.where(pair == target, 1.0, 0.0).astype(BF16)


def three_parts(value):
    high = value.astype(BF16)
    rest = value - high.astype(F32)
    middle = rest.astype(BF16)
    low = (rest - middle.astype(F32)).astype(BF16)
    return jnp.concatenate([high.astype(F32), middle.astype(F32), low.astype(F32)], axis=0).astype(BF16)


def swap_groups(tiles):
    return [jnp.concatenate([tile[b : b + 1] for tile in tiles], axis=0) for b in range(8)]


def bias_of_table(table, onehot):
    spread = dot(three_parts(table), onehot)
    spread = spread[:HEADS] + (spread[HEADS : 2 * HEADS] + spread[2 * HEADS :])
    tiles = swap_groups([spread[:, col * LANES : (col + 1) * LANES] for col in range(WINDOW)])
    lane = lax.broadcasted_iota(jnp.int32, (WINDOW, LANES), 1)
    blocks = []
    for key_row in range(WINDOW):
        back = (WINDOW - 1 - key_row) * WINDOW
        pieces = []
        for pair in range(HEADS // 2):
            even = pltpu.roll(tiles[2 * pair], (LANES - back) % LANES, axis=1)
            odd = pltpu.roll(tiles[2 * pair + 1], (LANES + SPAN - back) % LANES, axis=1)
            pieces.append(jnp.where(lane < SPAN, even, odd))
        blocks.append(jnp.concatenate(pieces, axis=1))
    return jnp.concatenate(blocks, axis=0)


def table_of_bias(gathered, onehot):
    lane = lax.broadcasted_iota(jnp.int32, (WINDOW, LANES), 1)
    zero = jnp.zeros((WINDOW, LANES), F32)
    tiles = []
    for head in range(HEADS):
        total = None
        for key_row in range(WINDOW):
            forth = (WINDOW - 1 - key_row) * WINDOW
            block = gathered[key_row * WINDOW : (key_row + 1) * WINDOW, half_lanes(head // 2)]
            if head % 2 == 0:
                moved = pltpu.roll(jnp.where(lane < SPAN, block, zero), forth, axis=1)
            else:
                moved = pltpu.roll(jnp.where(lane < SPAN, zero, block), (forth + SPAN) % LANES, axis=1)
            total = moved if total is None else total + moved
        tiles.append(total)
    spread = jnp.concatenate(swap_groups(tiles), axis=1)
    parts = dot_nt(three_parts(spread), onehot)
    return parts[:HEADS] + (parts[HEADS : 2 * HEADS] + parts[2 * HEADS :])


def attend_forward(qkv, bias_ref, layer, crop, probs_ref, frame, row_count):
    shifted = layer % 2 == 1
    windows = []
    for window in range(row_count // WINDOW):
        rows = slice(window * SPAN, (window + 1) * SPAN)
        mask = score_mask(crop[0], crop[1], shifted, window, row_count)
        halves = []
        for half in range(2):
            queries = qkv[rows, half * LANES : (half + 1) * LANES]
            keys = qkv[rows, WIDTH + half * LANES : WIDTH + (half + 1) * LANES]
            values = qkv[rows, 2 * WIDTH + half * LANES : 2 * WIDTH + (half + 1) * LANES]
            scores = dot_nt(keys, spread_heads(queries)) * SCALE
            scores = scores + bias_ref[layer, :, half_scores(half)] + mask
            exponent = jnp.exp(scores - jnp.max(scores, axis=0, keepdims=True))
            probs = exponent * (1.0 / jnp.sum(exponent, axis=0, keepdims=True))
            probs = probs.astype(BF16)
            at = (frame * (row_count // WINDOW) + window) * SPAN
            probs_ref[layer, pl.ds(pl.multiple_of(at, SPAN), SPAN), half_scores(half)] = probs
            halves.append(gather_heads(dot_tn(probs, values)))
        windows.append(jnp.concatenate(halves, axis=1))
    return jnp.concatenate(windows, axis=0)


def attend_backward(qkv, dcontext, layer, probs_ref, frame, gathered_ref, row_count):
    parts = []
    for window in range(row_count // WINDOW):
        rows = slice(window * SPAN, (window + 1) * SPAN)
        dqs, dks, dvs = [], [], []
        for half in range(2):
            queries = qkv[rows, half * LANES : (half + 1) * LANES]
            keys = qkv[rows, WIDTH + half * LANES : WIDTH + (half + 1) * LANES]
            values = qkv[rows, 2 * WIDTH + half * LANES : 2 * WIDTH + (half + 1) * LANES]
            dcs = spread_heads(dcontext[rows, half_lanes(half)])
            at = (frame * (row_count // WINDOW) + window) * SPAN
            low = probs_ref[layer, pl.ds(pl.multiple_of(at, SPAN), SPAN), half_scores(half)]
            probs = low.astype(F32)
            dvs.append(dot(low, dcs))
            dprobs = dot_nt(values, dcs)
            dscores = probs * (dprobs - jnp.sum(probs * dprobs, axis=0, keepdims=True))
            gathered_ref[layer, :, half_scores(half)] += dscores
            dscores = dscores.astype(BF16)
            dks.append(dot(dscores, spread_heads(queries)) * SCALE)
            dqs.append(gather_heads(dot_tn(dscores, keys)) * SCALE)
        parts.append([jnp.concatenate(d, axis=1) for d in (dqs, dks, dvs)])
    return [
        jnp.concatenate([part[i] for part in parts], axis=0).astype(BF16) for i in range(3)
    ]


def kernel(
    lon_count,
    batch_count,
    places,
    crop_ref,
    frames_ref,
    latent_ref,
    cotangent_ref,
    triple_ref,
    output_ref,
    expand_ref,
    shrink_ref,
    recurrent_ref,
    readout_ref,
    gains_ref,
    table_ref,
    act_out_ref,
    input_grad_ref,
    sums_out_ref,
    triple_low,
    output_low,
    expand_low,
    shrink_low,
    recurrent_low,
    readout_low,
    table_pad,
    bias_ref,
    onehot_ref,
    gathered_ref,
    gain_sums,
    stream_in,
    stream_one,
    stream_two,
    normed_ref,
    qkv_ref,
    probs_ref,
    context_ref,
    cell_ref,
    tangent_ref,
    state_ref,
    hidden_ref,
    active_ref,
    slope_ref,
    g_ref,
    gm_ref,
    gl_ref,
    gc_ref,
    gpre_ref,
    gstate_ref,
    dcontext_ref,
    dpacked_ref,
    out_halo,
    in_halo,
    grads_ref,
    sums_ref,
    core_in,
    lon_in,
    line_in,
    send_sem,
    recv_sem,
    sum_send_sem,
    sum_recv_sem,
    out_sem,
):
    frame_count = crop_ref.shape[1]
    tokens = frames_ref.shape[0] // frame_count
    row_count = tokens // WINDOW
    me_lon = lax.axis_index("lon")
    ahead = lax.rem(me_lon + 1, lon_count)
    behind = lax.rem(me_lon + lon_count - 1, lon_count)

    me_batch = lax.axis_index("batch")
    core, line = lax.rem(me_batch, 2), lax.div(me_batch, 2)
    line_count = batch_count // 2
    lon_peers = [lax.rem(me_lon + by, lon_count) for by in range(1, lon_count)]
    line_peers = [lax.rem(line + by, line_count) for by in range(1, line_count)]
    neighbours = [{"batch": 2 * line + 1 - core}]
    neighbours += [{"lon": peer} for peer in lon_peers]
    neighbours += [{"batch": 2 * peer + core} for peer in line_peers]

    barrier = pltpu.get_barrier_semaphore()
    for peer in neighbours:
        pl.semaphore_signal(barrier, inc=1, device_id=peer, device_id_type=MESH)
    pl.semaphore_wait(barrier, len(neighbours))

    def row_span(start, rows):
        return pl.ds(pl.multiple_of(start, ROW_TILE), rows)

    def sum_copies(section, phase):
        half = places.rows[section] // 2
        piece = half // lon_count
        shard = piece // line_count
        my_half = places.starts[section] + core * half
        my_piece = my_half + me_lon * piece
        my_shard = my_piece + line * shard
        wide = places.starts[section]
        first_sem = (0, 1, lon_count, lon_count + line_count - 1, lon_count + 2 * (line_count - 1), 2 * (lon_count + line_count - 1) - 1)[phase]
        if phase == 0:
            to = [(grads_ref, places.starts[section] + (1 - core) * half, core_in, wide // 2)]
            rows, peers = half, neighbours[:1]
        elif phase == 1:
            to = [
                (grads_ref, my_half + peer * piece, lon_in, (wide // 2 // lon_count) * (lon_count - 1) + i * piece)
                for i, peer in enumerate(lon_peers)
            ]
            rows, peers = piece, neighbours[1:lon_count]
        elif phase == 2:
            to = [
                (
                    grads_ref,
                    my_piece + peer * shard,
                    line_in,
                    (wide // 2 // lon_count // line_count) * (line_count - 1) + i * shard,
                )
                for i, peer in enumerate(line_peers)
            ]
            rows, peers = shard, neighbours[lon_count:]
        elif phase == 3:
            rows, peers = shard, neighbours[lon_count:]
            to = [(sums_ref, my_shard, sums_ref, my_shard)] * len(peers)
        elif phase == 4:
            rows, peers = piece, neighbours[1:lon_count]
            to = [(sums_ref, my_piece, sums_ref, my_piece)] * len(peers)
        else:
            rows, peers = half, neighbours[:1]
            to = [(sums_ref, my_half, sums_ref, my_half)]
        return [
            pltpu.make_async_remote_copy(
                src_ref=src.at[row_span(src_at, rows)],
                dst_ref=dst.at[row_span(dst_at, rows)],
                send_sem=sum_send_sem.at[section, first_sem + i],
                recv_sem=sum_recv_sem.at[section, first_sem + i],
                device_id=peer,
                device_id_type=MESH,
            )
            for i, ((src, src_at, dst, dst_at), peer) in enumerate(zip(to, peers))
        ]

    def add_up(start, rows, source, source_at, count, target):
        step = math.gcd(rows, LANES)

        def body(i, unused):
            at = row_span(start + i * step, step)
            total = grads_ref[at].astype(F32)
            for k in range(count):
                total = total + source[row_span(source_at + k * rows + i * step, step)].astype(F32)
            target[at] = total.astype(BF16)

        lax.fori_loop(0, rows // step, body, None)

    def sum_start(section, phase):
        for copy in sum_copies(section, phase):
            copy.start()

    def sum_take(section, phase):
        for copy in sum_copies(section, phase):
            copy.wait_recv()
        half = places.rows[section] // 2
        piece = half // lon_count
        shard = piece // line_count
        my_half = places.starts[section] + core * half
        my_piece = my_half + me_lon * piece
        wide = places.starts[section] // 2
        if phase == 0:
            add_up(my_half, half, core_in, wide, 1, grads_ref)
        elif phase == 1:
            at = wide // lon_count * (lon_count - 1)
            add_up(my_piece, piece, lon_in, at, lon_count - 1, grads_ref)
        elif phase == 2:
            at = wide // lon_count // line_count * (line_count - 1)
            add_up(my_piece + line * shard, shard, line_in, at, line_count - 1, sums_ref)

    def sum_step(section, phase):
        sum_take(section, phase)
        if phase < 5:
            sum_start(section, phase + 1)
        else:
            sums_out(section).start()

    def sums_out(section):
        rows = pl.ds(places.starts[section], places.rows[section])
        return pltpu.make_async_copy(sums_ref.at[rows], sums_out_ref.at[rows], out_sem.at[section])

    def sum_drain(section):
        for phase in range(6):
            for copy in sum_copies(section, phase):
                copy.wait_send()
        sums_out(section).wait()

    def halo(exchange, frame):
        return pltpu.make_async_remote_copy(
            src_ref=out_halo.at[exchange, frame],
            dst_ref=in_halo.at[exchange, frame],
            send_sem=send_sem.at[exchange, frame],
            recv_sem=recv_sem.at[exchange, frame],
            device_id={"lon": behind if exchange % 2 == 0 else ahead},
            device_id_type=MESH,
        )

    def send_halo(exchange, frame, value):
        out_halo[exchange, frame] = pack_half(value).astype(BF16)
        halo(exchange, frame).start()

    def take_halo(exchange, frame, own):
        halo(exchange, frame).wait_recv()
        return unpack_half(in_halo[exchange, frame].astype(F32), own)

    for layer in range(LAYERS):
        triple_low[layer] = triple_ref[layer].astype(BF16)
        output_low[layer] = output_ref[layer].astype(BF16)
        expand_low[layer] = expand_ref[layer].astype(BF16)
        shrink_low[layer] = shrink_ref[layer].astype(BF16)
        recurrent_low[layer] = recurrent_ref[layer].astype(BF16)
        readout_low[layer] = readout_ref[layer].astype(BF16)
        table_pad[...] = jnp.zeros_like(table_pad)
        table_pad[:, :PAIRS] = table_ref[layer]
        onehot_ref[layer] = offset_onehot(layer % 2 == 1)
        bias_ref[layer] = bias_of_table(table_pad[...], onehot_ref[layer])
    gathered_ref[...] = jnp.zeros_like(gathered_ref)
    gain_sums[...] = jnp.zeros_like(gain_sums)

    def span(frame):
        return pl.ds(pl.multiple_of(frame * tokens, tokens), tokens)

    def gain(layer, which):
        return gains_ref[which, layer : layer + 1, :]

    def attention_part(layer, frame, normed):
        at = span(frame)
        normed_ref[layer, at] = normed
        qkv = dot(normed, triple_low[layer]).astype(BF16)
        qkv_ref[layer, at] = qkv
        crop = (crop_ref[0, frame], crop_ref[1, frame])
        return attend_forward(qkv, bias_ref, layer, crop, probs_ref, frame, row_count)

    def middle(layer, frame, stream, context, latent):
        at = span(frame)
        context_ref[layer, at] = context
        one = stream + dot(context, output_low[layer])
        stream_one[layer, at] = one
        scaled, _ = norm_parts(one)
        cell = (scaled * gain(layer, 2)).astype(BF16)
        cell_ref[layer, at] = cell
        preact = dot_nt(cell, recurrent_low[layer, :, :WIDTH]) + dot_nt(latent, recurrent_low[layer, :, WIDTH:])
        tangent = jnp.tanh(preact)
        tangent_ref[layer, at] = tangent
        state = tangent.astype(BF16)
        state_ref[layer, at] = state
        two = one + dot(state, readout_low[layer])
        stream_two[layer, at] = two
        scaled, _ = norm_parts(two)
        hidden = (scaled * gain(layer, 1)).astype(BF16)
        hidden_ref[layer, at] = hidden
        for block in range(HIDDEN // WIDTH):
            cols = slice(block * WIDTH, (block + 1) * WIDTH)
            inner = dot(hidden, expand_low[layer, :, cols])
            square = inner * inner
            bend = GELU_C * (1.0 + GELU_A * square)
            gate = 0.5 * (1.0 + jnp.tanh(inner * bend))
            active = inner * gate
            slope = gate + active * (1.0 - gate) * (2.0 * GELU_C + 6.0 * GELU_C * GELU_A * square)
            active_ref[layer, at, cols] = active.astype(BF16)
            slope_ref[layer, at, cols] = slope.astype(BF16)
        return two + dot(active_ref[layer, at], shrink_low[layer])

    def middle_back(layer, frame, g, gstate):
        at = span(frame)
        gm = g.astype(BF16)
        gm_ref[at] = gm
        for block in range(HIDDEN // WIDTH):
            cols = slice(block * WIDTH, (block + 1) * WIDTH)
            dactive = dot_nt(gm, shrink_low[layer, cols])
            slope_ref[layer, at, cols] = (dactive * slope_ref[layer, at, cols].astype(F32)).astype(BF16)
        dhidden = dot_nt(slope_ref[layer, at], expand_low[layer])
        scaled, inverse = norm_parts(stream_two[layer, at])
        part, change = norm_back(dhidden, gain(layer, 1), scaled, inverse)
        gain_sums[layer, 1] += part
        g = g + change
        gl = g.astype(BF16)
        gl_ref[at] = gl
        dstate = dot_nt(gl, readout_low[layer])
        if gstate is not None:
            dstate = dstate + gstate
        tangent = tangent_ref[layer, at]
        gpre = (dstate * (1.0 - tangent * tangent)).astype(BF16)
        gpre_ref[at] = gpre
        if layer > 0:
            gstate_ref[at] = dot(gpre, recurrent_low[layer, :, WIDTH:])
        scaled, inverse = norm_parts(stream_one[layer, at])
        dcell = dot(gpre, recurrent_low[layer, :, :WIDTH])
        part, change = norm_back(dcell, gain(layer, 2), scaled, inverse)
        gain_sums[layer, 2] += part
        g = g + change
        gc = g.astype(BF16)
        gc_ref[at] = gc
        g_ref[at] = g
        return dot_nt(gc, output_low[layer])

    def attention_back(layer, frame, dcontext):
        at = span(frame)
        pieces = attend_backward(
            qkv_ref[layer, at], dcontext, layer, probs_ref, frame, gathered_ref, row_count
        )
        for which in range(3):
            dpacked_ref[at, which * WIDTH : (which + 1) * WIDTH] = pieces[which]
        return dot_nt(dpacked_ref[at], triple_low[layer])

    def stream_back(layer, frame, g, stream, dnormed):
        scaled, inverse = norm_parts(stream)
        part, change = norm_back(dnormed, gain(layer, 0), scaled, inverse)
        gain_sums[layer, 0] += part
        return g + change

    def put_blocks(start, value):
        rows = value.shape[0]
        for block in range(value.shape[1] // LANES):
            grads_ref[start + block * rows : start + (block + 1) * rows] = value[
                :, half_lanes(block)
            ].astype(BF16)

    def put_rows(start, total_rows, row, value):
        rows = value.shape[0]
        for block in range(value.shape[1] // LANES):
            at = start + block * total_rows + row
            grads_ref[at : at + rows] = value[:, half_lanes(block)].astype(BF16)

    def feed_grads(layer):
        for block in range(HIDDEN // WIDTH):
            cols = slice(block * WIDTH, (block + 1) * WIDTH)
            put_rows(
                places.shrink[layer], HIDDEN, block * WIDTH, dot_tn(active_ref[layer, :, cols], gm_ref[...])
            )
        for block in range(HIDDEN // WIDTH):
            cols = slice(block * WIDTH, (block + 1) * WIDTH)
            put_blocks(
                places.expand[layer] + 2 * block * WIDTH, dot_tn(hidden_ref[layer], slope_ref[layer, :, cols])
            )

    def small_grads(layer, latent):
        near = dot_tn(gpre_ref[...], cell_ref[layer])
        far = dot_tn(gpre_ref[...], latent)
        far = jnp.concatenate([far, jnp.zeros((LATENT, LANES - LATENT), F32)], axis=1)
        readout = dot_tn(state_ref[layer], gl_ref[...])
        return [near[:, :LANES], near[:, LANES:], far, readout[:, :LANES], readout[:, LANES:]]

    def put_small(layer, pieces):
        table = table_of_bias(gathered_ref[layer], onehot_ref[layer])
        gains = jnp.concatenate(
            [jnp.sum(gain_sums[layer, i], axis=0, keepdims=True) for i in range(3)]
            + [jnp.zeros((5, WIDTH), F32)],
            axis=0,
        )
        pieces = pieces + [table[:, :LANES], table[:, LANES:], gains[:, :LANES], gains[:, LANES:]]
        used = sum(piece.shape[0] for piece in pieces)
        pieces = pieces + [jnp.zeros((SMALL_ROWS - used, LANES), F32)]
        grads_ref[places.small[layer] : places.small[layer] + SMALL_ROWS] = jnp.concatenate(
            pieces, axis=0
        ).astype(BF16)

    def output_grads(layer):
        put_blocks(places.output[layer], dot_tn(context_ref[layer], gc_ref[...]))

    def triple_grads(layer):
        for block in range(3):
            cols = slice(block * WIDTH, (block + 1) * WIDTH)
            put_blocks(
                places.triple[layer] + 2 * block * WIDTH, dot_tn(normed_ref[layer], dpacked_ref[:, cols])
            )

    def loop(body, steps=()):
        def whole(frame, unused):
            body(frame)
            for after in range(frame_count):
                here = [(section, phase) for when, section, phase in steps if when == after]
                if here:

                    @pl.when(frame == after)
                    def _(here=here):
                        for section, phase in here:
                            sum_step(section, phase)

        lax.fori_loop(0, frame_count, whole, None)

    def first_layer(frame):
        at = span(frame)
        stream = frames_ref[at].astype(F32)
        scaled, _ = norm_parts(stream)
        normed = (scaled * gain(0, 0)).astype(BF16)
        context = attention_part(0, frame, normed).astype(BF16)
        stream = middle(0, frame, stream, context, latent_ref[at])
        stream_in[at] = stream
        scaled, _ = norm_parts(stream)
        normed = scaled * gain(1, 0)
        normed_ref[1, at] = normed.astype(BF16)
        send_halo(0, frame, normed)

    loop(first_layer)

    def second_attention(frame):
        at = span(frame)
        normed = take_halo(0, frame, normed_ref[1, at].astype(F32))
        context = attention_part(1, frame, rows_ahead(normed).astype(BF16))
        context = rows_behind(context)
        context_ref[1, at] = context.astype(BF16)
        send_halo(1, frame, context)

    loop(second_attention)

    def second_middle(frame):
        at = span(frame)
        context = take_halo(1, frame, context_ref[1, at].astype(F32)).astype(BF16)
        stream = middle(1, frame, stream_in[at], context, state_ref[0, at])
        act_out_ref[at] = stream.astype(BF16)
        dcontext = middle_back(1, frame, cotangent_ref[at].astype(F32), None)
        dcontext_ref[at] = dcontext.astype(BF16)
        send_halo(2, frame, dcontext)

    loop(second_middle)
    feed_grads(1)
    sum_start(FEED_ONE, 0)
    output_grads(1)
    small_one = small_grads(1, state_ref[0])

    def second_back(frame):
        at = span(frame)
        dcontext = take_halo(2, frame, dcontext_ref[at].astype(F32))
        dnormed = attention_back(1, frame, rows_ahead(dcontext).astype(BF16))
        dnormed = rows_behind(dnormed)
        dcontext_ref[at] = dnormed.astype(BF16)
        send_halo(3, frame, dnormed)

    loop(second_back, ((0, FEED_ONE, 0), (3, FEED_ONE, 1)))
    triple_grads(1)
    sum_start(ATTEND_ONE, 0)

    def first_middle_back(frame):
        at = span(frame)
        dnormed = take_halo(3, frame, dcontext_ref[at].astype(F32))
        g = stream_back(1, frame, g_ref[at], stream_in[at], dnormed)
        dcontext_ref[at] = middle_back(0, frame, g, gstate_ref[at]).astype(BF16)

    loop(
        first_middle_back,
        (
            (0, ATTEND_ONE, 0),
            (1, FEED_ONE, 2),
            (2, ATTEND_ONE, 1),
            (2, FEED_ONE, 3),
            (3, ATTEND_ONE, 2),
        ),
    )
    feed_grads(0)
    sum_start(FEED_ZERO, 0)
    put_small(1, small_one)
    output_grads(0)
    small_zero = small_grads(0, latent_ref[...])

    def first_back(frame):
        at = span(frame)
        dnormed = attention_back(0, frame, dcontext_ref[at])
        stream = frames_ref[at].astype(F32)
        input_grad_ref[at] = stream_back(0, frame, g_ref[at], stream, dnormed)

    loop(
        first_back,
        (
            (0, FEED_ZERO, 0),
            (0, ATTEND_ONE, 3),
            (1, FEED_ONE, 4),
            (2, ATTEND_ONE, 4),
            (3, FEED_ZERO, 1),
        ),
    )
    triple_grads(0)
    put_small(0, small_zero)
    sum_start(ATTEND_ZERO, 0)
    for section, phase in (
        (FEED_ONE, 5),
        (ATTEND_ONE, 5),
        (ATTEND_ZERO, 0),
        (FEED_ZERO, 2),
        (ATTEND_ZERO, 1),
        (FEED_ZERO, 3),
        (ATTEND_ZERO, 2),
        (FEED_ZERO, 4),
        (ATTEND_ZERO, 3),
        (FEED_ZERO, 5),
        (ATTEND_ZERO, 4),
        (ATTEND_ZERO, 5),
    ):
        sum_step(section, phase)

    def drain(frame, unused):
        for exchange in range(4):
            halo(exchange, frame).wait_send()

    lax.fori_loop(0, frame_count, drain, None)
    for section in range(len(places.rows)):
        sum_drain(section)


def layers_step(frames, latent, crop_band, cotangent, weights, lon_count, batch_count, places):
    frame_count, row_count, col_count, features = frames.shape
    count = frame_count * row_count * col_count
    tokens = row_count * col_count
    flat = lambda a: a.reshape(count, a.shape[-1])
    vmem = pl.BlockSpec(memory_space=pltpu.VMEM)
    both = lambda *shape: pltpu.VMEM((LAYERS,) + shape, BF16)
    one = lambda *shape: pltpu.VMEM(shape, BF16)
    wide = lambda *shape: pltpu.VMEM(shape, F32)
    line_count = batch_count // 2
    sections = len(places.rows)
    scratch = [
        both(WIDTH, 3 * WIDTH),
        both(WIDTH, WIDTH),
        both(WIDTH, HIDDEN),
        both(HIDDEN, WIDTH),
        both(LATENT, WIDTH + LATENT),
        both(LATENT, WIDTH),
        wide(HEADS, WIDTH),
        wide(LAYERS, SPAN, HEADS * SPAN),
        both(WIDTH, WINDOW * LANES),
        wide(LAYERS, SPAN, HEADS * SPAN),
        wide(LAYERS, 3, 8, WIDTH),
        wide(count, WIDTH),
        wide(LAYERS, count, WIDTH),
        wide(LAYERS, count, WIDTH),
        both(count, WIDTH),
        both(count, 3 * WIDTH),
        both(count, HEADS * SPAN),
        both(count, WIDTH),
        both(count, WIDTH),
        wide(LAYERS, count, LATENT),
        both(count, LATENT),
        both(count, WIDTH),
        both(count, HIDDEN),
        both(count, HIDDEN),
        wide(count, WIDTH),
        one(count, WIDTH),
        one(count, WIDTH),
        one(count, WIDTH),
        one(count, LATENT),
        wide(count, LATENT),
        one(count, WIDTH),
        one(count, 3 * WIDTH),
        one(4, frame_count, tokens // 2, WIDTH),
        one(4, frame_count, tokens // 2, WIDTH),
        one(places.total, LANES),
        one(places.total, LANES),
        one(places.total // 2, LANES),
        one(places.total // 2 // lon_count * (lon_count - 1), LANES),
        one(places.total // 2 // lon_count // line_count * (line_count - 1), LANES),
        pltpu.SemaphoreType.DMA((4, frame_count)),
        pltpu.SemaphoreType.DMA((4, frame_count)),
        pltpu.SemaphoreType.DMA((sections, 2 * (lon_count + line_count - 1))),
        pltpu.SemaphoreType.DMA((sections, 2 * (lon_count + line_count - 1))),
        pltpu.SemaphoreType.DMA((sections,)),
    ]
    return pl.pallas_call(
        functools.partial(kernel, lon_count, batch_count, places),
        out_shape=(
            jax.ShapeDtypeStruct((count, WIDTH), BF16),
            jax.ShapeDtypeStruct((count, WIDTH), F32),
            jax.ShapeDtypeStruct((places.total, LANES), BF16),
        ),
        in_specs=[pl.BlockSpec(memory_space=pltpu.SMEM)] + [vmem] * (3 + len(weights)),
        out_specs=(vmem, vmem, pl.BlockSpec(memory_space=pl.ANY)),
        scratch_shapes=scratch,
        compiler_params=pltpu.CompilerParams(
            collective_id=0, has_side_effects=True, vmem_limit_bytes=60 * 1024 * 1024
        ),
        name="swin_step",
    )(crop_band.T, flat(frames), flat(latent), flat(cotangent), *weights)


def update_kernel(scale, places, sums_hbm, result_hbm, grad_hbm, *refs):
    count = 24
    given, result_out, grad_out = refs[:count], refs[count], refs[count + 1]
    made = refs[count + 2 : 2 * count + 2]
    sums, held = refs[2 * count + 2], refs[2 * count + 3 : 3 * count + 3]
    sums_sem, pass_sem, in_sem, out_sem = refs[3 * count + 3 :]
    triple, output, expand, shrink, recurrent, readout, gains, table = range(8)

    passing = [
        pltpu.make_async_copy(result_hbm, result_out, pass_sem.at[0]),
        pltpu.make_async_copy(grad_hbm, grad_out, pass_sem.at[1]),
    ]
    units = [
        (FEED_ONE, expand, 1),
        (FEED_ONE, shrink, 1),
        (ATTEND_ONE, output, 1),
        (ATTEND_ONE, triple, 1),
        (FEED_ZERO, expand, 0),
        (FEED_ZERO, shrink, 0),
        (ATTEND_ZERO, output, 0),
        (ATTEND_ZERO, triple, 0),
        (ATTEND_ZERO, recurrent, None),
        (ATTEND_ZERO, readout, None),
        (ATTEND_ZERO, gains, None),
        (ATTEND_ZERO, table, None),
    ]

    def part(ref, layer):
        return ref if layer is None else ref.at[layer]

    def coming(index):
        section, which, layer = units[index]
        return [
            pltpu.make_async_copy(
                part(given[3 * which + i], layer), part(held[3 * which + i], layer), in_sem.at[index, i]
            )
            for i in range(3)
        ]

    def going(index):
        section, which, layer = units[index]
        return [
            pltpu.make_async_copy(
                part(held[3 * which + i], layer), part(made[3 * which + i], layer), out_sem.at[index, i]
            )
            for i in range(3)
        ]

    def sums_in(section):
        rows = pl.ds(places.starts[section], places.rows[section])
        return pltpu.make_async_copy(sums_hbm.at[rows], sums.at[rows], sums_sem.at[section])

    begun = set()
    for index, (section, which, layer) in enumerate(units):
        if section not in begun:
            begun.add(section)
            sums_in(section).start()
        for copy in coming(index):
            copy.start()
    for copy in passing:
        copy.start()

    def change(which, at, summed):
        weight, moment, average = held[3 * which : 3 * which + 3]
        gradient = summed.astype(F32) * scale
        velocity = MOMENTUM_RATE * moment[at] + gradient
        updated = weight[at] - LEARN_RATE * (gradient + MOMENTUM_RATE * velocity)
        average[at] = AVERAGE_DECAY * average[at] + (1.0 - AVERAGE_DECAY) * updated
        weight[at] = updated
        moment[at] = velocity

    def change_blocks(which, layer, start, rows, cols):
        step = 64

        def body(i, unused):
            row = pl.multiple_of(i * step, step)
            for block in range(cols // LANES):
                summed = sums[pl.ds(start + block * rows + row, step)]
                change(which, (layer, pl.ds(row, step), half_lanes(block)), summed)

        lax.fori_loop(0, rows // step, body, None)

    for index, (section, which, layer) in enumerate(units):
        if section in begun:
            begun.remove(section)
            sums_in(section).wait()
        for copy in coming(index):
            copy.wait()
        if which == expand:
            change_blocks(expand, layer, places.expand[layer], WIDTH, HIDDEN)
        elif which == shrink:
            change_blocks(shrink, layer, places.shrink[layer], HIDDEN, WIDTH)
        elif which == output:
            change_blocks(output, layer, places.output[layer], WIDTH, WIDTH)
        elif which == triple:
            change_blocks(triple, layer, places.triple[layer], WIDTH, 3 * WIDTH)
        else:
            for each in range(LAYERS):
                at = places.small[each]
                if which == recurrent:
                    for block in range(3):
                        lanes = slice(block * LANES, min((block + 1) * LANES, WIDTH + LATENT))
                        rows = sums[pl.ds(at + block * LATENT, LATENT)]
                        change(which, (each, slice(0, LATENT), lanes), rows[:, : lanes.stop - lanes.start])
                elif which == readout:
                    for block in range(2):
                        rows = sums[pl.ds(at + 96 + block * LATENT, LATENT)]
                        change(which, (each, slice(0, LATENT), half_lanes(block)), rows)
                else:
                    rows = sums[pl.ds(at + 160, 32)].astype(F32)
                    if which == table:
                        change(which, (each, slice(0, HEADS), slice(0, LANES)), rows[:8])
                        change(which, (each, slice(0, HEADS), slice(LANES, PAIRS)), rows[8:16, : PAIRS - LANES])
                    else:
                        for norm in range(3):
                            for block in range(2):
                                row = 16 + block * 8 + norm
                                at_one = (norm, slice(each, each + 1), half_lanes(block))
                                change(which, at_one, rows[row : row + 1])
        for copy in going(index):
            copy.start()
    for index in range(len(units)):
        for copy in going(index):
            copy.wait()
    for copy in passing:
        copy.wait()


def update_step(sums, result, input_grad, parameters, scale, places):
    anywhere = pl.BlockSpec(memory_space=pl.ANY)
    like = lambda a: jax.ShapeDtypeStruct(a.shape, a.dtype)
    return pl.pallas_call(
        functools.partial(update_kernel, scale, places),
        out_shape=(like(result), like(input_grad)) + tuple(like(a) for a in parameters),
        in_specs=[anywhere] * (3 + len(parameters)),
        out_specs=(anywhere,) * (2 + len(parameters)),
        scratch_shapes=[pltpu.VMEM(sums.shape, BF16)]
        + [pltpu.VMEM(a.shape, F32) for a in parameters]
        + [
            pltpu.SemaphoreType.DMA((len(places.rows),)),
            pltpu.SemaphoreType.DMA((2,)),
            pltpu.SemaphoreType.DMA((12, 3)),
            pltpu.SemaphoreType.DMA((12, 3)),
        ],
        compiler_params=pltpu.CompilerParams(vmem_limit_bytes=48 * 1024 * 1024),
        name="nesterov_step",
    )(sums, result, input_grad, *parameters)


def per_device(frames, latent_init, crop_band, cotangent, *parameters):
    shape = frames.shape
    lon_count, batch_count = lax.axis_size("lon"), lax.axis_size("batch")
    places = Places(lon_count * batch_count)
    turned = {4: (0, 2, 1), 6: (1, 0, 2)}
    parameters = [
        a.transpose(turned[i // 3]) if i // 3 in turned else a for i, a in enumerate(parameters)
    ]
    result, input_grad, sums = layers_step(
        frames, latent_init, crop_band, cotangent, parameters[0::3], lon_count, batch_count, places
    )
    tokens = shape[0] * shape[1] * shape[2] * lon_count * batch_count
    result, input_grad, *updated = update_step(
        sums, result, input_grad, parameters, float(tokens) ** (-0.5), places
    )
    updated = [a.transpose(turned[i // 3]) if i // 3 in turned else a for i, a in enumerate(updated)]
    return (result.reshape(shape), input_grad.reshape(shape), *updated)


def solution(mesh):
    split = P("batch", None, "lon", None)
    return jax.shard_map(
        per_device,
        mesh=mesh,
        in_specs=(split, split, P("batch", None), split) + (P(),) * 24,
        out_specs=(split, split) + (P(),) * 24,
        check_vma=False,
    )
```

```python
import functools
import math

import jax
import jax.numpy as jnp
from jax import lax
from jax.experimental import pallas as pl
from jax.experimental.pallas import tpu as pltpu
from jax.sharding import PartitionSpec as P

WINDOW = 8
HALF = WINDOW // 2
SPAN = WINDOW * WINDOW
HEADS = 8
LANES = 128
LAYERS = 2
WIDTH = 256
HIDDEN = 1024
LATENT = 32
OFFSETS = 2 * WINDOW - 1
PAIRS = OFFSETS * OFFSETS

LEARN_RATE = 0.2
MOMENTUM_RATE = 0.9
AVERAGE_DECAY = 0.5
NORM_EPS = 1e-05
MASK_FILL = -100.0
HEAD_WIDTH = WIDTH // HEADS
HEADS_A_HALF = LANES // HEAD_WIDTH
SCALE = HEAD_WIDTH ** (-0.5)
GELU_C = 0.7978845608028654
GELU_A = 0.044715

F32 = jnp.float32
BF16 = jnp.bfloat16
MESH = pl.DeviceIdType.MESH

SMALL_ROWS = 256
FEED_ROWS = HIDDEN * WIDTH // LANES
OUTPUT_ROWS = WIDTH * WIDTH // LANES
TRIPLE_ROWS = 3 * OUTPUT_ROWS
SHRINK_ONE, EXPAND_ONE, ATTEND_ONE, SHRINK_ZERO, EXPAND_ZERO, OUTPUT_ZERO, TRIPLE_ZERO = range(7)
SECTION_ROWS = (
    FEED_ROWS,
    FEED_ROWS,
    OUTPUT_ROWS + TRIPLE_ROWS,
    FEED_ROWS,
    FEED_ROWS,
    2 * OUTPUT_ROWS + LAYERS * SMALL_ROWS,
    2 * OUTPUT_ROWS,
)
ROW_TILE = 16
EARLY_ROWS = 5 * LATENT
TABLE_ROWS = 16


SECTION_PHASES = (
    ("core", "up", "line"),
    ("core", "down", "line"),
    ("core", "up", "line"),
    ("core", "lon", "line"),
    ("core", "lon", "line"),
    ("core", "lon", "line"),
    ("core", "both"),
)


class Places:
    def __init__(self, lon_count, batch_count):
        self.lon_count, self.line_count = lon_count, batch_count // 2
        self.ahead = lon_count * batch_count <= 32
        self.grant = (85 if self.ahead else 96) * 2**19
        unit = ROW_TILE * lon_count * batch_count
        few = self.few = unit <= 512
        self.few_members = lon_count * self.line_count if few else 1
        groups = [[i] for i in range(7)] if few else [[0, 1], [2], [3, 4], [5, 6]]
        self.leader = [group[-1] for group in groups for _ in group]
        self.first = [group[0] for group in groups for _ in group]
        self.rows, starts, at = {}, {}, 0
        for group in groups:
            begin = at
            for i in group:
                starts[i] = at
                at += SECTION_ROWS[i]
            rows = -(-(at - begin) // unit) * unit
            self.rows[group[-1]] = rows
            at = begin + rows
        self.total = at
        self.starts = starts
        self.phases, self.inbox, self.sems = {}, {}, {}
        bits = [1 << i for i in range(lon_count.bit_length() - 1)]
        inbox = 0
        for section, rows in self.rows.items():
            phases = []
            for name in SECTION_PHASES[section]:
                if name == "up":
                    phases += [("bit", bit, 2) for bit in bits]
                elif name == "down":
                    phases += [("bit", bit, 2) for bit in reversed(bits)]
                elif name == "both" and few:
                    phases.append((name, 0, lon_count * self.line_count))
                elif name == "both":
                    phases += [("lon", 0, lon_count), ("line", 0, self.line_count)]
                else:
                    phases.append((name, 0, {"core": 2, "lon": lon_count, "line": batch_count // 2}[name]))
            self.phases[section] = phases
            self.inbox[section], self.sems[section], sem = [], [], 0
            for _, _, members in phases:
                rows //= members
                self.inbox[section].append(inbox)
                self.sems[section].append(sem)
                inbox += rows * (members - 1)
                sem += members - 1
            for _, _, members in reversed(phases):
                self.sems[section].append(sem)
                sem += members - 1
        self.inbox_rows = inbox
        self.most_sems = max(2 * sum(m - 1 for _, _, m in phases) for phases in self.phases.values())
        self.shrink = (starts[SHRINK_ZERO], starts[SHRINK_ONE])
        self.expand = (starts[EXPAND_ZERO], starts[EXPAND_ONE])
        self.output = (starts[OUTPUT_ZERO], starts[ATTEND_ONE])
        self.triple = (
            (starts[TRIPLE_ZERO], starts[TRIPLE_ZERO] + OUTPUT_ROWS, starts[OUTPUT_ZERO] + OUTPUT_ROWS),
            tuple(starts[ATTEND_ONE] + i * OUTPUT_ROWS for i in (1, 2, 3)),
        )
        small = starts[OUTPUT_ZERO] + 2 * OUTPUT_ROWS
        self.early = (small, small + SMALL_ROWS)
        table = self.total if few else starts[TRIPLE_ZERO] + SECTION_ROWS[TRIPLE_ZERO]
        self.table = (table, small + SMALL_ROWS + EARLY_ROWS)
        self.sum_rows = self.total + (TABLE_ROWS if few else 0)
        self.spare = {}
        for section, rows in self.rows.items():
            begin = starts[self.first[section]]
            used = starts[section] + SECTION_ROWS[section]
            if section == TRIPLE_ZERO and not few:
                used += TABLE_ROWS
            self.spare[section] = (used, begin + rows)


def dot(a, b):
    return jnp.dot(a, b, preferred_element_type=F32)


def dot_nt(a, b):
    return lax.dot_general(a, b, (((1,), (1,)), ((), ())), preferred_element_type=F32)


def dot_tn(a, b):
    return lax.dot_general(a, b, (((0,), (0,)), ((), ())), preferred_element_type=F32)


def norm_parts(stream):
    center = stream - jnp.mean(stream, axis=-1, keepdims=True)
    inverse = lax.rsqrt(jnp.mean(center * center, axis=-1, keepdims=True) + NORM_EPS)
    return center * inverse, inverse


def norm_back(upstream, gain_row, scaled, inverse):
    weighted = upstream * gain_row
    along = jnp.mean(weighted * scaled, axis=-1, keepdims=True)
    return inverse * (weighted - jnp.mean(weighted, axis=-1, keepdims=True) - scaled * along)


def lower_slots(shape):
    return lax.broadcasted_iota(jnp.int32, shape, 1) < HALF


def pack_half(own):
    tokens, features = own.shape
    rows = own.reshape(tokens // WINDOW, WINDOW, features)
    count = tokens // WINDOW // 2
    moved = pltpu.roll(rows[count:], HALF, axis=1)
    return jnp.where(lower_slots(moved.shape), rows[:count], moved).reshape(tokens // 2, features)


def unpack_half(packed, own):
    tokens, features = own.shape
    pairs = packed.reshape(tokens // WINDOW // 2, WINDOW, features)
    full = jnp.concatenate([pairs, pltpu.roll(pairs, HALF, axis=1)], axis=0)
    rows = own.reshape(tokens // WINDOW, WINDOW, features)
    return jnp.where(lower_slots(full.shape), full, rows).reshape(tokens, features)


def rows_ahead(value):
    cut = HALF * WINDOW
    return jnp.concatenate([value[cut:], value[:cut]], axis=0)


def rows_behind(value):
    cut = value.shape[0] - HALF * WINDOW
    return jnp.concatenate([value[cut:], value[:cut]], axis=0)


def head_of_lane(shape):
    return lax.broadcasted_iota(jnp.int32, shape, 1) // HEAD_WIDTH


def spread_heads(block):
    lane_head = head_of_lane(block.shape)
    zero = jnp.zeros_like(block)
    return jnp.concatenate(
        [jnp.where(lane_head == head, block, zero) for head in range(HEADS_A_HALF)], axis=0
    )


def gather_heads(stacked):
    count = stacked.shape[0] // HEADS_A_HALF
    lane_head = head_of_lane((count, LANES))
    out = stacked[:count]
    for head in range(1, HEADS_A_HALF):
        out = jnp.where(lane_head == head, stacked[head * count : (head + 1) * count], out)
    return out


def half_lanes(half):
    return slice(half * LANES, (half + 1) * LANES)


def half_scores(half):
    return slice(half * HEADS_A_HALF * SPAN, (half + 1) * HEADS_A_HALF * SPAN)


def score_mask(crop_start, crop_end, shifted, window, row_count):
    shape = (SPAN, HEADS_A_HALF * SPAN)
    key_row = lax.broadcasted_iota(jnp.int32, shape, 0) // WINDOW
    source = key_row + window * WINDOW
    if shifted:
        source = source + HALF
        if window == row_count // WINDOW - 1:
            source = jnp.where(source >= row_count, source - row_count, source)
    allowed = (source >= crop_start) & (source < crop_end)
    if shifted and window == row_count // WINDOW - 1:
        query_row = lax.broadcasted_iota(jnp.int32, shape, 1) % SPAN // WINDOW
        allowed = allowed & ((key_row < HALF) == (query_row < HALF))
    return jnp.where(allowed, 0.0, MASK_FILL).astype(F32)


def offset_onehot(shifted):
    shape = (WINDOW * LANES, WIDTH)
    row = lax.broadcasted_iota(jnp.int32, shape, 0)
    key_col = row // LANES
    row_offset = row % LANES // WINDOW
    query_col = row % WINDOW
    if shifted:
        key_col = (key_col + HALF) % WINDOW
        query_col = (query_col + HALF) % WINDOW
    target = row_offset * OFFSETS + query_col - key_col + WINDOW - 1
    target = jnp.where(row_offset < OFFSETS, target, -1)
    pair = lax.broadcasted_iota(jnp.int32, shape, 1)
    return jnp.where(pair == target, 1.0, 0.0).astype(BF16)


def three_parts(value):
    high = value.astype(BF16)
    rest = value - high.astype(F32)
    middle = rest.astype(BF16)
    low = (rest - middle.astype(F32)).astype(BF16)
    return jnp.concatenate([high.astype(F32), middle.astype(F32), low.astype(F32)], axis=0).astype(BF16)


def swap_groups(tiles):
    return [jnp.concatenate([tile[b : b + 1] for tile in tiles], axis=0) for b in range(8)]


def bias_of_table(table, onehot):
    spread = dot_nt(three_parts(table), onehot)
    spread = spread[:HEADS] + (spread[HEADS : 2 * HEADS] + spread[2 * HEADS :])
    tiles = swap_groups([spread[:, col * LANES : (col + 1) * LANES] for col in range(WINDOW)])
    lane = lax.broadcasted_iota(jnp.int32, (WINDOW, LANES), 1)
    blocks = []
    for key_row in range(WINDOW):
        back = (WINDOW - 1 - key_row) * WINDOW
        pieces = []
        for pair in range(HEADS // 2):
            even = pltpu.roll(tiles[2 * pair], (LANES - back) % LANES, axis=1)
            odd = pltpu.roll(tiles[2 * pair + 1], (LANES + SPAN - back) % LANES, axis=1)
            pieces.append(jnp.where(lane < SPAN, even, odd))
        blocks.append(jnp.concatenate(pieces, axis=1))
    return jnp.concatenate(blocks, axis=0)


def table_of_bias(gathered, onehot):
    lane = lax.broadcasted_iota(jnp.int32, (WINDOW, LANES), 1)
    zero = jnp.zeros((WINDOW, LANES), F32)
    tiles = []
    for head in range(HEADS):
        total = None
        for key_row in range(WINDOW):
            forth = (WINDOW - 1 - key_row) * WINDOW
            block = gathered[key_row * WINDOW : (key_row + 1) * WINDOW, half_lanes(head // 2)]
            if head % 2 == 0:
                moved = pltpu.roll(jnp.where(lane < SPAN, block, zero), forth, axis=1)
            else:
                moved = pltpu.roll(jnp.where(lane < SPAN, zero, block), (forth + SPAN) % LANES, axis=1)
            total = moved if total is None else total + moved
        tiles.append(total)
    spread = jnp.concatenate(swap_groups(tiles), axis=1)
    parts = dot(three_parts(spread), onehot)
    return parts[:HEADS] + (parts[HEADS : 2 * HEADS] + parts[2 * HEADS :])


def attend_forward(qkv, bias_ref, layer, crop, probs_ref, frame, row_count):
    shifted = layer % 2 == 1
    units = [(window, half) for window in range(row_count // WINDOW) for half in range(2)]
    piece = lambda which, window, half: qkv[
        window * SPAN : (window + 1) * SPAN, which * WIDTH + half * LANES : which * WIDTH + (half + 1) * LANES
    ]
    masks = [
        score_mask(crop[0], crop[1], shifted, window, row_count) for window in range(row_count // WINDOW)
    ]
    scores = [dot_nt(piece(1, *unit), spread_heads(piece(0, *unit))) for unit in units]
    probs = []
    for (window, half), score in zip(units, scores):
        score = score * SCALE + bias_ref[layer, :, half_scores(half)] + masks[window]
        exponent = jnp.exp(score - jnp.max(score, axis=0, keepdims=True))
        low = (exponent * (1.0 / jnp.sum(exponent, axis=0, keepdims=True))).astype(BF16)
        at = (frame * (row_count // WINDOW) + window) * SPAN
        probs_ref[layer, pl.ds(pl.multiple_of(at, SPAN), SPAN), half_scores(half)] = low
        probs.append(low)
    outs = [gather_heads(dot_tn(low, piece(2, *unit))) for unit, low in zip(units, probs)]
    return jnp.concatenate(
        [jnp.concatenate(outs[i : i + 2], axis=1) for i in range(0, len(outs), 2)], axis=0
    )


def value_grads(dcontext, layer, probs_ref, frame, row_count):
    windows = []
    for window in range(row_count // WINDOW):
        rows = slice(window * SPAN, (window + 1) * SPAN)
        at = (frame * (row_count // WINDOW) + window) * SPAN
        halves = []
        for half in range(2):
            low = probs_ref[layer, pl.ds(pl.multiple_of(at, SPAN), SPAN), half_scores(half)]
            halves.append(dot(low, spread_heads(dcontext[rows, half_lanes(half)])))
        windows.append(jnp.concatenate(halves, axis=1))
    return jnp.concatenate(windows, axis=0).astype(BF16)


def attend_backward(qkv, dcontext, layer, probs_ref, frame, gathered_ref, row_count):
    units = [(window, half) for window in range(row_count // WINDOW) for half in range(2)]
    piece = lambda which, window, half: qkv[
        window * SPAN : (window + 1) * SPAN, which * WIDTH + half * LANES : which * WIDTH + (half + 1) * LANES
    ]
    dprobs = [
        dot_nt(
            piece(2, window, half),
            spread_heads(dcontext[window * SPAN : (window + 1) * SPAN, half_lanes(half)]),
        )
        for window, half in units
    ]
    lows = []
    gathered = [None, None]
    for (window, half), dprob in zip(units, dprobs):
        at = (frame * (row_count // WINDOW) + window) * SPAN
        probs = probs_ref[layer, pl.ds(pl.multiple_of(at, SPAN), SPAN), half_scores(half)].astype(F32)
        dscores = probs * (dprob - jnp.sum(probs * dprob, axis=0, keepdims=True))
        gathered_ref[layer, :, half_scores(half)] += dscores
        lows.append(dscores.astype(BF16))
    dks = [dot(low, spread_heads(piece(0, *unit))) * SCALE for unit, low in zip(units, lows)]
    dqs = [gather_heads(dot_tn(low, piece(1, *unit))) * SCALE for unit, low in zip(units, lows)]
    return [
        jnp.concatenate(
            [jnp.concatenate(d[i : i + 2], axis=1) for i in range(0, len(d), 2)], axis=0
        ).astype(BF16)
        for d in (dqs, dks)
    ]


STEPS = {
    "second_middle_back": (),
    "second_back": (
        (0, SHRINK_ONE, 0),
        (0, EXPAND_ONE, 0),
        (2, SHRINK_ONE, 1),
        (2, EXPAND_ONE, 1),
    ),
    "first_feed_back": ((0, SHRINK_ONE, 2), (1, EXPAND_ONE, 2), (2, ATTEND_ONE, 0)),
    "after_shrink": (),
    "first_middle_back": (
        (0, SHRINK_ONE, 3),
        (0, ATTEND_ONE, 1),
        (1, EXPAND_ONE, 3),
        (2, SHRINK_ZERO, 0),
        (2, EXPAND_ZERO, 0),
        (3, ATTEND_ONE, 2),
    ),
    "after_output": ((SHRINK_ONE, 4), (EXPAND_ONE, 4)),
    "first_back": (
        (0, SHRINK_ZERO, 1),
        (0, OUTPUT_ZERO, 0),
        (0, ATTEND_ONE, 3),
        (1, SHRINK_ONE, 5),
        (1, EXPAND_ZERO, 1),
        (1, EXPAND_ONE, 5),
        (2, SHRINK_ZERO, 2),
        (2, ATTEND_ONE, 4),
        (3, SHRINK_ONE, 6),
        (3, OUTPUT_ZERO, 1),
        (3, EXPAND_ONE, 6),
        (3, EXPAND_ZERO, 2),
    ),
    "last_back": ((0, TRIPLE_ZERO, 0), (2, SHRINK_ZERO, 3), (3, EXPAND_ZERO, 3)),
    "last": (
        (OUTPUT_ZERO, 2),
        (ATTEND_ONE, 5),
        (SHRINK_ONE, 7),
        (EXPAND_ONE, 7),
        (TRIPLE_ZERO, 1),
        (OUTPUT_ZERO, 3),
        (SHRINK_ZERO, 4),
        (ATTEND_ONE, 6),
        (EXPAND_ZERO, 4),
        (ATTEND_ONE, 7),
        (OUTPUT_ZERO, 4),
        (TRIPLE_ZERO, 2),
        (SHRINK_ZERO, 5),
        (EXPAND_ZERO, 5),
        (OUTPUT_ZERO, 5),
        (TRIPLE_ZERO, 3),
    ),
}


def kernel(
    places,
    crop_ref,
    gains_ref,
    table_ref,
    frames_hbm,
    latent_hbm,
    cotangent_hbm,
    *refs,
):
    wide_hbm = refs[:12]
    recurrent_hbm, readout_hbm, act_out_hbm, input_grad_hbm, sums_ref = refs[12:17]
    held = refs[17 : 17 + (12 if places.ahead else 4)]
    (
        frames_ref,
        latent_ref,
        cotangent_ref,
        input_grad_ref,
        recurrent_wide,
        readout_wide,
        triple_low,
        output_low,
        expand_low,
        shrink_low,
        recurrent_low,
        readout_low,
        table_pad,
        bias_ref,
        gathered_ref,
        stream_in,
        stream_one,
        stream_two,
        normed_ref,
        qkv_ref,
        probs_ref,
        context_ref,
        cell_ref,
        bend_ref,
        state_ref,
        hidden_ref,
        active_ref,
        slope_ref,
        g_ref,
        gm_ref,
        gl_ref,
        gc_ref,
        gpre_ref,
        gstate_ref,
        dcontext_ref,
        dpacked_ref,
        out_halo,
        in_halo,
        grads_ref,
        sum_in,
        table_own,
        table_in,
        send_sem,
        recv_sem,
        sum_send_sem,
        sum_recv_sem,
        table_send_sem,
        table_recv_sem,
        weight_sem,
        token_sem,
        result_sem,
    ) = refs[17 + len(held) :]
    lon_count, line_count = places.lon_count, places.line_count
    frame_count = crop_ref.shape[1]
    tokens = frames_ref.shape[0] // frame_count
    row_count = tokens // WINDOW
    me_lon = lax.axis_index("lon")
    ahead = lax.rem(me_lon + 1, lon_count)
    behind = lax.rem(me_lon + lon_count - 1, lon_count)

    me_batch = lax.axis_index("batch")
    core, line = lax.rem(me_batch, 2), lax.div(me_batch, 2)
    lon_peers = [lax.rem(me_lon + by, lon_count) for by in range(1, lon_count)]
    line_peers = [lax.rem(line + by, line_count) for by in range(1, line_count)]
    neighbours = [{"batch": 2 * line + 1 - core}]
    if places.few:
        for i in range(1, lon_count * line_count):
            at = lax.rem(line + i % line_count, line_count)
            lon = lax.rem(me_lon + i // line_count, lon_count)
            neighbours.append({"lon": lon, "batch": 2 * at + core})
    else:
        neighbours += [{"lon": peer} for peer in lon_peers]
        neighbours += [{"batch": 2 * peer + core} for peer in line_peers]

    barrier = pltpu.get_barrier_semaphore()
    for peer in neighbours:
        pl.semaphore_signal(barrier, inc=1, device_id=peer, device_id_type=MESH)

    def row_span(start, rows):
        return pl.ds(pl.multiple_of(start, ROW_TILE), rows)

    def members_of(kind, bit):
        if kind == "core":
            return core, [(1 - core, neighbours[0])]
        if kind == "lon":
            return me_lon, [(peer, {"lon": peer}) for peer in lon_peers]
        if kind == "both":
            others = []
            for i in range(1, lon_count * line_count):
                lon = lax.rem(me_lon + i // line_count, lon_count)
                at = lax.rem(line + i % line_count, line_count)
                others.append((lon * line_count + at, {"lon": lon, "batch": 2 * at + core}))
            return me_lon * line_count + line, others
        if kind == "line":
            return line, [(peer, {"batch": 2 * peer + core}) for peer in line_peers]
        mine = lax.rem(lax.div(me_lon, bit), 2)
        return mine, [(1 - mine, {"lon": me_lon + bit - 2 * bit * mine})]

    def sum_range(section, depth):
        start, rows = places.starts[places.first[section]], places.rows[section]
        for kind, bit, members in places.phases[section][:depth]:
            rows //= members
            start = start + members_of(kind, bit)[0] * rows
        return start, rows

    def sum_copies(section, phase):
        phases = places.phases[section]
        back = phase >= len(phases)
        depth = 2 * len(phases) - 1 - phase if back else phase
        kind, bit, members = phases[depth]
        start, rows = sum_range(section, depth)
        piece = rows // members
        mine, others = members_of(kind, bit)
        copies = []
        for i, (place, device) in enumerate(others):
            if back:
                rows_out = row_span(start + mine * piece, piece)
                src, dst = sums_ref.at[rows_out], sums_ref.at[rows_out]
            else:
                src = grads_ref.at[row_span(start + place * piece, piece)]
                dst = sum_in.at[row_span(places.inbox[section][phase] + i * piece, piece)]
            sem = places.sems[section][phase] + i
            copies.append(
                pltpu.make_async_remote_copy(
                    src_ref=src,
                    dst_ref=dst,
                    send_sem=sum_send_sem.at[section, sem],
                    recv_sem=sum_recv_sem.at[section, sem],
                    device_id=device,
                    device_id_type=MESH,
                )
            )
        return copies

    def add_up(start, rows, source_at, count, target):
        step = math.gcd(rows, LANES)

        def body(i, unused):
            at = row_span(start + i * step, step)
            total = grads_ref[at].astype(F32)
            for k in range(count):
                total = total + sum_in[row_span(source_at + k * rows + i * step, step)].astype(F32)
            target[at] = total.astype(BF16)

        lax.fori_loop(0, rows // step, body, None)

    def sum_start(section, phase=0):
        if places.leader[section] == section:
            for copy in sum_copies(section, phase):
                copy.start()

    def sum_step(section, phase):
        if places.leader[section] != section:
            return
        for copy in sum_copies(section, phase):
            copy.wait_recv()
        depth = len(places.phases[section])
        if phase < depth:
            start, rows = sum_range(section, phase + 1)
            target = grads_ref if phase < depth - 1 else sums_ref
            add_up(start, rows, places.inbox[section][phase], places.phases[section][phase][2] - 1, target)
        if phase < 2 * depth - 1:
            sum_start(section, phase + 1)

    def sum_drain(section):
        for phase in range(2 * len(places.phases[section])):
            for copy in sum_copies(section, phase):
                copy.wait_send()

    def halo(exchange, frame):
        return pltpu.make_async_remote_copy(
            src_ref=out_halo.at[exchange % 2, frame],
            dst_ref=in_halo.at[exchange % 2, frame],
            send_sem=send_sem.at[exchange, frame],
            recv_sem=recv_sem.at[exchange, frame],
            device_id={"lon": behind if exchange % 2 == 0 else ahead},
            device_id_type=MESH,
        )

    def send_halo(exchange, frame, value):
        if exchange >= 2:
            halo(exchange - 2, frame).wait_send()
        out_halo[exchange % 2, frame] = pack_half(value).astype(BF16)
        halo(exchange, frame).start()

    def take_halo(exchange, frame, own):
        halo(exchange, frame).wait_recv()
        return unpack_half(in_halo[exchange % 2, frame].astype(F32), own)

    tokens_in = [
        pltpu.make_async_copy(hbm, ref, token_sem.at[i])
        for i, (hbm, ref) in enumerate(
            ((frames_hbm, frames_ref), (latent_hbm, latent_ref), (cotangent_hbm, cotangent_ref))
        )
    ]

    def wide_in(which, kind, layer):
        at = 3 * which + kind if places.ahead else which
        return pltpu.make_async_copy(
            wide_hbm[3 * which + kind].at[layer], held[at].at[layer], weight_sem.at[3 * which + kind, layer]
        )

    small_in = [
        pltpu.make_async_copy(recurrent_hbm, recurrent_wide, token_sem.at[3]),
        pltpu.make_async_copy(readout_hbm, readout_wide, token_sem.at[4]),
    ]

    def weights_take(which, layer):
        wide_in(which, 0, layer).wait()
        low = (triple_low, output_low, expand_low, shrink_low)[which]
        wide = held[3 * which if places.ahead else which]
        step = 64

        def body(i, unused):
            at = pl.ds(pl.multiple_of(i * step, step), step)
            low[layer, at] = wide[layer, at].astype(BF16)

        lax.fori_loop(0, wide.shape[1] // step, body, None)

    tokens_in[0].start()
    wide_in(0, 0, 0).start()
    tokens_in[1].start()
    for copy in small_in:
        copy.start()
    for which in (1, 2, 3):
        wide_in(which, 0, 0).start()
    for which in range(4):
        wide_in(which, 0, 1).start()
    tokens_in[2].start()

    for layer, onehot_ref in ((0, gm_ref), (1, gl_ref)):
        table_pad[...] = jnp.zeros_like(table_pad)
        table_pad[:, :PAIRS] = table_ref[layer]
        onehot_ref[...] = offset_onehot(layer % 2 == 1)
        bias_ref[layer] = bias_of_table(table_pad[...], onehot_ref[...])
    for copy in small_in:
        copy.wait()
    for layer in range(LAYERS):
        recurrent_low[layer] = recurrent_wide[layer].astype(BF16)
        readout_low[layer] = readout_wide[layer].astype(BF16)
    tokens_in[0].wait()
    tokens_in[1].wait()
    for which in range(4):
        weights_take(which, 0)
    pl.semaphore_wait(barrier, len(neighbours))
    gathered_ref[...] = jnp.zeros_like(gathered_ref)

    def span(frame):
        return pl.ds(pl.multiple_of(frame * tokens, tokens), tokens)

    def gain(layer, which):
        return gains_ref[which, layer : layer + 1, :]

    def attention_part(layer, frame, normed):
        at = span(frame)
        normed_ref[layer, at] = normed
        qkv = dot(normed, triple_low[layer]).astype(BF16)
        qkv_ref[layer, at] = qkv
        crop = (crop_ref[0, frame], crop_ref[1, frame])
        return attend_forward(qkv, bias_ref, layer, crop, probs_ref, frame, row_count)

    def middle(layer, frame, stream, context, latent):
        at = span(frame)
        context_ref[layer, at] = context
        one = stream + dot(context, output_low[layer])
        (stream_one, input_grad_ref)[layer][at] = one
        scaled, _ = norm_parts(one)
        cell = (scaled * gain(layer, 2)).astype(BF16)
        cell_ref[layer, at] = cell
        preact = dot_nt(cell, recurrent_low[layer, :, :WIDTH]) + dot_nt(latent, recurrent_low[layer, :, WIDTH:])
        tangent = jnp.tanh(preact)
        bend_ref[layer, at] = (1.0 - tangent * tangent).astype(BF16)
        state = tangent.astype(BF16)
        state_ref[layer, at] = state
        two = one + dot(state, readout_low[layer])
        (stream_two, g_ref)[layer][at] = two
        scaled, _ = norm_parts(two)
        hidden = (scaled * gain(layer, 1)).astype(BF16)
        hidden_ref[layer, at] = hidden
        for block in range(HIDDEN // WIDTH):
            cols = slice(block * WIDTH, (block + 1) * WIDTH)
            inner = dot(hidden, expand_low[layer, :, cols])
            square = inner * inner
            bend = GELU_C * (1.0 + GELU_A * square)
            gate = 0.5 * (1.0 + jnp.tanh(inner * bend))
            active = inner * gate
            slope = gate + active * (1.0 - gate) * (2.0 * GELU_C + 6.0 * GELU_C * GELU_A * square)
            active_ref[layer, at, cols] = active.astype(BF16)
            slope_ref[layer, at, cols] = slope.astype(BF16)
        return two + dot(active_ref[layer, at], shrink_low[layer])

    def feed_back(layer, frame, g):
        at = span(frame)
        gm = g.astype(BF16)
        gm_ref[at] = gm
        for block in range(HIDDEN // WIDTH):
            cols = slice(block * WIDTH, (block + 1) * WIDTH)
            dactive = dot_nt(gm, shrink_low[layer, cols])
            slope_ref[layer, at, cols] = (dactive * slope_ref[layer, at, cols].astype(F32)).astype(BF16)

    def middle_back(layer, frame, g, gstate):
        at = span(frame)
        dhidden = dot_nt(slope_ref[layer, at], expand_low[layer])
        scaled, inverse = norm_parts((stream_two, g_ref)[layer][at])
        g = g + norm_back(dhidden, gain(layer, 1), scaled, inverse)
        gl = g.astype(BF16)
        gl_ref[at] = gl
        dstate = dot_nt(gl, readout_low[layer])
        if gstate is not None:
            dstate = dstate + gstate
        gpre = (dstate * bend_ref[layer, at].astype(F32)).astype(BF16)
        gpre_ref[at] = gpre
        if layer > 0:
            gstate_ref[at] = dot(gpre, recurrent_low[layer, :, WIDTH:])
        scaled, inverse = norm_parts((stream_one, input_grad_ref)[layer][at])
        dcell = dot(gpre, recurrent_low[layer, :, :WIDTH])
        g = g + norm_back(dcell, gain(layer, 2), scaled, inverse)
        gc = g.astype(BF16)
        gc_ref[at] = gc
        g_ref[at] = g
        return dot_nt(gc, output_low[layer])

    def values_back(layer, frame, dcontext):
        dpacked_ref[span(frame), 2 * WIDTH :] = value_grads(dcontext, layer, probs_ref, frame, row_count)

    def attention_back(layer, frame, dcontext):
        at = span(frame)
        pieces = attend_backward(
            qkv_ref[layer, at], dcontext, layer, probs_ref, frame, gathered_ref, row_count
        )
        for which in range(2):
            dpacked_ref[at, which * WIDTH : (which + 1) * WIDTH] = pieces[which]

    def packed_back(layer, frame):
        return dot_nt(dpacked_ref[span(frame)], triple_low[layer])

    def stream_back(layer, frame, g, stream, dnormed):
        scaled, inverse = norm_parts(stream)
        return g + norm_back(dnormed, gain(layer, 0), scaled, inverse)

    def put_blocks(start, value):
        rows = value.shape[0]
        for block in range(value.shape[1] // LANES):
            grads_ref[start + block * rows : start + (block + 1) * rows] = value[
                :, half_lanes(block)
            ].astype(BF16)

    def put_rows(start, total_rows, row, value):
        rows = value.shape[0]
        for block in range(value.shape[1] // LANES):
            at = start + block * total_rows + row
            grads_ref[at : at + rows] = value[:, half_lanes(block)].astype(BF16)

    def shrink_grads(layer):
        for block in range(HIDDEN // WIDTH):
            cols = slice(block * WIDTH, (block + 1) * WIDTH)
            put_rows(
                places.shrink[layer], HIDDEN, block * WIDTH, dot_tn(active_ref[layer, :, cols], gm_ref[...])
            )

    def expand_grads(layer):
        for block in range(HIDDEN // WIDTH):
            cols = slice(block * WIDTH, (block + 1) * WIDTH)
            put_blocks(
                places.expand[layer] + 2 * block * WIDTH, dot_tn(hidden_ref[layer], slope_ref[layer, :, cols])
            )

    def small_grads(layer, latent):
        near = dot_tn(gpre_ref[...], cell_ref[layer])
        far = dot_tn(gpre_ref[...], latent)
        far = jnp.concatenate([far, jnp.zeros((LATENT, LANES - LATENT), F32)], axis=1)
        readout = dot_tn(state_ref[layer], gl_ref[...])
        return [near[:, :LANES], near[:, LANES:], far, readout[:, :LANES], readout[:, LANES:]]

    def table_pieces(layer):
        gm_ref[...] = offset_onehot(layer % 2 == 1)
        table = table_of_bias(gathered_ref[layer], gm_ref[...])
        return [table[:, :LANES], table[:, LANES:]]

    def put_pieces(start, pieces):
        used = sum(piece.shape[0] for piece in pieces)
        value = jnp.concatenate(pieces, axis=0).astype(BF16)
        grads_ref[start : start + used] = value
        return start + used

    def clear_spare(section):
        if section in places.spare:
            clear_rows(*places.spare[section])

    def clear_rows(start, stop):
        if stop > start:
            grads_ref[start:stop] = jnp.zeros((stop - start, LANES), BF16)

    def output_grads(layer):
        put_blocks(places.output[layer], dot_tn(context_ref[layer], gc_ref[...]))

    def triple_grads(layer, blocks):
        for block in blocks:
            cols = slice(block * WIDTH, (block + 1) * WIDTH)
            put_blocks(places.triple[layer][block], dot_tn(normed_ref[layer], dpacked_ref[:, cols]))

    def table_core():
        here = row_span(0, TABLE_ROWS)
        return pltpu.make_async_remote_copy(
            src_ref=table_own.at[here],
            dst_ref=table_in.at[row_span(members * TABLE_ROWS, TABLE_ROWS)],
            send_sem=table_send_sem.at[0],
            recv_sem=table_recv_sem.at[0],
            device_id=neighbours[0],
            device_id_type=MESH,
        )

    members = lon_count * line_count

    def table_copies():
        mine = row_span((me_lon * line_count + line) * TABLE_ROWS, TABLE_ROWS)
        return [
            pltpu.make_async_remote_copy(
                src_ref=table_in.at[mine],
                dst_ref=table_in.at[mine],
                send_sem=table_send_sem.at[1 + i],
                recv_sem=table_recv_sem.at[1 + i],
                device_id=device,
                device_id_type=MESH,
            )
            for i, (_, device) in enumerate(members_of("both", 0)[1])
        ]

    def table_start():
        table_own[...] = jnp.concatenate(table_pieces(0), axis=0).astype(BF16)
        table_core().start()

    def table_spread():
        table_core().wait_recv()
        other = table_in[members * TABLE_ROWS : (members + 1) * TABLE_ROWS].astype(F32)
        mine = row_span((me_lon * line_count + line) * TABLE_ROWS, TABLE_ROWS)
        table_in[mine] = (table_own[...].astype(F32) + other).astype(BF16)
        for copy in table_copies():
            copy.start()

    def table_take():
        for copy in table_copies():
            copy.wait_recv()
        total = table_in[:TABLE_ROWS].astype(F32)
        for i in range(1, members):
            total = total + table_in[i * TABLE_ROWS : (i + 1) * TABLE_ROWS].astype(F32)
        sums_ref[places.table[0] : places.table[0] + TABLE_ROWS] = total.astype(BF16)

    def loop(body, steps=()):
        def whole(frame, unused):
            body(frame)
            for after in range(frame_count):
                here = [(section, phase) for when, section, phase in steps if when == after]
                if here:

                    @pl.when(frame == after)
                    def _(here=here):
                        for section, phase in here:
                            sum_step(section, phase)

        lax.fori_loop(0, frame_count, whole, None)

    def sum_steps(*steps):
        for section, phase in steps:
            sum_step(section, phase)

    def first_layer(frame):
        at = span(frame)
        stream = frames_ref[at].astype(F32)
        scaled, _ = norm_parts(stream)
        normed = (scaled * gain(0, 0)).astype(BF16)
        context = attention_part(0, frame, normed).astype(BF16)
        stream = middle(0, frame, stream, context, latent_ref[at])
        stream_in[at] = stream
        scaled, _ = norm_parts(stream)
        normed = scaled * gain(1, 0)
        normed_ref[1, at] = normed.astype(BF16)
        send_halo(0, frame, normed)

    loop(first_layer)
    for which in range(4):
        weights_take(which, 1)
    if places.ahead:
        for layer in (1, 0):
            for which in range(4):
                for kind in (1, 2):
                    wide_in(which, kind, layer).start()

    def second_attention(frame):
        at = span(frame)
        normed = take_halo(0, frame, normed_ref[1, at].astype(F32))
        context = attention_part(1, frame, rows_ahead(normed).astype(BF16))
        context = rows_behind(context)
        context_ref[1, at] = context.astype(BF16)
        send_halo(1, frame, context)

    loop(second_attention)
    tokens_in[2].wait()

    def second_middle(frame):
        at = span(frame)
        context = take_halo(1, frame, context_ref[1, at].astype(F32)).astype(BF16)
        stream = middle(1, frame, stream_in[at], context, state_ref[0, at])
        feed_back(1, frame, cotangent_ref[at].astype(F32))
        cotangent_ref[at] = stream.astype(BF16)

    loop(second_middle)
    act_out = pltpu.make_async_copy(cotangent_ref, act_out_hbm, result_sem.at[frame_count])
    act_out.start()
    shrink_grads(1)
    sum_start(SHRINK_ONE)
    expand_grads(1)
    sum_start(EXPAND_ONE)

    def second_middle_back(frame):
        at = span(frame)
        dcontext = middle_back(1, frame, gm_ref[at].astype(F32), None)
        dcontext_ref[at] = dcontext.astype(BF16)
        send_halo(2, frame, dcontext)

    loop(second_middle_back, STEPS["second_middle_back"])
    output_grads(1)
    early_one = put_pieces(places.early[1], small_grads(1, state_ref[0]))

    def second_back(frame):
        at = span(frame)
        dcontext = take_halo(2, frame, dcontext_ref[at].astype(F32))
        dcontext = rows_ahead(dcontext).astype(BF16)
        values_back(1, frame, dcontext)
        attention_back(1, frame, dcontext)
        dnormed = rows_behind(packed_back(1, frame))
        dcontext_ref[at] = dnormed.astype(BF16)
        send_halo(3, frame, dnormed)

    loop(second_back, STEPS["second_back"])
    triple_grads(1, (0, 1, 2))
    clear_spare(ATTEND_ONE)
    sum_start(ATTEND_ONE)

    def first_feed_back(frame):
        at = span(frame)
        dnormed = take_halo(3, frame, dcontext_ref[at].astype(F32))
        g = stream_back(1, frame, g_ref[at], stream_in[at], dnormed)
        g_ref[at] = g
        feed_back(0, frame, g)

    loop(first_feed_back, STEPS["first_feed_back"])
    shrink_grads(0)
    sum_start(SHRINK_ZERO)
    sum_steps(*STEPS["after_shrink"])
    expand_grads(0)
    sum_start(EXPAND_ZERO)

    def first_middle_back(frame):
        at = span(frame)
        dcontext = middle_back(0, frame, g_ref[at], gstate_ref[at]).astype(BF16)
        dcontext_ref[at] = dcontext
        values_back(0, frame, dcontext)

    loop(first_middle_back, STEPS["first_middle_back"])
    output_grads(0)
    triple_grads(0, (2,))
    clear_rows(put_pieces(early_one, table_pieces(1)), places.early[1] + SMALL_ROWS)
    clear_rows(put_pieces(places.early[0], small_grads(0, latent_ref[...])), places.early[1])
    clear_spare(OUTPUT_ZERO)
    sum_start(OUTPUT_ZERO)
    sum_steps(*STEPS["after_output"])

    def grad_out(frame):
        at = span(frame)
        return pltpu.make_async_copy(input_grad_ref.at[at], input_grad_hbm.at[at], result_sem.at[frame])

    def first_back(frame):
        attention_back(0, frame, dcontext_ref[span(frame)])

    loop(first_back, STEPS["first_back"])
    triple_grads(0, (0, 1))
    if not places.few:
        put_pieces(places.table[0], table_pieces(0))
        clear_spare(TRIPLE_ZERO)
    sum_start(TRIPLE_ZERO)
    if places.few:
        table_start()

    def last_back(frame):
        at = span(frame)
        stream = frames_ref[at].astype(F32)
        input_grad_ref[at] = stream_back(0, frame, g_ref[at], stream, packed_back(0, frame))
        grad_out(frame).start()

    loop(last_back, STEPS["last_back"])
    if places.few:
        table_spread()
    sum_steps(*STEPS["last"])
    if places.few:
        table_take()
        table_core().wait_send()
        for copy in table_copies():
            copy.wait_send()

    def drain(frame, unused):
        for exchange in (2, 3):
            halo(exchange, frame).wait_send()
        grad_out(frame).wait()

    lax.fori_loop(0, frame_count, drain, None)
    act_out.wait()
    if places.ahead:
        for layer in (1, 0):
            for which in range(4):
                for kind in (1, 2):
                    wide_in(which, kind, layer).wait()
    for section in places.rows:
        sum_drain(section)


def flat_tokens(array):
    return array.reshape(-1, array.shape[-1])


def in_hbm(array):
    return pltpu.with_memory_space_constraint(array, pltpu.HBM)


def layers_step(frames, latent, crop_band, cotangent, parameters, places):
    frame_count, row_count, col_count, features = frames.shape
    count = frame_count * row_count * col_count
    tokens = row_count * col_count
    vmem = pl.BlockSpec(memory_space=pltpu.VMEM)
    hbm = pl.BlockSpec(memory_space=pltpu.HBM)
    both = lambda *shape: pltpu.VMEM((LAYERS,) + shape, BF16)
    one = lambda *shape: pltpu.VMEM(shape, BF16)
    wide = lambda *shape: pltpu.VMEM(shape, F32)
    scratch = [
        one(count, WIDTH),
        one(count, LATENT),
        one(count, WIDTH),
        wide(count, WIDTH),
        wide(LAYERS, LATENT, WIDTH + LATENT),
        wide(LAYERS, LATENT, WIDTH),
        both(WIDTH, 3 * WIDTH),
        both(WIDTH, WIDTH),
        both(WIDTH, HIDDEN),
        both(HIDDEN, WIDTH),
        both(LATENT, WIDTH + LATENT),
        both(LATENT, WIDTH),
        wide(HEADS, WIDTH),
        wide(LAYERS, SPAN, HEADS * SPAN),
        wide(LAYERS, SPAN, HEADS * SPAN),
        wide(count, WIDTH),
        wide(count, WIDTH),
        wide(count, WIDTH),
        both(count, WIDTH),
        both(count, 3 * WIDTH),
        both(count, HEADS * SPAN),
        both(count, WIDTH),
        both(count, WIDTH),
        both(count, LATENT),
        both(count, LATENT),
        both(count, WIDTH),
        both(count, HIDDEN),
        both(count, HIDDEN),
        wide(count, WIDTH),
        one(count, WIDTH),
        one(count, WIDTH),
        one(count, WIDTH),
        one(count, LATENT),
        wide(count, LATENT),
        one(count, WIDTH),
        one(count, 3 * WIDTH),
        one(2, frame_count, tokens // 2, WIDTH),
        one(2, frame_count, tokens // 2, WIDTH),
        one(places.total, LANES),
        one(places.inbox_rows, LANES),
        one(TABLE_ROWS, LANES),
        one((places.few_members + 1) * TABLE_ROWS, LANES),
        pltpu.SemaphoreType.DMA((4, frame_count)),
        pltpu.SemaphoreType.DMA((4, frame_count)),
        pltpu.SemaphoreType.DMA((len(SECTION_ROWS), places.most_sems)),
        pltpu.SemaphoreType.DMA((len(SECTION_ROWS), places.most_sems)),
        pltpu.SemaphoreType.DMA((places.few_members,)),
        pltpu.SemaphoreType.DMA((places.few_members,)),
        pltpu.SemaphoreType.DMA((12, LAYERS)),
        pltpu.SemaphoreType.DMA((5,)),
        pltpu.SemaphoreType.DMA((frame_count + 1,)),
    ]
    wide_parameters = parameters[:12]
    recurrent, readout, gains, table = parameters[12::3]
    held = [a for i, a in enumerate(wide_parameters) if places.ahead or i % 3 == 0]
    given = (frames, latent, cotangent)
    outs = pl.pallas_call(
        functools.partial(kernel, places),
        out_shape=(
            pltpu.HBM((count, WIDTH), BF16),
            pltpu.HBM((count, WIDTH), F32),
            pltpu.VMEM((places.sum_rows, LANES), BF16),
        )
        + tuple(pltpu.VMEM(a.shape, F32) for a in held),
        in_specs=[pl.BlockSpec(memory_space=pltpu.SMEM), vmem, vmem] + [hbm] * 17,
        out_specs=(hbm, hbm, vmem) + (vmem,) * len(held),
        scratch_shapes=scratch,
        compiler_params=pltpu.CompilerParams(
            collective_id=0, has_side_effects=True, vmem_limit_bytes=places.grant
        ),
        name="swin_step",
    )(
        crop_band.T,
        gains,
        table,
        *(in_hbm(flat_tokens(a)) for a in given),
        *(in_hbm(a) for a in wide_parameters),
        in_hbm(recurrent),
        in_hbm(readout),
    )
    return outs[0], outs[1], outs[2], outs[3:]


def update_kernel(scale, places, sums, result_hbm, grad_hbm, *refs):
    count = 24
    given, result_out, grad_out = refs[:count], refs[count], refs[count + 1]
    made, held = refs[count + 2 : 2 * count + 2], refs[2 * count + 2 : 3 * count + 2]
    result_held, products, pass_sem, in_sem, out_sem = refs[3 * count + 2 :]
    triple, output, expand, shrink, recurrent, readout, gains, table = range(8)
    grad_held = held[3 * shrink].at[0]

    passing_in = [
        pltpu.make_async_copy(result_hbm, result_held, pass_sem.at[0]),
        pltpu.make_async_copy(grad_hbm, grad_held, pass_sem.at[1]),
    ]
    passing_out = [
        pltpu.make_async_copy(result_held, result_out, pass_sem.at[2]),
        pltpu.make_async_copy(grad_held, grad_out, pass_sem.at[3]),
    ]
    units = [
        (shrink, 1),
        (expand, 1),
        (triple, 1),
        (output, 1),
        (shrink, 0),
        (expand, 0),
        (output, 0),
        (triple, 0),
        (recurrent, None),
        (readout, None),
        (table, None),
        (gains, None),
    ]

    def part(ref, layer):
        return ref if layer is None else ref.at[layer]

    def is_held(which, kind):
        return which < recurrent and (places.ahead or kind == 0)

    def coming(index):
        which, layer = units[index]
        return [
            pltpu.make_async_copy(
                part(given[3 * which + i], layer), part(held[3 * which + i], layer), in_sem.at[index, i]
            )
            for i in range(3)
            if not is_held(which, i)
        ]

    def going(index):
        which, layer = units[index]
        return [
            pltpu.make_async_copy(
                part(held[3 * which + i], layer), part(made[3 * which + i], layer), out_sem.at[index, i]
            )
            for i in range(3)
        ]

    for index in range(len(units)):
        for copy in coming(index):
            copy.start()
    for copy in passing_in:
        copy.start()

    def change(which, at, summed):
        old = [(given if is_held(which, i) else held)[3 * which + i][at] for i in range(3)]
        weight, moment, average = held[3 * which : 3 * which + 3]
        gradient = summed.astype(F32) * scale
        velocity = MOMENTUM_RATE * old[1] + gradient
        updated = old[0] - LEARN_RATE * (gradient + MOMENTUM_RATE * velocity)
        average[at] = AVERAGE_DECAY * old[2] + (1.0 - AVERAGE_DECAY) * updated
        weight[at] = updated
        moment[at] = velocity
        return old[0].astype(BF16).astype(F32) * gradient

    def change_blocks(which, layer, starts, rows, norm=None):
        step = 32

        def body(i, unused):
            row = pl.multiple_of(i * step, step)
            total = None
            for block, start in enumerate(starts):
                summed = sums[pl.ds(start + row, step)]
                product = change(which, (layer, pl.ds(row, step), half_lanes(block)), summed)
                total = product if total is None else total + product
            if norm is not None:
                products[layer, norm, pl.ds(row, step)] = total

        lax.fori_loop(0, rows // step, body, None)

    def sum_lanes(ones, value):
        rows = value.shape[0]
        parts = three_parts(value)
        sums_of = [dot_nt(ones, parts[i * rows : (i + 1) * rows])[:1] for i in range(3)]
        return sums_of[0] + (sums_of[1] + sums_of[2])

    cell_rows = []

    def blocks_at(start, rows, count):
        return [start + i * rows for i in range(count)]

    for index, (which, layer) in enumerate(units):
        for copy in coming(index):
            copy.wait()
        if which == expand:
            change_blocks(expand, layer, blocks_at(places.expand[layer], WIDTH, HIDDEN // LANES), WIDTH, 1)
        elif which == shrink:
            change_blocks(shrink, layer, blocks_at(places.shrink[layer], HIDDEN, 2), HIDDEN)
        elif which == output:
            change_blocks(output, layer, blocks_at(places.output[layer], WIDTH, 2), WIDTH)
        elif which == triple:
            starts = [at for start in places.triple[layer] for at in blocks_at(start, WIDTH, 2)]
            change_blocks(triple, layer, starts, WIDTH, 0)
        else:
            for each in range(LAYERS):
                at = places.early[each]
                if which == recurrent:
                    rows = []
                    for block in range(3):
                        lanes = slice(block * LANES, min((block + 1) * LANES, WIDTH + LATENT))
                        summed = sums[pl.ds(at + block * LATENT, LATENT)][:, : lanes.stop - lanes.start]
                        product = change(which, (each, slice(0, LATENT), lanes), summed)
                        rows.append(jnp.sum(product, axis=0, keepdims=True))
                    cell_rows.append(jnp.concatenate(rows[:2], axis=1))
                elif which == readout:
                    for block in range(2):
                        rows = sums[pl.ds(at + 96 + block * LATENT, LATENT)]
                        change(which, (each, slice(0, LATENT), half_lanes(block)), rows)
                elif which == table:
                    rows = sums[pl.ds(places.table[each], TABLE_ROWS)].astype(F32)
                    change(which, (each, slice(0, HEADS), slice(0, LANES)), rows[:8])
                    change(which, (each, slice(0, HEADS), slice(LANES, PAIRS)), rows[8:16, : PAIRS - LANES])
                else:
                    ones = jnp.ones((8, LANES), BF16)
                    for norm in range(3):
                        gain_row = held[3 * gains][norm, each : each + 1, :]
                        if norm == 2:
                            total = cell_rows[each]
                        else:
                            total = sum_lanes(ones, products[each, norm])
                        change(which, (norm, slice(each, each + 1)), total / (gain_row * scale))
        for copy in going(index):
            copy.start()
        if index == 1:
            for copy in passing_in:
                copy.wait()
            for copy in passing_out:
                copy.start()
        if index == 3:
            for copy in passing_out:
                copy.wait()
    for index in range(len(units)):
        for copy in going(index):
            copy.wait()


def update_step(sums, result, input_grad, held, parameters, scale, places):
    hbm = pl.BlockSpec(memory_space=pltpu.HBM)
    vmem = pl.BlockSpec(memory_space=pltpu.VMEM)
    in_vmem = lambda a: pltpu.with_memory_space_constraint(a, pltpu.VMEM)
    held = list(held)
    given, specs = [], []
    for i, a in enumerate(parameters):
        if i < 12 and (places.ahead or i % 3 == 0):
            given.append(in_vmem(held.pop(0)))
            specs.append(vmem)
        else:
            given.append(in_hbm(a))
            specs.append(hbm)
    like = lambda a: pltpu.HBM(a.shape, a.dtype)
    return pl.pallas_call(
        functools.partial(update_kernel, scale, places),
        out_shape=(like(result), like(input_grad)) + tuple(like(a) for a in parameters),
        in_specs=[vmem, hbm, hbm] + specs,
        out_specs=(hbm,) * (2 + len(parameters)),
        scratch_shapes=[pltpu.VMEM(a.shape, F32) for a in parameters]
        + [
            pltpu.VMEM(result.shape, result.dtype),
            pltpu.VMEM((LAYERS, 2, WIDTH, LANES), F32),
            pltpu.SemaphoreType.DMA((4,)),
            pltpu.SemaphoreType.DMA((12, 3)),
            pltpu.SemaphoreType.DMA((12, 3)),
        ],
        compiler_params=pltpu.CompilerParams(vmem_limit_bytes=20 * 2**20),
        name="nesterov_step",
    )(in_vmem(sums), in_hbm(result), in_hbm(input_grad), *given)


def per_device(frames, latent_init, crop_band, cotangent, *parameters):
    shape = frames.shape
    lon_count, batch_count = lax.axis_size("lon"), lax.axis_size("batch")
    places = Places(lon_count, batch_count)
    turned = {4: (0, 2, 1), 6: (1, 0, 2)}
    parameters = [
        a.transpose(turned[i // 3]) if i // 3 in turned else a for i, a in enumerate(parameters)
    ]
    result, input_grad, sums, held = layers_step(
        frames, latent_init, crop_band, cotangent, parameters, places
    )
    tokens = shape[0] * shape[1] * shape[2] * lon_count * batch_count
    result, input_grad, *updated = update_step(
        sums, result, input_grad, held, parameters, float(tokens) ** (-0.5), places
    )
    updated = [a.transpose(turned[i // 3]) if i // 3 in turned else a for i, a in enumerate(updated)]
    return (result.reshape(shape), input_grad.reshape(shape), *updated)


def solution(mesh):
    split = P("batch", None, "lon", None)
    return jax.shard_map(
        per_device,
        mesh=mesh,
        in_specs=(split, split, P("batch", None), split) + (P(),) * 24,
        out_specs=(split, split) + (P(),) * 24,
        check_vma=False,
    )
```

```python
import functools
import math

import jax
import jax.numpy as jnp
from jax import lax
from jax.experimental import pallas as pl
from jax.experimental.pallas import tpu as pltpu
from jax.sharding import PartitionSpec as P

WINDOW = 8
HALF = WINDOW // 2
SPAN = WINDOW * WINDOW
HEADS = 8
LANES = 128
LAYERS = 2
WIDTH = 256
HIDDEN = 1024
LATENT = 32
OFFSETS = 2 * WINDOW - 1
PAIRS = OFFSETS * OFFSETS

LEARN_RATE = 0.2
MOMENTUM_RATE = 0.9
AVERAGE_DECAY = 0.5
NORM_EPS = 1e-05
MASK_FILL = -100.0
HEAD_WIDTH = WIDTH // HEADS
HEADS_A_HALF = LANES // HEAD_WIDTH
SCALE = HEAD_WIDTH ** (-0.5)
GELU_C = 0.7978845608028654
GELU_A = 0.044715

F32 = jnp.float32
BF16 = jnp.bfloat16
MESH = pl.DeviceIdType.MESH

SMALL_ROWS = 256
FEED_ROWS = HIDDEN * WIDTH // LANES
OUTPUT_ROWS = WIDTH * WIDTH // LANES
TRIPLE_ROWS = 3 * OUTPUT_ROWS
SHRINK_ONE, EXPAND_ONE, ATTEND_ONE, SHRINK_ZERO, SHRINK_MORE, EXPAND_ZERO, EXPAND_MORE, OUTPUT_ZERO, TRIPLE_ZERO = range(9)
SECTION_ROWS = (
    FEED_ROWS,
    FEED_ROWS,
    OUTPUT_ROWS + TRIPLE_ROWS,
    FEED_ROWS // 2,
    FEED_ROWS // 2,
    FEED_ROWS // 2,
    FEED_ROWS // 2,
    2 * OUTPUT_ROWS + LAYERS * SMALL_ROWS,
    2 * OUTPUT_ROWS,
)
ROW_TILE = 16
EARLY_ROWS = 5 * LATENT
TABLE_ROWS = 16


SECTION_PHASES = (
    ("core", "lon", "line"),
    ("core", "line", "x", "y"),
    ("core", "lon", "line sum"),
    ("core", "lon", "line"),
    ("core", "lon", "line"),
    ("core", "lon", "line"),
    ("core", "lon", "line sum"),
    ("core", "lon", "line"),
    ("core", "lon", "line sum"),
)


class Places:
    def __init__(self, lon_count, batch_count):
        self.lon_count, self.line_count = lon_count, batch_count // 2
        self.ahead = lon_count * batch_count <= 32
        self.grant = (171 if self.ahead else 192) * 2**18
        unit = ROW_TILE * lon_count * batch_count
        few = self.few = unit <= 512
        self.few_members = lon_count * self.line_count if few else 1
        groups = [[i] for i in range(9)] if few else [[0, 1], [2], [3, 4, 5, 6], [7, 8]]
        self.leader = [group[-1] for group in groups for _ in group]
        self.first = [group[0] for group in groups for _ in group]
        self.rows, starts, at = {}, {}, 0
        for group in groups:
            begin = at
            for i in group:
                starts[i] = at
                at += SECTION_ROWS[i]
            rows = -(-(at - begin) // unit) * unit
            self.rows[group[-1]] = rows
            at = begin + rows
        self.total = at
        self.starts = starts
        self.phases, self.back, self.inbox, self.sems = {}, {}, {}, {}
        self.most_sems = 0
        bits = [1 << i for i in range(lon_count.bit_length() - 1)]
        inbox = 0
        for section, rows in self.rows.items():
            phases = []
            names = SECTION_PHASES[section]
            for name in names:
                if name == "x":
                    phases += [("bit", bit, 2) for bit in bits[:1]]
                elif name == "y":
                    phases += [("bit", bit, 2) for bit in bits[1:]]
                elif name == "both" and few:
                    phases.append((name, 0, lon_count * self.line_count))
                elif name == "both":
                    phases += [("lon", 0, lon_count), ("line", 0, self.line_count)]
                elif name == "line sum":
                    phases.append(("gather", 0, self.line_count))
                elif name != "at once":
                    phases.append((name, 0, {"core": 2, "lon": lon_count, "line": batch_count // 2}[name]))
            self.phases[section] = phases
            back = [phase + (depth,) for depth, phase in enumerate(phases, 1) if phase[0] != "gather"][::-1]
            if few and "at once" in names:
                back = [("both", 0, lon_count * self.line_count, len(phases)), back[-1]]
            self.back[section] = back
            self.inbox[section], self.sems[section], sem = [], [], 0
            for kind, _, members in phases:
                self.inbox[section].append(inbox)
                self.sems[section].append(sem)
                if kind == "gather":
                    inbox += rows * members
                else:
                    rows //= members
                    inbox += rows * (members - 1)
                sem += members - 1
            for _, _, members, _ in back:
                self.sems[section].append(sem)
                sem += members - 1
            self.most_sems = max(self.most_sems, sem)
        self.inbox_rows = inbox
        self.shrink = (starts[SHRINK_ZERO], starts[SHRINK_ONE])
        self.expand = (starts[EXPAND_ZERO], starts[EXPAND_ONE])
        self.output = (starts[OUTPUT_ZERO], starts[ATTEND_ONE])
        self.triple = (
            (starts[TRIPLE_ZERO], starts[TRIPLE_ZERO] + OUTPUT_ROWS, starts[OUTPUT_ZERO] + OUTPUT_ROWS),
            tuple(starts[ATTEND_ONE] + i * OUTPUT_ROWS for i in (1, 2, 3)),
        )
        small = starts[OUTPUT_ZERO] + 2 * OUTPUT_ROWS
        self.early = (small, small + SMALL_ROWS)
        table = self.total if few else starts[TRIPLE_ZERO] + SECTION_ROWS[TRIPLE_ZERO]
        self.table = (table, small + SMALL_ROWS + EARLY_ROWS)
        self.sum_rows = self.total + (TABLE_ROWS if few else 0)
        self.spare = {}
        for section, rows in self.rows.items():
            begin = starts[self.first[section]]
            used = starts[section] + SECTION_ROWS[section]
            if section == TRIPLE_ZERO and not few:
                used += TABLE_ROWS
            self.spare[section] = (used, begin + rows)


def dot(a, b):
    return jnp.dot(a, b, preferred_element_type=F32)


def dot_nt(a, b):
    return lax.dot_general(a, b, (((1,), (1,)), ((), ())), preferred_element_type=F32)


def dot_tn(a, b):
    return lax.dot_general(a, b, (((0,), (0,)), ((), ())), preferred_element_type=F32)


def norm_parts(stream):
    center = stream - jnp.mean(stream, axis=-1, keepdims=True)
    inverse = lax.rsqrt(jnp.mean(center * center, axis=-1, keepdims=True) + NORM_EPS)
    return center * inverse, inverse


def norm_back(upstream, gain_row, scaled, inverse):
    weighted = upstream * gain_row
    along = jnp.mean(weighted * scaled, axis=-1, keepdims=True)
    return inverse * (weighted - jnp.mean(weighted, axis=-1, keepdims=True) - scaled * along)


def lower_slots(shape):
    return lax.broadcasted_iota(jnp.int32, shape, 1) < HALF


def pack_half(own):
    tokens, features = own.shape
    rows = own.reshape(tokens // WINDOW, WINDOW, features)
    count = tokens // WINDOW // 2
    moved = pltpu.roll(rows[count:], HALF, axis=1)
    return jnp.where(lower_slots(moved.shape), rows[:count], moved).reshape(tokens // 2, features)


def unpack_half(packed, own):
    tokens, features = own.shape
    pairs = packed.reshape(tokens // WINDOW // 2, WINDOW, features)
    full = jnp.concatenate([pairs, pltpu.roll(pairs, HALF, axis=1)], axis=0)
    rows = own.reshape(tokens // WINDOW, WINDOW, features)
    return jnp.where(lower_slots(full.shape), full, rows).reshape(tokens, features)


def rows_ahead(value):
    cut = HALF * WINDOW
    return jnp.concatenate([value[cut:], value[:cut]], axis=0)


def rows_behind(value):
    cut = value.shape[0] - HALF * WINDOW
    return jnp.concatenate([value[cut:], value[:cut]], axis=0)


def head_of_lane(shape):
    return lax.broadcasted_iota(jnp.int32, shape, 1) // HEAD_WIDTH


def spread_heads(block):
    lane_head = head_of_lane(block.shape)
    zero = jnp.zeros_like(block)
    return jnp.concatenate(
        [jnp.where(lane_head == head, block, zero) for head in range(HEADS_A_HALF)], axis=0
    )


def gather_heads(stacked):
    count = stacked.shape[0] // HEADS_A_HALF
    lane_head = head_of_lane((count, LANES))
    out = stacked[:count]
    for head in range(1, HEADS_A_HALF):
        out = jnp.where(lane_head == head, stacked[head * count : (head + 1) * count], out)
    return out


def half_lanes(half):
    return slice(half * LANES, (half + 1) * LANES)


def half_scores(half):
    return slice(half * HEADS_A_HALF * SPAN, (half + 1) * HEADS_A_HALF * SPAN)


def score_mask(crop_start, crop_end, shifted, window, row_count):
    shape = (SPAN, HEADS_A_HALF * SPAN)
    key_row = lax.broadcasted_iota(jnp.int32, shape, 0) // WINDOW
    source = key_row + window * WINDOW
    if shifted:
        source = source + HALF
        if window == row_count // WINDOW - 1:
            source = jnp.where(source >= row_count, source - row_count, source)
    allowed = (source >= crop_start) & (source < crop_end)
    if shifted and window == row_count // WINDOW - 1:
        query_row = lax.broadcasted_iota(jnp.int32, shape, 1) % SPAN // WINDOW
        allowed = allowed & ((key_row < HALF) == (query_row < HALF))
    return jnp.where(allowed, 0.0, MASK_FILL).astype(F32)


def offset_onehot(shifted):
    shape = (WINDOW * LANES, WIDTH)
    row = lax.broadcasted_iota(jnp.int32, shape, 0)
    key_col = row // LANES
    row_offset = row % LANES // WINDOW
    query_col = row % WINDOW
    if shifted:
        key_col = (key_col + HALF) % WINDOW
        query_col = (query_col + HALF) % WINDOW
    target = row_offset * OFFSETS + query_col - key_col + WINDOW - 1
    target = jnp.where(row_offset < OFFSETS, target, -1)
    pair = lax.broadcasted_iota(jnp.int32, shape, 1)
    return jnp.where(pair == target, 1.0, 0.0).astype(BF16)


def three_parts(value):
    high = value.astype(BF16)
    rest = value - high.astype(F32)
    middle = rest.astype(BF16)
    low = (rest - middle.astype(F32)).astype(BF16)
    return jnp.concatenate([high.astype(F32), middle.astype(F32), low.astype(F32)], axis=0).astype(BF16)


def swap_groups(tiles):
    return [jnp.concatenate([tile[b : b + 1] for tile in tiles], axis=0) for b in range(8)]


def bias_of_table(table, onehot):
    spread = dot_nt(three_parts(table), onehot)
    spread = spread[:HEADS] + (spread[HEADS : 2 * HEADS] + spread[2 * HEADS :])
    tiles = swap_groups([spread[:, col * LANES : (col + 1) * LANES] for col in range(WINDOW)])
    lane = lax.broadcasted_iota(jnp.int32, (WINDOW, LANES), 1)
    blocks = []
    for key_row in range(WINDOW):
        back = (WINDOW - 1 - key_row) * WINDOW
        pieces = []
        for pair in range(HEADS // 2):
            even = pltpu.roll(tiles[2 * pair], (LANES - back) % LANES, axis=1)
            odd = pltpu.roll(tiles[2 * pair + 1], (LANES + SPAN - back) % LANES, axis=1)
            pieces.append(jnp.where(lane < SPAN, even, odd))
        blocks.append(jnp.concatenate(pieces, axis=1))
    return jnp.concatenate(blocks, axis=0)


def table_of_bias(gathered, onehot):
    lane = lax.broadcasted_iota(jnp.int32, (WINDOW, LANES), 1)
    zero = jnp.zeros((WINDOW, LANES), F32)
    tiles = []
    for head in range(HEADS):
        total = None
        for key_row in range(WINDOW):
            forth = (WINDOW - 1 - key_row) * WINDOW
            block = gathered[key_row * WINDOW : (key_row + 1) * WINDOW, half_lanes(head // 2)]
            if head % 2 == 0:
                moved = pltpu.roll(jnp.where(lane < SPAN, block, zero), forth, axis=1)
            else:
                moved = pltpu.roll(jnp.where(lane < SPAN, zero, block), (forth + SPAN) % LANES, axis=1)
            total = moved if total is None else total + moved
        tiles.append(total)
    spread = jnp.concatenate(swap_groups(tiles), axis=1)
    parts = dot(three_parts(spread), onehot)
    return parts[:HEADS] + (parts[HEADS : 2 * HEADS] + parts[2 * HEADS :])


def attend_forward(qkv, bias_ref, layer, crop, probs_ref, frame, row_count):
    shifted = layer % 2 == 1
    units = [(window, half) for window in range(row_count // WINDOW) for half in range(2)]
    piece = lambda which, window, half: qkv[
        window * SPAN : (window + 1) * SPAN, which * WIDTH + half * LANES : which * WIDTH + (half + 1) * LANES
    ]
    masks = [
        score_mask(crop[0], crop[1], shifted, window, row_count) for window in range(row_count // WINDOW)
    ]
    scores = [dot_nt(piece(1, *unit), spread_heads(piece(0, *unit))) for unit in units]
    probs = []
    for (window, half), score in zip(units, scores):
        score = score * SCALE + bias_ref[layer, :, half_scores(half)] + masks[window]
        exponent = jnp.exp(score - jnp.max(score, axis=0, keepdims=True))
        low = (exponent * (1.0 / jnp.sum(exponent, axis=0, keepdims=True))).astype(BF16)
        at = (frame * (row_count // WINDOW) + window) * SPAN
        probs_ref[layer, pl.ds(pl.multiple_of(at, SPAN), SPAN), half_scores(half)] = low
        probs.append(low)
    outs = [gather_heads(dot_tn(low, piece(2, *unit))) for unit, low in zip(units, probs)]
    return jnp.concatenate(
        [jnp.concatenate(outs[i : i + 2], axis=1) for i in range(0, len(outs), 2)], axis=0
    )


def value_grads(dcontext, layer, probs_ref, frame, row_count):
    windows = []
    for window in range(row_count // WINDOW):
        rows = slice(window * SPAN, (window + 1) * SPAN)
        at = (frame * (row_count // WINDOW) + window) * SPAN
        halves = []
        for half in range(2):
            low = probs_ref[layer, pl.ds(pl.multiple_of(at, SPAN), SPAN), half_scores(half)]
            halves.append(dot(low, spread_heads(dcontext[rows, half_lanes(half)])))
        windows.append(jnp.concatenate(halves, axis=1))
    return jnp.concatenate(windows, axis=0).astype(BF16)


def attend_backward(qkv, dcontext, layer, probs_ref, frame, gathered_ref, row_count):
    units = [(window, half) for window in range(row_count // WINDOW) for half in range(2)]
    piece = lambda which, window, half: qkv[
        window * SPAN : (window + 1) * SPAN, which * WIDTH + half * LANES : which * WIDTH + (half + 1) * LANES
    ]
    dprobs = [
        dot_nt(
            piece(2, window, half),
            spread_heads(dcontext[window * SPAN : (window + 1) * SPAN, half_lanes(half)]),
        )
        for window, half in units
    ]
    lows = []
    gathered = [None, None]
    for (window, half), dprob in zip(units, dprobs):
        at = (frame * (row_count // WINDOW) + window) * SPAN
        probs = probs_ref[layer, pl.ds(pl.multiple_of(at, SPAN), SPAN), half_scores(half)].astype(F32)
        dscores = probs * (dprob - jnp.sum(probs * dprob, axis=0, keepdims=True))
        gathered_ref[layer, :, half_scores(half)] += dscores
        lows.append(dscores.astype(BF16))
    dks = [dot(low, spread_heads(piece(0, *unit))) * SCALE for unit, low in zip(units, lows)]
    dqs = [gather_heads(dot_tn(low, piece(1, *unit))) * SCALE for unit, low in zip(units, lows)]
    return [
        jnp.concatenate(
            [jnp.concatenate(d[i : i + 2], axis=1) for i in range(0, len(d), 2)], axis=0
        ).astype(BF16)
        for d in (dqs, dks)
    ]


STEPS = {
    "second_middle_back": (),
    "before_second_back": (),
    "second_back": ((0, SHRINK_ONE), (0, EXPAND_ONE)),
    "before_first_feed_back": (),
    "first_feed_back": ((1, ATTEND_ONE), (1, SHRINK_ONE), (2, EXPAND_ONE)),
    "after_shrink": (),
    "first_middle_back": (
        (0, SHRINK_ZERO), (0, SHRINK_MORE), (0, SHRINK_ONE), (0, EXPAND_ZERO), (0, EXPAND_MORE),
        (0, ATTEND_ONE), (0, EXPAND_ONE),
    ),
    "after_output": (),
    "first_back": ((2, OUTPUT_ZERO), (2, SHRINK_ZERO), (3, SHRINK_ONE)),
    "first_back_more": (),
    "last_back": ((0, SHRINK_MORE), (1, EXPAND_ZERO), (1, TRIPLE_ZERO), (3, EXPAND_ONE), (3, EXPAND_MORE)),
    "last": (
        ATTEND_ONE, OUTPUT_ZERO, SHRINK_ZERO, SHRINK_MORE, EXPAND_ZERO, SHRINK_ONE, EXPAND_ONE, SHRINK_ONE,
        TRIPLE_ZERO, EXPAND_MORE, OUTPUT_ZERO, SHRINK_ZERO, SHRINK_MORE, EXPAND_ONE, ATTEND_ONE, EXPAND_ZERO,
        ATTEND_ONE, EXPAND_MORE, EXPAND_MORE, TRIPLE_ZERO, SHRINK_ZERO, OUTPUT_ZERO, SHRINK_ZERO,
        SHRINK_MORE, SHRINK_MORE, EXPAND_ZERO, EXPAND_ZERO, TRIPLE_ZERO, TRIPLE_ZERO, OUTPUT_ZERO,
        EXPAND_ONE, OUTPUT_ZERO, EXPAND_ONE,
    ),
}


def kernel(
    places,
    crop_ref,
    gains_ref,
    table_ref,
    frames_hbm,
    latent_hbm,
    cotangent_hbm,
    *refs,
):
    wide_hbm = refs[:12]
    recurrent_hbm, readout_hbm, act_out_hbm, input_grad_hbm, sums_ref = refs[12:17]
    held = refs[17 : 17 + (12 if places.ahead else 4)]
    (
        frames_ref,
        latent_ref,
        input_grad_ref,
        recurrent_wide,
        readout_wide,
        triple_low,
        output_low,
        expand_low,
        shrink_low,
        recurrent_low,
        readout_low,
        table_pad,
        bias_ref,
        gathered_ref,
        stream_in,
        stream_one,
        stream_two,
        normed_ref,
        qkv_ref,
        probs_ref,
        context_ref,
        cell_ref,
        bend_ref,
        state_ref,
        hidden_ref,
        active_ref,
        slope_ref,
        g_ref,
        gm_ref,
        gl_ref,
        gc_ref,
        gpre_ref,
        gstate_ref,
        dpacked_ref,
        out_halo,
        in_halo,
        grads_ref,
        sum_in,
        table_own,
        table_in,
        send_sem,
        recv_sem,
        sum_send_sem,
        sum_recv_sem,
        table_send_sem,
        table_recv_sem,
        weight_sem,
        token_sem,
        result_sem,
    ) = refs[17 + len(held) :]
    lon_count, line_count = places.lon_count, places.line_count
    frame_count = crop_ref.shape[1]
    tokens = frames_ref.shape[0] // frame_count
    row_count = tokens // WINDOW
    me_lon = lax.axis_index("lon")
    ahead = lax.rem(me_lon + 1, lon_count)
    behind = lax.rem(me_lon + lon_count - 1, lon_count)

    me_batch = lax.axis_index("batch")
    core, line = lax.rem(me_batch, 2), lax.div(me_batch, 2)
    lon_peers = [lax.rem(me_lon + by, lon_count) for by in range(1, lon_count)]
    line_peers = [lax.rem(line + by, line_count) for by in range(1, line_count)]
    neighbours = [{"batch": 2 * line + 1 - core}]
    if places.few:
        for i in range(1, lon_count * line_count):
            at = lax.rem(line + i % line_count, line_count)
            lon = lax.rem(me_lon + i // line_count, lon_count)
            neighbours.append({"lon": lon, "batch": 2 * at + core})
    else:
        neighbours += [{"lon": peer} for peer in lon_peers]
        neighbours += [{"batch": 2 * peer + core} for peer in line_peers]

    barrier = pltpu.get_barrier_semaphore()
    for peer in neighbours:
        pl.semaphore_signal(barrier, inc=1, device_id=peer, device_id_type=MESH)

    def row_span(start, rows):
        return pl.ds(pl.multiple_of(start, ROW_TILE), rows)

    def members_of(kind, bit):
        if kind == "core":
            return core, [(1 - core, neighbours[0])]
        if kind == "lon":
            return me_lon, [(peer, {"lon": peer}) for peer in lon_peers]
        if kind == "both":
            others = []
            for i in range(1, lon_count * line_count):
                lon = lax.rem(me_lon + i // line_count, lon_count)
                at = lax.rem(line + i % line_count, line_count)
                others.append((lon * line_count + at, {"lon": lon, "batch": 2 * at + core}))
            return me_lon * line_count + line, others
        if kind in ("line", "gather"):
            return line, [(peer, {"batch": 2 * peer + core}) for peer in line_peers]
        mine = lax.rem(lax.div(me_lon, bit), 2)
        return mine, [(1 - mine, {"lon": me_lon + bit - 2 * bit * mine})]

    def sum_range(section, depth):
        start, rows = places.starts[places.first[section]], places.rows[section]
        for kind, bit, members in places.phases[section][:depth]:
            if kind != "gather":
                rows //= members
                start = start + members_of(kind, bit)[0] * rows
        return start, rows

    def sum_copies(section, phase):
        depth = len(places.phases[section])
        back = phase >= depth
        if back:
            kind, bit, members, depth = places.back[section][phase - depth]
        else:
            kind, bit, members = places.phases[section][phase]
            depth = phase
        start, rows = sum_range(section, depth)
        copies = []
        for i, (place, device) in enumerate(members_of(kind, bit)[1]):
            if back:
                src, dst = sums_ref.at[row_span(start, rows)], sums_ref.at[row_span(start, rows)]
            elif kind == "gather":
                own = row_span(places.inbox[section][phase] + line * rows, rows)
                src, dst = sum_in.at[own], sum_in.at[own]
            else:
                piece = rows // members
                src = grads_ref.at[row_span(start + place * piece, piece)]
                dst = sum_in.at[row_span(places.inbox[section][phase] + i * piece, piece)]
            sem = places.sems[section][phase] + i
            copies.append(
                pltpu.make_async_remote_copy(
                    src_ref=src,
                    dst_ref=dst,
                    send_sem=sum_send_sem.at[section, sem],
                    recv_sem=sum_recv_sem.at[section, sem],
                    device_id=device,
                    device_id_type=MESH,
                )
            )
        return copies

    def add_up(start, rows, source_at, count, target, own=True):
        step = math.gcd(rows, LANES)

        def body(i, unused):
            at = row_span(start + i * step, step)
            terms = [grads_ref[at]] if own else []
            terms += [sum_in[row_span(source_at + k * rows + i * step, step)] for k in range(count)]
            total = terms[0].astype(F32)
            for term in terms[1:]:
                total = total + term.astype(F32)
            target[at] = total.astype(BF16)

        lax.fori_loop(0, rows // step, body, None)

    begun = {}

    def sum_send(section, phase):
        depth = len(places.phases[section])
        if phase < depth and places.phases[section][phase][0] == "gather":
            start, rows = sum_range(section, phase)
            sum_in[row_span(places.inbox[section][phase] + line * rows, rows)] = grads_ref[row_span(start, rows)]
        for copy in sum_copies(section, phase):
            copy.start()

    def sum_start(section):
        if places.leader[section] == section:
            begun[section] = 0
            sum_send(section, 0)

    def sum_left(section):
        return len(places.phases[section]) + len(places.back[section]) - begun[section]

    def sum_step(section):
        if section not in begun or sum_left(section) == 0:
            return
        phase = begun[section]
        for copy in sum_copies(section, phase):
            copy.wait_recv()
        depth = len(places.phases[section])
        if phase < depth:
            start, rows = sum_range(section, phase + 1)
            target = grads_ref if phase < depth - 1 else sums_ref
            kind, _, members = places.phases[section][phase]
            whole = kind == "gather"
            add_up(start, rows, places.inbox[section][phase], members - (not whole), target, not whole)
        begun[section] = phase + 1
        if sum_left(section):
            sum_send(section, phase + 1)

    def sum_drain(section):
        for phase in range(len(places.phases[section]) + len(places.back[section])):
            for copy in sum_copies(section, phase):
                copy.wait_send()

    def halo(exchange, frame):
        return pltpu.make_async_remote_copy(
            src_ref=out_halo.at[exchange % 2, frame],
            dst_ref=in_halo.at[exchange % 2, frame],
            send_sem=send_sem.at[exchange, frame],
            recv_sem=recv_sem.at[exchange, frame],
            device_id={"lon": behind if exchange % 2 == 0 else ahead},
            device_id_type=MESH,
        )

    def send_halo(exchange, frame, value):
        if exchange >= 2:
            halo(exchange - 2, frame).wait_send()
        out_halo[exchange % 2, frame] = pack_half(value).astype(BF16)
        halo(exchange, frame).start()

    def take_halo(exchange, frame, own):
        halo(exchange, frame).wait_recv()
        return unpack_half(in_halo[exchange % 2, frame].astype(F32), own)

    tokens_in = [
        pltpu.make_async_copy(hbm, ref, token_sem.at[i])
        for i, (hbm, ref) in enumerate(
            ((frames_hbm, frames_ref), (latent_hbm, latent_ref), (cotangent_hbm, gm_ref))
        )
    ]

    def wide_in(which, kind, layer):
        at = 3 * which + kind if places.ahead else which
        return pltpu.make_async_copy(
            wide_hbm[3 * which + kind].at[layer], held[at].at[layer], weight_sem.at[3 * which + kind, layer]
        )

    small_in = [
        pltpu.make_async_copy(recurrent_hbm, recurrent_wide, token_sem.at[3]),
        pltpu.make_async_copy(readout_hbm, readout_wide, token_sem.at[4]),
    ]

    def weights_take(which, layer):
        wide_in(which, 0, layer).wait()
        low = (triple_low, output_low, expand_low, shrink_low)[which]
        wide = held[3 * which if places.ahead else which]
        step = 64

        def body(i, unused):
            at = pl.ds(pl.multiple_of(i * step, step), step)
            low[layer, at] = wide[layer, at].astype(BF16)

        lax.fori_loop(0, wide.shape[1] // step, body, None)

    tokens_in[0].start()
    wide_in(0, 0, 0).start()
    tokens_in[1].start()
    for copy in small_in:
        copy.start()
    for which in (1, 2, 3):
        wide_in(which, 0, 0).start()

    def make_bias(layer):
        table_pad[...] = jnp.zeros_like(table_pad)
        table_pad[:, :PAIRS] = table_ref[layer]
        gl_ref[...] = offset_onehot(layer % 2 == 1)
        bias_ref[layer] = bias_of_table(table_pad[...], gl_ref[...])

    make_bias(0)
    for copy in small_in:
        copy.wait()
    for layer in range(LAYERS):
        recurrent_low[layer] = recurrent_wide[layer].astype(BF16)
        readout_low[layer] = readout_wide[layer].astype(BF16)
    tokens_in[0].wait()
    tokens_in[1].wait()
    for which in range(4):
        weights_take(which, 0)
    for which in range(4):
        wide_in(which, 0, 1).start()
    tokens_in[2].start()
    gathered_ref[...] = jnp.zeros_like(gathered_ref)

    def span(frame):
        return pl.ds(pl.multiple_of(frame * tokens, tokens), tokens)

    def gain(layer, which):
        return gains_ref[which, layer : layer + 1, :]

    def attention_part(layer, frame, normed):
        at = span(frame)
        normed_ref[layer, at] = normed
        qkv = dot(normed, triple_low[layer]).astype(BF16)
        qkv_ref[layer, at] = qkv
        crop = (crop_ref[0, frame], crop_ref[1, frame])
        return attend_forward(qkv, bias_ref, layer, crop, probs_ref, frame, row_count)

    def middle(layer, at, stream, context, latent):
        context_ref[layer, at] = context
        one = stream + dot(context, output_low[layer])
        (stream_one, input_grad_ref)[layer][at] = one
        scaled, _ = norm_parts(one)
        cell = (scaled * gain(layer, 2)).astype(BF16)
        cell_ref[layer, at] = cell
        preact = dot_nt(cell, recurrent_low[layer, :, :WIDTH]) + dot_nt(latent, recurrent_low[layer, :, WIDTH:])
        tangent = jnp.tanh(preact)
        bend_ref[layer, at] = (1.0 - tangent * tangent).astype(BF16)
        state = tangent.astype(BF16)
        state_ref[layer, at] = state
        two = one + dot(state, readout_low[layer])
        (stream_two, g_ref)[layer][at] = two
        scaled, _ = norm_parts(two)
        hidden = (scaled * gain(layer, 1)).astype(BF16)
        hidden_ref[layer, at] = hidden
        for block in range(HIDDEN // WIDTH):
            cols = slice(block * WIDTH, (block + 1) * WIDTH)
            inner = dot(hidden, expand_low[layer, :, cols])
            square = inner * inner
            gate = 0.5 + 0.5 * jnp.tanh(inner * (GELU_C + (GELU_C * GELU_A) * square))
            active = inner * gate
            slope = gate + active * (1.0 - gate) * (2.0 * GELU_C + (6.0 * GELU_C * GELU_A) * square)
            active_ref[layer, at, cols] = active.astype(BF16)
            if layer == LAYERS - 1:
                slope = slope * slope_ref[layer, at, cols].astype(F32)
            slope_ref[layer, at, cols] = slope.astype(BF16)
        return two + dot(active_ref[layer, at], shrink_low[layer])

    def feed_back(layer, at, g):
        if layer < LAYERS - 1:
            gm_ref[at] = g.astype(BF16)
        gm = gm_ref[at]
        for block in range(HIDDEN // WIDTH):
            cols = slice(block * WIDTH, (block + 1) * WIDTH)
            dactive = dot_nt(gm, shrink_low[layer, cols])
            if layer < LAYERS - 1:
                dactive = dactive * slope_ref[layer, at, cols].astype(F32)
            slope_ref[layer, at, cols] = dactive.astype(BF16)

    def middle_back(layer, at, g, gstate):
        dhidden = dot_nt(slope_ref[layer, at], expand_low[layer])
        scaled, inverse = norm_parts((stream_two, g_ref)[layer][at])
        scaled_one, inverse_one = norm_parts((stream_one, input_grad_ref)[layer][at])
        g = g + norm_back(dhidden, gain(layer, 1), scaled, inverse)
        gl = g.astype(BF16)
        gl_ref[at] = gl
        dstate = dot_nt(gl, readout_low[layer])
        if gstate is not None:
            dstate = dstate + gstate.astype(F32)
        gpre = (dstate * bend_ref[layer, at].astype(F32)).astype(BF16)
        gpre_ref[at] = gpre
        if layer > 0:
            gstate_ref[at] = dot(gpre, recurrent_low[layer, :, WIDTH:]).astype(BF16)
        dcell = dot(gpre, recurrent_low[layer, :, :WIDTH])
        g = g + norm_back(dcell, gain(layer, 2), scaled_one, inverse_one)
        gc = g.astype(BF16)
        gc_ref[at] = gc
        g_ref[at] = g
        return dot_nt(gc, output_low[layer])

    def values_back(layer, frame, dcontext):
        dpacked_ref[span(frame), 2 * WIDTH :] = value_grads(dcontext, layer, probs_ref, frame, row_count)

    def attention_back(layer, frame, dcontext):
        at = span(frame)
        pieces = attend_backward(
            qkv_ref[layer, at], dcontext, layer, probs_ref, frame, gathered_ref, row_count
        )
        for which in range(2):
            dpacked_ref[at, which * WIDTH : (which + 1) * WIDTH] = pieces[which]

    def packed_back(layer, frame):
        return dot_nt(dpacked_ref[span(frame)], triple_low[layer])

    def stream_back(layer, frame, g, stream, dnormed):
        scaled, inverse = norm_parts(stream)
        return g + norm_back(dnormed, gain(layer, 0), scaled, inverse)

    def put_blocks(start, value):
        rows = value.shape[0]
        for block in range(value.shape[1] // LANES):
            grads_ref[start + block * rows : start + (block + 1) * rows] = value[
                :, half_lanes(block)
            ].astype(BF16)

    def put_rows(start, total_rows, row, value):
        rows = value.shape[0]
        for block in range(value.shape[1] // LANES):
            at = start + block * total_rows + row
            grads_ref[at : at + rows] = value[:, half_lanes(block)].astype(BF16)

    def shrink_grads(layer):
        for block in range(HIDDEN // WIDTH):
            cols = slice(block * WIDTH, (block + 1) * WIDTH)
            put_rows(
                places.shrink[layer], HIDDEN, block * WIDTH, dot_tn(active_ref[layer, :, cols], gm_ref[...])
            )

    def expand_grads(layer):
        for block in range(HIDDEN // WIDTH):
            cols = slice(block * WIDTH, (block + 1) * WIDTH)
            put_blocks(
                places.expand[layer] + 2 * block * WIDTH, dot_tn(hidden_ref[layer], slope_ref[layer, :, cols])
            )

    def small_grads(layer, latent):
        near = dot_tn(gpre_ref[...], cell_ref[layer])
        far = dot_tn(gpre_ref[...], latent)
        far = jnp.concatenate([far, jnp.zeros((LATENT, LANES - LATENT), F32)], axis=1)
        readout = dot_tn(state_ref[layer], gl_ref[...])
        return [near[:, :LANES], near[:, LANES:], far, readout[:, :LANES], readout[:, LANES:]]

    def table_pieces(layer):
        gl_ref[...] = offset_onehot(layer % 2 == 1)
        table = table_of_bias(gathered_ref[layer], gl_ref[...])
        return [table[:, :LANES], table[:, LANES:]]

    def put_pieces(start, pieces):
        used = sum(piece.shape[0] for piece in pieces)
        value = jnp.concatenate(pieces, axis=0).astype(BF16)
        grads_ref[start : start + used] = value
        return start + used

    def clear_spare(section):
        if section in places.spare:
            clear_rows(*places.spare[section])

    def clear_rows(start, stop):
        if stop > start:
            grads_ref[start:stop] = jnp.zeros((stop - start, LANES), BF16)

    def output_grads(layer):
        put_blocks(places.output[layer], dot_tn(context_ref[layer], gc_ref[...]))

    def triple_grads(layer, blocks):
        for block in blocks:
            cols = slice(block * WIDTH, (block + 1) * WIDTH)
            put_blocks(places.triple[layer][block], dot_tn(normed_ref[layer], dpacked_ref[:, cols]))

    def table_core():
        here = row_span(0, TABLE_ROWS)
        return pltpu.make_async_remote_copy(
            src_ref=table_own.at[here],
            dst_ref=table_in.at[row_span(members * TABLE_ROWS, TABLE_ROWS)],
            send_sem=table_send_sem.at[0],
            recv_sem=table_recv_sem.at[0],
            device_id=neighbours[0],
            device_id_type=MESH,
        )

    members = lon_count * line_count

    def table_copies():
        mine = row_span((me_lon * line_count + line) * TABLE_ROWS, TABLE_ROWS)
        return [
            pltpu.make_async_remote_copy(
                src_ref=table_in.at[mine],
                dst_ref=table_in.at[mine],
                send_sem=table_send_sem.at[1 + i],
                recv_sem=table_recv_sem.at[1 + i],
                device_id=device,
                device_id_type=MESH,
            )
            for i, (_, device) in enumerate(members_of("both", 0)[1])
        ]

    def table_start():
        table_own[...] = jnp.concatenate(table_pieces(0), axis=0).astype(BF16)
        table_core().start()

    def table_spread():
        table_core().wait_recv()
        other = table_in[members * TABLE_ROWS : (members + 1) * TABLE_ROWS].astype(F32)
        mine = row_span((me_lon * line_count + line) * TABLE_ROWS, TABLE_ROWS)
        table_in[mine] = (table_own[...].astype(F32) + other).astype(BF16)
        for copy in table_copies():
            copy.start()

    def table_take():
        for copy in table_copies():
            copy.wait_recv()
        total = table_in[:TABLE_ROWS].astype(F32)
        for i in range(1, members):
            total = total + table_in[i * TABLE_ROWS : (i + 1) * TABLE_ROWS].astype(F32)
        sums_ref[places.table[0] : places.table[0] + TABLE_ROWS] = total.astype(BF16)

    def loop(body, steps=(), count=frame_count):
        def whole(frame, unused):
            body(frame)
            for after in range(count):
                here = [section for when, section in steps if when == after]
                if here:

                    @pl.when(frame == after)
                    def _(here=here):
                        sum_steps(*here)

        lax.fori_loop(0, count, whole, None)

    def sum_steps(*sections):
        for section in sections:
            sum_step(section)

    paired = 2 - frame_count % 2
    pairs = frame_count // paired

    def pair_span(pair):
        return pl.ds(pl.multiple_of(pair * paired * tokens, paired * tokens), paired * tokens)

    def frames_of(pair):
        return [(pair * paired + i, slice(i * tokens, (i + 1) * tokens)) for i in range(paired)]

    def first_layer(pair):
        at = pair_span(pair)
        stream = frames_ref[at].astype(F32)
        scaled, _ = norm_parts(stream)
        normed = (scaled * gain(0, 0)).astype(BF16)
        context = jnp.concatenate(
            [attention_part(0, frame, normed[rows]).astype(BF16) for frame, rows in frames_of(pair)], axis=0
        )
        stream = middle(0, at, stream, context, latent_ref[at])
        stream_in[at] = stream
        scaled, _ = norm_parts(stream)
        normed = scaled * gain(1, 0)
        normed_ref[1, at] = normed.astype(BF16)

        @pl.when(pair == 0)
        def _():
            pl.semaphore_wait(barrier, len(neighbours))

        for frame, rows in frames_of(pair):
            send_halo(0, frame, normed[rows])

    loop(first_layer, count=pairs)
    make_bias(1)
    for which in range(4):
        weights_take(which, 1)
    tokens_in[2].wait()
    if places.ahead:
        for layer in (1, 0):
            for which in range(4):
                for kind in (1, 2):
                    wide_in(which, kind, layer).start()

    def second_attention(frame):
        at = span(frame)
        normed = take_halo(0, frame, normed_ref[1, at].astype(F32))
        context = attention_part(1, frame, rows_ahead(normed).astype(BF16))
        context = rows_behind(context)
        context_ref[1, at] = context.astype(BF16)
        send_halo(1, frame, context)

    loop(second_attention)

    def second_feed_back(pair):
        feed_back(1, pair_span(pair), None)

    loop(second_feed_back, count=pairs)

    def second_middle(pair):
        at = pair_span(pair)
        context = jnp.concatenate(
            [
                take_halo(1, frame, context_ref[1, span(frame)].astype(F32)).astype(BF16)
                for frame, _ in frames_of(pair)
            ],
            axis=0,
        )
        dpacked_ref[at, WIDTH : 2 * WIDTH] = middle(1, at, stream_in[at], context, state_ref[0, at]).astype(BF16)

    loop(second_middle, count=pairs)
    act_out = pltpu.make_async_copy(dpacked_ref.at[:, pl.ds(WIDTH, WIDTH)], act_out_hbm, result_sem.at[frame_count])
    act_out.start()

    def second_middle_back(pair):
        at = pair_span(pair)
        dcontext = middle_back(1, at, gm_ref[at].astype(F32), None)
        dpacked_ref[at, :WIDTH] = dcontext.astype(BF16)
        for frame, rows in frames_of(pair):
            send_halo(2, frame, dcontext[rows])

    loop(second_middle_back, STEPS["second_middle_back"], pairs)
    shrink_grads(1)
    sum_start(SHRINK_ONE)
    expand_grads(1)
    sum_start(EXPAND_ONE)
    output_grads(1)
    early_one = put_pieces(places.early[1], small_grads(1, state_ref[0]))
    sum_steps(*STEPS["before_second_back"])
    act_out.wait()

    def second_back(frame):
        at = span(frame)
        dcontext = take_halo(2, frame, dpacked_ref[at, :WIDTH].astype(F32))
        dcontext = rows_ahead(dcontext).astype(BF16)
        values_back(1, frame, dcontext)
        attention_back(1, frame, dcontext)
        dnormed = rows_behind(packed_back(1, frame))
        gc_ref[at] = dnormed.astype(BF16)
        send_halo(3, frame, dnormed)

    loop(second_back, STEPS["second_back"])
    triple_grads(1, (0, 1, 2))
    clear_spare(ATTEND_ONE)
    sum_start(ATTEND_ONE)
    clear_rows(put_pieces(early_one, table_pieces(1)), places.early[1] + SMALL_ROWS)
    sum_steps(*STEPS["before_first_feed_back"])

    def first_feed_back(frame):
        at = span(frame)
        dnormed = take_halo(3, frame, gc_ref[at].astype(F32))
        g = stream_back(1, frame, g_ref[at], stream_in[at], dnormed)
        g_ref[at] = g
        feed_back(0, at, g)

    loop(first_feed_back, STEPS["first_feed_back"])
    shrink_grads(0)
    sum_start(SHRINK_ZERO)
    sum_start(SHRINK_MORE)
    sum_steps(*STEPS["after_shrink"])
    expand_grads(0)
    sum_start(EXPAND_ZERO)
    sum_start(EXPAND_MORE)

    def first_middle_back(pair):
        at = pair_span(pair)
        dcontext = middle_back(0, at, g_ref[at], gstate_ref[at]).astype(BF16)
        dpacked_ref[at, :WIDTH] = dcontext
        for frame, rows in frames_of(pair):
            values_back(0, frame, dcontext[rows])

    loop(first_middle_back, STEPS["first_middle_back"], pairs)
    output_grads(0)
    triple_grads(0, (2,))
    clear_rows(put_pieces(places.early[0], small_grads(0, latent_ref[...])), places.early[1])
    clear_spare(OUTPUT_ZERO)
    sum_start(OUTPUT_ZERO)
    sum_steps(*STEPS["after_output"])

    def grad_out(frame):
        at = span(frame)
        return pltpu.make_async_copy(input_grad_ref.at[at], input_grad_hbm.at[at], result_sem.at[frame])

    def first_back(frame):
        attention_back(0, frame, dpacked_ref[span(frame), :WIDTH])

    loop(first_back, STEPS["first_back"])
    triple_grads(0, (0, 1))
    if not places.few:
        put_pieces(places.table[0], table_pieces(0))
        clear_spare(TRIPLE_ZERO)
    sum_start(TRIPLE_ZERO)
    if places.few:
        table_start()

    def last_back(frame):
        at = span(frame)
        stream = frames_ref[at].astype(F32)
        input_grad_ref[at] = stream_back(0, frame, g_ref[at], stream, packed_back(0, frame))
        grad_out(frame).start()

    loop(last_back, STEPS["last_back"])
    if places.few:
        table_spread()
    sum_steps(*STEPS["last"])
    while any(sum_left(section) for section in begun):
        sum_steps(*begun)
    if places.few:
        table_take()
        table_core().wait_send()
        for copy in table_copies():
            copy.wait_send()

    def drain(frame, unused):
        for exchange in (2, 3):
            halo(exchange, frame).wait_send()
        grad_out(frame).wait()

    lax.fori_loop(0, frame_count, drain, None)
    if places.ahead:
        for layer in (1, 0):
            for which in range(4):
                for kind in (1, 2):
                    wide_in(which, kind, layer).wait()
    for section in places.rows:
        sum_drain(section)


def flat_tokens(array):
    return array.reshape(-1, array.shape[-1])


def in_hbm(array):
    return pltpu.with_memory_space_constraint(array, pltpu.HBM)


def layers_step(frames, latent, crop_band, cotangent, parameters, places):
    frame_count, row_count, col_count, features = frames.shape
    count = frame_count * row_count * col_count
    tokens = row_count * col_count
    vmem = pl.BlockSpec(memory_space=pltpu.VMEM)
    hbm = pl.BlockSpec(memory_space=pltpu.HBM)
    both = lambda *shape: pltpu.VMEM((LAYERS,) + shape, BF16)
    one = lambda *shape: pltpu.VMEM(shape, BF16)
    wide = lambda *shape: pltpu.VMEM(shape, F32)
    scratch = [
        one(count, WIDTH),
        one(count, LATENT),
        wide(count, WIDTH),
        wide(LAYERS, LATENT, WIDTH + LATENT),
        wide(LAYERS, LATENT, WIDTH),
        both(WIDTH, 3 * WIDTH),
        both(WIDTH, WIDTH),
        both(WIDTH, HIDDEN),
        both(HIDDEN, WIDTH),
        both(LATENT, WIDTH + LATENT),
        both(LATENT, WIDTH),
        wide(HEADS, WIDTH),
        wide(LAYERS, SPAN, HEADS * SPAN),
        wide(LAYERS, SPAN, HEADS * SPAN),
        wide(count, WIDTH),
        wide(count, WIDTH),
        wide(count, WIDTH),
        both(count, WIDTH),
        both(count, 3 * WIDTH),
        both(count, HEADS * SPAN),
        both(count, WIDTH),
        both(count, WIDTH),
        both(count, LATENT),
        both(count, LATENT),
        both(count, WIDTH),
        both(count, HIDDEN),
        both(count, HIDDEN),
        wide(count, WIDTH),
        one(count, WIDTH),
        one(count, WIDTH),
        one(count, WIDTH),
        one(count, LATENT),
        one(count, LATENT),
        one(count, 3 * WIDTH),
        one(2, frame_count, tokens // 2, WIDTH),
        one(2, frame_count, tokens // 2, WIDTH),
        one(places.total, LANES),
        one(places.inbox_rows, LANES),
        one(TABLE_ROWS, LANES),
        one((places.few_members + 1) * TABLE_ROWS, LANES),
        pltpu.SemaphoreType.DMA((4, frame_count)),
        pltpu.SemaphoreType.DMA((4, frame_count)),
        pltpu.SemaphoreType.DMA((len(SECTION_ROWS), places.most_sems)),
        pltpu.SemaphoreType.DMA((len(SECTION_ROWS), places.most_sems)),
        pltpu.SemaphoreType.DMA((places.few_members,)),
        pltpu.SemaphoreType.DMA((places.few_members,)),
        pltpu.SemaphoreType.DMA((12, LAYERS)),
        pltpu.SemaphoreType.DMA((5,)),
        pltpu.SemaphoreType.DMA((frame_count + 1,)),
    ]
    wide_parameters = parameters[:12]
    recurrent, readout, gains, table = parameters[12::3]
    held = [a for i, a in enumerate(wide_parameters) if places.ahead or i % 3 == 0]
    given = (frames, latent, cotangent)
    outs = pl.pallas_call(
        functools.partial(kernel, places),
        out_shape=(
            pltpu.HBM((count, WIDTH), BF16),
            pltpu.HBM((count, WIDTH), F32),
            pltpu.VMEM((places.sum_rows, LANES), BF16),
        )
        + tuple(pltpu.VMEM(a.shape, F32) for a in held),
        in_specs=[pl.BlockSpec(memory_space=pltpu.SMEM), vmem, vmem] + [hbm] * 17,
        out_specs=(hbm, hbm, vmem) + (vmem,) * len(held),
        scratch_shapes=scratch,
        compiler_params=pltpu.CompilerParams(
            collective_id=0, has_side_effects=True, vmem_limit_bytes=places.grant
        ),
        name="swin_step",
    )(
        crop_band.T,
        gains,
        table,
        *(in_hbm(flat_tokens(a)) for a in given),
        *(in_hbm(a) for a in wide_parameters),
        in_hbm(recurrent),
        in_hbm(readout),
    )
    return outs[0], outs[1], outs[2], outs[3:]


def update_kernel(scale, places, sums, result_hbm, grad_hbm, *refs):
    count = 24
    given, result_out, grad_out = refs[:count], refs[count], refs[count + 1]
    made, held = refs[count + 2 : 2 * count + 2], refs[2 * count + 2 : 3 * count + 2]
    result_held, products, pass_sem, in_sem, out_sem = refs[3 * count + 2 :]
    triple, output, expand, shrink, recurrent, readout, gains, table = range(8)
    grad_held = held[3 * shrink].at[0]

    passing_in = [
        pltpu.make_async_copy(result_hbm, result_held, pass_sem.at[0]),
        pltpu.make_async_copy(grad_hbm, grad_held, pass_sem.at[1]),
    ]
    passing_out = [
        pltpu.make_async_copy(result_held, result_out, pass_sem.at[2]),
        pltpu.make_async_copy(grad_held, grad_out, pass_sem.at[3]),
    ]
    units = [
        (shrink, 1),
        (expand, 1),
        (triple, 1),
        (output, 1),
        (shrink, 0),
        (expand, 0),
        (output, 0),
        (triple, 0),
        (recurrent, None),
        (readout, None),
        (table, None),
        (gains, None),
    ]

    def part(ref, layer):
        return ref if layer is None else ref.at[layer]

    def is_held(which, kind):
        return which < recurrent and (places.ahead or kind == 0)

    def coming(index):
        which, layer = units[index]
        return [
            pltpu.make_async_copy(
                part(given[3 * which + i], layer), part(held[3 * which + i], layer), in_sem.at[index, i]
            )
            for i in range(3)
            if not is_held(which, i)
        ]

    def going(index):
        which, layer = units[index]
        return [
            pltpu.make_async_copy(
                part(held[3 * which + i], layer), part(made[3 * which + i], layer), out_sem.at[index, i]
            )
            for i in range(3)
        ]

    for index in range(len(units)):
        for copy in coming(index):
            copy.start()
    for copy in passing_in:
        copy.start()

    def change(which, at, summed):
        old = [(given if is_held(which, i) else held)[3 * which + i][at] for i in range(3)]
        weight, moment, average = held[3 * which : 3 * which + 3]
        gradient = summed.astype(F32) * scale
        velocity = MOMENTUM_RATE * old[1] + gradient
        updated = old[0] - LEARN_RATE * (gradient + MOMENTUM_RATE * velocity)
        average[at] = AVERAGE_DECAY * old[2] + (1.0 - AVERAGE_DECAY) * updated
        weight[at] = updated
        moment[at] = velocity
        return old[0].astype(BF16).astype(F32) * gradient

    def change_blocks(which, layer, starts, rows, norm=None):
        step = 256 // len(starts)
        step = 32 if step < 64 else min(step, 128)

        def body(i, unused):
            row = pl.multiple_of(i * step, step)
            total = None
            for block, start in enumerate(starts):
                summed = sums[pl.ds(start + row, step)]
                product = change(which, (layer, pl.ds(row, step), half_lanes(block)), summed)
                total = product if total is None else total + product
            if norm is not None:
                products[layer, norm, pl.ds(row, step)] = total

        lax.fori_loop(0, rows // step, body, None)

    def sum_lanes(ones, value):
        rows = value.shape[0]
        parts = three_parts(value)
        sums_of = [dot_nt(ones, parts[i * rows : (i + 1) * rows])[:1] for i in range(3)]
        return sums_of[0] + (sums_of[1] + sums_of[2])

    cell_rows = []

    def blocks_at(start, rows, count):
        return [start + i * rows for i in range(count)]

    for index, (which, layer) in enumerate(units):
        for copy in coming(index):
            copy.wait()
        if which == expand:
            change_blocks(expand, layer, blocks_at(places.expand[layer], WIDTH, HIDDEN // LANES), WIDTH, 1)
        elif which == shrink:
            change_blocks(shrink, layer, blocks_at(places.shrink[layer], HIDDEN, 2), HIDDEN)
        elif which == output:
            change_blocks(output, layer, blocks_at(places.output[layer], WIDTH, 2), WIDTH)
        elif which == triple:
            starts = [at for start in places.triple[layer] for at in blocks_at(start, WIDTH, 2)]
            change_blocks(triple, layer, starts, WIDTH, 0)
        else:
            for each in range(LAYERS):
                at = places.early[each]
                if which == recurrent:
                    rows = []
                    for block in range(3):
                        lanes = slice(block * LANES, min((block + 1) * LANES, WIDTH + LATENT))
                        summed = sums[pl.ds(at + block * LATENT, LATENT)][:, : lanes.stop - lanes.start]
                        product = change(which, (each, slice(0, LATENT), lanes), summed)
                        rows.append(jnp.sum(product, axis=0, keepdims=True))
                    cell_rows.append(jnp.concatenate(rows[:2], axis=1))
                elif which == readout:
                    for block in range(2):
                        rows = sums[pl.ds(at + 96 + block * LATENT, LATENT)]
                        change(which, (each, slice(0, LATENT), half_lanes(block)), rows)
                elif which == table:
                    rows = sums[pl.ds(places.table[each], TABLE_ROWS)].astype(F32)
                    change(which, (each, slice(0, HEADS), slice(0, LANES)), rows[:8])
                    change(which, (each, slice(0, HEADS), slice(LANES, PAIRS)), rows[8:16, : PAIRS - LANES])
                else:
                    ones = jnp.ones((8, LANES), BF16)
                    for norm in range(3):
                        gain_row = held[3 * gains][norm, each : each + 1, :]
                        if norm == 2:
                            total = cell_rows[each]
                        else:
                            total = sum_lanes(ones, products[each, norm])
                        change(which, (norm, slice(each, each + 1)), total / (gain_row * scale))
        for copy in going(index):
            copy.start()
        if index == 1:
            for copy in passing_in:
                copy.wait()
            for copy in passing_out:
                copy.start()
        if index == 3:
            for copy in passing_out:
                copy.wait()
    for index in range(len(units)):
        for copy in going(index):
            copy.wait()


def update_step(sums, result, input_grad, held, parameters, scale, places):
    hbm = pl.BlockSpec(memory_space=pltpu.HBM)
    vmem = pl.BlockSpec(memory_space=pltpu.VMEM)
    in_vmem = lambda a: pltpu.with_memory_space_constraint(a, pltpu.VMEM)
    held = list(held)
    given, specs = [], []
    for i, a in enumerate(parameters):
        if i < 12 and (places.ahead or i % 3 == 0):
            given.append(in_vmem(held.pop(0)))
            specs.append(vmem)
        else:
            given.append(in_hbm(a))
            specs.append(hbm)
    like = lambda a: pltpu.HBM(a.shape, a.dtype)
    return pl.pallas_call(
        functools.partial(update_kernel, scale, places),
        out_shape=(like(result), like(input_grad)) + tuple(like(a) for a in parameters),
        in_specs=[vmem, hbm, hbm] + specs,
        out_specs=(hbm,) * (2 + len(parameters)),
        scratch_shapes=[pltpu.VMEM(a.shape, F32) for a in parameters]
        + [
            pltpu.VMEM(result.shape, result.dtype),
            pltpu.VMEM((LAYERS, 2, WIDTH, LANES), F32),
            pltpu.SemaphoreType.DMA((4,)),
            pltpu.SemaphoreType.DMA((12, 3)),
            pltpu.SemaphoreType.DMA((12, 3)),
        ],
        compiler_params=pltpu.CompilerParams(vmem_limit_bytes=20 * 2**20),
        name="nesterov_step",
    )(in_vmem(sums), in_hbm(result), in_hbm(input_grad), *given)


def per_device(frames, latent_init, crop_band, cotangent, *parameters):
    shape = frames.shape
    lon_count, batch_count = lax.axis_size("lon"), lax.axis_size("batch")
    places = Places(lon_count, batch_count)
    turned = {4: (0, 2, 1), 6: (1, 0, 2)}
    parameters = [
        a.transpose(turned[i // 3]) if i // 3 in turned else a for i, a in enumerate(parameters)
    ]
    result, input_grad, sums, held = layers_step(
        frames, latent_init, crop_band, cotangent, parameters, places
    )
    tokens = shape[0] * shape[1] * shape[2] * lon_count * batch_count
    result, input_grad, *updated = update_step(
        sums, result, input_grad, held, parameters, float(tokens) ** (-0.5), places
    )
    updated = [a.transpose(turned[i // 3]) if i // 3 in turned else a for i, a in enumerate(updated)]
    return (result.reshape(shape), input_grad.reshape(shape), *updated)


def solution(mesh):
    split = P("batch", None, "lon", None)
    return jax.shard_map(
        per_device,
        mesh=mesh,
        in_specs=(split, split, P("batch", None), split) + (P(),) * 24,
        out_specs=(split, split) + (P(),) * 24,
        check_vma=False,
    )
```

```python
import functools
import math

import jax
import jax.numpy as jnp
from jax import lax
from jax.experimental import pallas as pl
from jax.experimental.pallas import tpu as pltpu
from jax.sharding import PartitionSpec as P

WINDOW = 8
HALF = WINDOW // 2
SPAN = WINDOW * WINDOW
HEADS = 8
LANES = 128
LAYERS = 2
WIDTH = 256
HIDDEN = 1024
LATENT = 32
OFFSETS = 2 * WINDOW - 1
PAIRS = OFFSETS * OFFSETS

LEARN_RATE = 0.2
MOMENTUM_RATE = 0.9
AVERAGE_DECAY = 0.5
NORM_EPS = 1e-05
MASK_FILL = -100.0
HEAD_WIDTH = WIDTH // HEADS
HEADS_A_HALF = LANES // HEAD_WIDTH
SCALE = HEAD_WIDTH ** (-0.5)
GELU_C = 0.7978845608028654
GELU_A = 0.044715

F32 = jnp.float32
BF16 = jnp.bfloat16
MESH = pl.DeviceIdType.MESH

SMALL_ROWS = 256
FEED_ROWS = HIDDEN * WIDTH // LANES
OUTPUT_ROWS = WIDTH * WIDTH // LANES
TRIPLE_ROWS = 3 * OUTPUT_ROWS
SHRINK_ONE, EXPAND_ONE, ATTEND_ONE, SHRINK_ZERO, SHRINK_MORE, EXPAND_ZERO, EXPAND_MORE, OUTPUT_ZERO, TRIPLE_ZERO = range(9)
SECTION_ROWS = (
    FEED_ROWS,
    FEED_ROWS,
    OUTPUT_ROWS + TRIPLE_ROWS,
    FEED_ROWS // 2,
    FEED_ROWS // 2,
    FEED_ROWS // 2,
    FEED_ROWS // 2,
    2 * OUTPUT_ROWS + LAYERS * SMALL_ROWS,
    2 * OUTPUT_ROWS,
)
ROW_TILE = 16
EARLY_ROWS = 5 * LATENT
TABLE_ROWS = 16


SECTION_PHASES = (
    ("core", "lon", "line"),
    ("core", "line", "x", "y"),
    ("core", "lon", "line sum"),
    ("core", "lon", "line"),
    ("core", "lon", "line"),
    ("core", "lon", "line"),
    ("core", "lon", "line sum"),
    ("core", "lon", "line"),
    ("core", "lon", "line sum"),
)


class Places:
    def __init__(self, lon_count, batch_count):
        self.lon_count, self.line_count = lon_count, batch_count // 2
        self.ahead = lon_count * batch_count <= 32
        self.grant = (171 if self.ahead else 192) * 2**18
        unit = ROW_TILE * lon_count * batch_count
        few = self.few = unit <= 512
        self.few_members = lon_count * self.line_count if few else 1
        groups = [[i] for i in range(9)] if few else [[0, 1], [2], [3, 4, 5, 6], [7, 8]]
        self.leader = [group[-1] for group in groups for _ in group]
        self.first = [group[0] for group in groups for _ in group]
        self.rows, starts, at = {}, {}, 0
        for group in groups:
            begin = at
            for i in group:
                starts[i] = at
                at += SECTION_ROWS[i]
            rows = -(-(at - begin) // unit) * unit
            self.rows[group[-1]] = rows
            at = begin + rows
        self.total = at
        self.starts = starts
        self.phases, self.back, self.inbox, self.sems = {}, {}, {}, {}
        self.most_sems = 0
        bits = [1 << i for i in range(lon_count.bit_length() - 1)]
        inbox = 0
        for section, rows in self.rows.items():
            phases = []
            names = SECTION_PHASES[section]
            for name in names:
                if name == "x":
                    phases += [("bit", bit, 2) for bit in bits[:1]]
                elif name == "y":
                    phases += [("bit", bit, 2) for bit in bits[1:]]
                elif name == "both" and few:
                    phases.append((name, 0, lon_count * self.line_count))
                elif name == "both":
                    phases += [("lon", 0, lon_count), ("line", 0, self.line_count)]
                elif name == "line sum":
                    phases.append(("gather", 0, self.line_count))
                elif name != "at once":
                    phases.append((name, 0, {"core": 2, "lon": lon_count, "line": batch_count // 2}[name]))
            self.phases[section] = phases
            back = [phase + (depth,) for depth, phase in enumerate(phases, 1) if phase[0] != "gather"][::-1]
            if few and "at once" in names:
                back = [("both", 0, lon_count * self.line_count, len(phases)), back[-1]]
            self.back[section] = back
            self.inbox[section], self.sems[section], sem = [], [], 0
            for kind, _, members in phases:
                self.inbox[section].append(inbox)
                self.sems[section].append(sem)
                if kind == "gather":
                    inbox += rows * members
                else:
                    rows //= members
                    inbox += rows * (members - 1)
                sem += members - 1
            for _, _, members, _ in back:
                self.sems[section].append(sem)
                sem += members - 1
            self.most_sems = max(self.most_sems, sem)
        self.inbox_rows = inbox
        self.shrink = (starts[SHRINK_ZERO], starts[SHRINK_ONE])
        self.expand = (starts[EXPAND_ZERO], starts[EXPAND_ONE])
        self.output = (starts[OUTPUT_ZERO], starts[ATTEND_ONE])
        self.triple = (
            (starts[TRIPLE_ZERO], starts[TRIPLE_ZERO] + OUTPUT_ROWS, starts[OUTPUT_ZERO] + OUTPUT_ROWS),
            tuple(starts[ATTEND_ONE] + i * OUTPUT_ROWS for i in (1, 2, 3)),
        )
        small = starts[OUTPUT_ZERO] + 2 * OUTPUT_ROWS
        self.early = (small, small + SMALL_ROWS)
        table = self.total if few else starts[TRIPLE_ZERO] + SECTION_ROWS[TRIPLE_ZERO]
        self.table = (table, small + SMALL_ROWS + EARLY_ROWS)
        self.sum_rows = self.total + (TABLE_ROWS if few else 0)
        self.spare = {}
        for section, rows in self.rows.items():
            begin = starts[self.first[section]]
            used = starts[section] + SECTION_ROWS[section]
            if section == TRIPLE_ZERO and not few:
                used += TABLE_ROWS
            self.spare[section] = (used, begin + rows)


def dot(a, b):
    return jnp.dot(a, b, preferred_element_type=F32)


def dot_nt(a, b):
    return lax.dot_general(a, b, (((1,), (1,)), ((), ())), preferred_element_type=F32)


def dot_tn(a, b):
    return lax.dot_general(a, b, (((0,), (0,)), ((), ())), preferred_element_type=F32)


def norm_parts(stream):
    center = stream - jnp.mean(stream, axis=-1, keepdims=True)
    inverse = lax.rsqrt(jnp.mean(center * center, axis=-1, keepdims=True) + NORM_EPS)
    return center * inverse, inverse


def norm_back(upstream, gain_row, scaled, inverse):
    weighted = upstream * gain_row
    along = jnp.mean(weighted * scaled, axis=-1, keepdims=True)
    return inverse * (weighted - jnp.mean(weighted, axis=-1, keepdims=True) - scaled * along)


def lower_slots(shape):
    return lax.broadcasted_iota(jnp.int32, shape, 1) < HALF


def pack_half(own):
    tokens, features = own.shape
    rows = own.reshape(tokens // WINDOW, WINDOW, features)
    count = tokens // WINDOW // 2
    moved = pltpu.roll(rows[count:], HALF, axis=1)
    return jnp.where(lower_slots(moved.shape), rows[:count], moved).reshape(tokens // 2, features)


def unpack_half(packed, own):
    tokens, features = own.shape
    pairs = packed.reshape(tokens // WINDOW // 2, WINDOW, features)
    full = jnp.concatenate([pairs, pltpu.roll(pairs, HALF, axis=1)], axis=0)
    rows = own.reshape(tokens // WINDOW, WINDOW, features)
    return jnp.where(lower_slots(full.shape), full, rows).reshape(tokens, features)


def rows_ahead(value):
    cut = HALF * WINDOW
    return jnp.concatenate([value[cut:], value[:cut]], axis=0)


def rows_behind(value):
    cut = value.shape[0] - HALF * WINDOW
    return jnp.concatenate([value[cut:], value[:cut]], axis=0)


def head_of_lane(shape):
    return lax.broadcasted_iota(jnp.int32, shape, 1) // HEAD_WIDTH


def spread_heads(block):
    lane_head = head_of_lane(block.shape)
    zero = jnp.zeros_like(block)
    return jnp.concatenate(
        [jnp.where(lane_head == head, block, zero) for head in range(HEADS_A_HALF)], axis=0
    )


def gather_heads(stacked):
    count = stacked.shape[0] // HEADS_A_HALF
    lane_head = head_of_lane((count, LANES))
    out = stacked[:count]
    for head in range(1, HEADS_A_HALF):
        out = jnp.where(lane_head == head, stacked[head * count : (head + 1) * count], out)
    return out


def half_lanes(half):
    return slice(half * LANES, (half + 1) * LANES)


def half_scores(half):
    return slice(half * HEADS_A_HALF * SPAN, (half + 1) * HEADS_A_HALF * SPAN)


def score_mask(crop_start, crop_end, shifted, window, row_count):
    shape = (SPAN, HEADS_A_HALF * SPAN)
    key_row = lax.broadcasted_iota(jnp.int32, shape, 0) // WINDOW
    source = key_row + window * WINDOW
    if shifted:
        source = source + HALF
        if window == row_count // WINDOW - 1:
            source = jnp.where(source >= row_count, source - row_count, source)
    allowed = (source >= crop_start) & (source < crop_end)
    if shifted and window == row_count // WINDOW - 1:
        query_row = lax.broadcasted_iota(jnp.int32, shape, 1) % SPAN // WINDOW
        allowed = allowed & ((key_row < HALF) == (query_row < HALF))
    return jnp.where(allowed, 0.0, MASK_FILL).astype(F32)


def offset_onehot(shifted):
    shape = (WINDOW * LANES, WIDTH)
    row = lax.broadcasted_iota(jnp.int32, shape, 0)
    key_col = row // LANES
    row_offset = row % LANES // WINDOW
    query_col = row % WINDOW
    if shifted:
        key_col = (key_col + HALF) % WINDOW
        query_col = (query_col + HALF) % WINDOW
    target = row_offset * OFFSETS + query_col - key_col + WINDOW - 1
    target = jnp.where(row_offset < OFFSETS, target, -1)
    pair = lax.broadcasted_iota(jnp.int32, shape, 1)
    return jnp.where(pair == target, 1.0, 0.0).astype(BF16)


def three_parts(value):
    high = value.astype(BF16)
    rest = value - high.astype(F32)
    middle = rest.astype(BF16)
    low = (rest - middle.astype(F32)).astype(BF16)
    return jnp.concatenate([high.astype(F32), middle.astype(F32), low.astype(F32)], axis=0).astype(BF16)


def swap_groups(tiles):
    return [jnp.concatenate([tile[b : b + 1] for tile in tiles], axis=0) for b in range(8)]


def bias_of_table(table, onehot):
    spread = dot_nt(three_parts(table), onehot)
    spread = spread[:HEADS] + (spread[HEADS : 2 * HEADS] + spread[2 * HEADS :])
    tiles = swap_groups([spread[:, col * LANES : (col + 1) * LANES] for col in range(WINDOW)])
    lane = lax.broadcasted_iota(jnp.int32, (WINDOW, LANES), 1)
    blocks = []
    for key_row in range(WINDOW):
        back = (WINDOW - 1 - key_row) * WINDOW
        pieces = []
        for pair in range(HEADS // 2):
            even = pltpu.roll(tiles[2 * pair], (LANES - back) % LANES, axis=1)
            odd = pltpu.roll(tiles[2 * pair + 1], (LANES + SPAN - back) % LANES, axis=1)
            pieces.append(jnp.where(lane < SPAN, even, odd))
        blocks.append(jnp.concatenate(pieces, axis=1))
    return jnp.concatenate(blocks, axis=0)


def table_of_bias(gathered, onehot):
    lane = lax.broadcasted_iota(jnp.int32, (WINDOW, LANES), 1)
    zero = jnp.zeros((WINDOW, LANES), F32)
    tiles = []
    for head in range(HEADS):
        total = None
        for key_row in range(WINDOW):
            forth = (WINDOW - 1 - key_row) * WINDOW
            block = gathered[key_row * WINDOW : (key_row + 1) * WINDOW, half_lanes(head // 2)]
            if head % 2 == 0:
                moved = pltpu.roll(jnp.where(lane < SPAN, block, zero), forth, axis=1)
            else:
                moved = pltpu.roll(jnp.where(lane < SPAN, zero, block), (forth + SPAN) % LANES, axis=1)
            total = moved if total is None else total + moved
        tiles.append(total)
    spread = jnp.concatenate(swap_groups(tiles), axis=1)
    parts = dot(three_parts(spread), onehot)
    return parts[:HEADS] + (parts[HEADS : 2 * HEADS] + parts[2 * HEADS :])


def attend_forward(qkv, bias_ref, layer, crop, probs_ref, frame, row_count):
    shifted = layer % 2 == 1
    units = [(window, half) for window in range(row_count // WINDOW) for half in range(2)]
    piece = lambda which, window, half: qkv[
        window * SPAN : (window + 1) * SPAN, which * WIDTH + half * LANES : which * WIDTH + (half + 1) * LANES
    ]
    masks = [
        score_mask(crop[0], crop[1], shifted, window, row_count) for window in range(row_count // WINDOW)
    ]
    scores = [dot_nt(piece(1, *unit), spread_heads(piece(0, *unit))) for unit in units]
    probs = []
    for (window, half), score in zip(units, scores):
        score = score * SCALE + bias_ref[layer, :, half_scores(half)] + masks[window]
        exponent = jnp.exp(score - jnp.max(score, axis=0, keepdims=True))
        low = (exponent * (1.0 / jnp.sum(exponent, axis=0, keepdims=True))).astype(BF16)
        at = (frame * (row_count // WINDOW) + window) * SPAN
        probs_ref[layer, pl.ds(pl.multiple_of(at, SPAN), SPAN), half_scores(half)] = low
        probs.append(low)
    outs = [gather_heads(dot_tn(low, piece(2, *unit))) for unit, low in zip(units, probs)]
    return jnp.concatenate(
        [jnp.concatenate(outs[i : i + 2], axis=1) for i in range(0, len(outs), 2)], axis=0
    )


def value_grads(dcontext, layer, probs_ref, frame, row_count):
    windows = []
    for window in range(row_count // WINDOW):
        rows = slice(window * SPAN, (window + 1) * SPAN)
        at = (frame * (row_count // WINDOW) + window) * SPAN
        halves = []
        for half in range(2):
            low = probs_ref[layer, pl.ds(pl.multiple_of(at, SPAN), SPAN), half_scores(half)]
            halves.append(dot(low, spread_heads(dcontext[rows, half_lanes(half)])))
        windows.append(jnp.concatenate(halves, axis=1))
    return jnp.concatenate(windows, axis=0).astype(BF16)


def attend_backward(qkv, dcontext, layer, probs_ref, frame, gathered_ref, row_count):
    units = [(window, half) for window in range(row_count // WINDOW) for half in range(2)]
    piece = lambda which, window, half: qkv[
        window * SPAN : (window + 1) * SPAN, which * WIDTH + half * LANES : which * WIDTH + (half + 1) * LANES
    ]
    dprobs = [
        dot_nt(
            piece(2, window, half),
            spread_heads(dcontext[window * SPAN : (window + 1) * SPAN, half_lanes(half)]),
        )
        for window, half in units
    ]
    lows = []
    gathered = [None, None]
    for (window, half), dprob in zip(units, dprobs):
        at = (frame * (row_count // WINDOW) + window) * SPAN
        probs = probs_ref[layer, pl.ds(pl.multiple_of(at, SPAN), SPAN), half_scores(half)].astype(F32)
        dscores = probs * (dprob - jnp.sum(probs * dprob, axis=0, keepdims=True))
        gathered_ref[layer, :, half_scores(half)] += dscores
        lows.append(dscores.astype(BF16))
    dks = [dot(low, spread_heads(piece(0, *unit))) * SCALE for unit, low in zip(units, lows)]
    dqs = [gather_heads(dot_tn(low, piece(1, *unit))) * SCALE for unit, low in zip(units, lows)]
    return [
        jnp.concatenate(
            [jnp.concatenate(d[i : i + 2], axis=1) for i in range(0, len(d), 2)], axis=0
        ).astype(BF16)
        for d in (dqs, dks)
    ]


LAST_STEPS = 6
STEPS = {
    "second_middle_back": (),
    "before_second_back": (),
    "second_back": ((0, SHRINK_ONE), (0, EXPAND_ONE)),
    "before_first_feed_back": (),
    "first_feed_back": ((1, ATTEND_ONE), (1, SHRINK_ONE), (2, EXPAND_ONE)),
    "after_shrink": (),
    "first_middle_back": (
        (0, SHRINK_ZERO), (0, SHRINK_MORE), (0, SHRINK_ONE), (0, EXPAND_ZERO), (0, EXPAND_MORE),
        (0, ATTEND_ONE), (0, EXPAND_ONE),
    ),
    "after_output": (),
    "first_back": ((2, OUTPUT_ZERO), (2, SHRINK_ZERO), (2, SHRINK_ONE), (3, SHRINK_MORE)),
    "first_back_more": (),
    "last_back": ((0, EXPAND_ZERO), (1, TRIPLE_ZERO), (3, EXPAND_ONE), (3, EXPAND_MORE)),
    "last": (
        ATTEND_ONE, OUTPUT_ZERO, SHRINK_ZERO, SHRINK_MORE, EXPAND_ZERO, SHRINK_ONE, EXPAND_ONE, SHRINK_ONE,
        TRIPLE_ZERO, EXPAND_MORE, OUTPUT_ZERO, SHRINK_ZERO, SHRINK_MORE, EXPAND_ONE, ATTEND_ONE, EXPAND_ZERO,
        ATTEND_ONE, EXPAND_MORE, EXPAND_MORE, TRIPLE_ZERO, SHRINK_ZERO, OUTPUT_ZERO, SHRINK_ZERO,
        SHRINK_MORE, SHRINK_MORE, EXPAND_ZERO, EXPAND_ZERO, TRIPLE_ZERO, TRIPLE_ZERO, OUTPUT_ZERO,
        EXPAND_ONE, OUTPUT_ZERO, EXPAND_ONE,
    ),
}


def kernel(
    places,
    crop_ref,
    gains_ref,
    table_ref,
    frames_hbm,
    latent_hbm,
    cotangent_hbm,
    *refs,
):
    wide_hbm = refs[:12]
    recurrent_hbm, readout_hbm, act_out_hbm, input_grad_hbm, sums_ref = refs[12:17]
    held = refs[17 : 17 + (12 if places.ahead else 4)]
    (
        frames_ref,
        latent_ref,
        input_grad_ref,
        recurrent_wide,
        readout_wide,
        triple_low,
        output_low,
        expand_low,
        shrink_low,
        recurrent_low,
        readout_low,
        table_pad,
        bias_ref,
        gathered_ref,
        stream_in,
        stream_one,
        stream_two,
        normed_ref,
        qkv_ref,
        probs_ref,
        context_ref,
        cell_ref,
        bend_ref,
        state_ref,
        hidden_ref,
        active_ref,
        slope_ref,
        g_ref,
        gm_ref,
        gl_ref,
        gc_ref,
        gpre_ref,
        gstate_ref,
        dpacked_ref,
        out_halo,
        in_halo,
        grads_ref,
        sum_in,
        table_own,
        table_in,
        send_sem,
        recv_sem,
        sum_send_sem,
        sum_recv_sem,
        table_send_sem,
        table_recv_sem,
        weight_sem,
        token_sem,
        result_sem,
    ) = refs[17 + len(held) :]
    lon_count, line_count = places.lon_count, places.line_count
    frame_count = crop_ref.shape[1]
    tokens = frames_ref.shape[0] // frame_count
    row_count = tokens // WINDOW
    me_lon = lax.axis_index("lon")
    ahead = lax.rem(me_lon + 1, lon_count)
    behind = lax.rem(me_lon + lon_count - 1, lon_count)

    me_batch = lax.axis_index("batch")
    core, line = lax.rem(me_batch, 2), lax.div(me_batch, 2)
    lon_peers = [lax.rem(me_lon + by, lon_count) for by in range(1, lon_count)]
    line_peers = [lax.rem(line + by, line_count) for by in range(1, line_count)]
    neighbours = [{"batch": 2 * line + 1 - core}]
    if places.few:
        for i in range(1, lon_count * line_count):
            at = lax.rem(line + i % line_count, line_count)
            lon = lax.rem(me_lon + i // line_count, lon_count)
            neighbours.append({"lon": lon, "batch": 2 * at + core})
    else:
        neighbours += [{"lon": peer} for peer in lon_peers]
        neighbours += [{"batch": 2 * peer + core} for peer in line_peers]

    barrier = pltpu.get_barrier_semaphore()
    for peer in neighbours:
        pl.semaphore_signal(barrier, inc=1, device_id=peer, device_id_type=MESH)

    def row_span(start, rows):
        return pl.ds(pl.multiple_of(start, ROW_TILE), rows)

    def members_of(kind, bit):
        if kind == "core":
            return core, [(1 - core, neighbours[0])]
        if kind == "lon":
            return me_lon, [(peer, {"lon": peer}) for peer in lon_peers]
        if kind == "both":
            others = []
            for i in range(1, lon_count * line_count):
                lon = lax.rem(me_lon + i // line_count, lon_count)
                at = lax.rem(line + i % line_count, line_count)
                others.append((lon * line_count + at, {"lon": lon, "batch": 2 * at + core}))
            return me_lon * line_count + line, others
        if kind in ("line", "gather"):
            return line, [(peer, {"batch": 2 * peer + core}) for peer in line_peers]
        mine = lax.rem(lax.div(me_lon, bit), 2)
        return mine, [(1 - mine, {"lon": me_lon + bit - 2 * bit * mine})]

    def sum_range(section, depth):
        start, rows = places.starts[places.first[section]], places.rows[section]
        for kind, bit, members in places.phases[section][:depth]:
            if kind != "gather":
                rows //= members
                start = start + members_of(kind, bit)[0] * rows
        return start, rows

    def sum_copies(section, phase):
        depth = len(places.phases[section])
        back = phase >= depth
        if back:
            kind, bit, members, depth = places.back[section][phase - depth]
        else:
            kind, bit, members = places.phases[section][phase]
            depth = phase
        start, rows = sum_range(section, depth)
        copies = []
        for i, (place, device) in enumerate(members_of(kind, bit)[1]):
            if back:
                src, dst = sums_ref.at[row_span(start, rows)], sums_ref.at[row_span(start, rows)]
            elif kind == "gather":
                own = row_span(places.inbox[section][phase] + line * rows, rows)
                src, dst = sum_in.at[own], sum_in.at[own]
            else:
                piece = rows // members
                src = grads_ref.at[row_span(start + place * piece, piece)]
                dst = sum_in.at[row_span(places.inbox[section][phase] + i * piece, piece)]
            sem = places.sems[section][phase] + i
            copies.append(
                pltpu.make_async_remote_copy(
                    src_ref=src,
                    dst_ref=dst,
                    send_sem=sum_send_sem.at[section, sem],
                    recv_sem=sum_recv_sem.at[section, sem],
                    device_id=device,
                    device_id_type=MESH,
                )
            )
        return copies

    def add_up(start, rows, source_at, count, target, own=True):
        step = math.gcd(rows, LANES)

        def body(i, unused):
            at = row_span(start + i * step, step)
            terms = [grads_ref[at]] if own else []
            terms += [sum_in[row_span(source_at + k * rows + i * step, step)] for k in range(count)]
            total = terms[0].astype(F32)
            for term in terms[1:]:
                total = total + term.astype(F32)
            target[at] = total.astype(BF16)

        lax.fori_loop(0, rows // step, body, None)

    begun = {}

    def sum_send(section, phase):
        depth = len(places.phases[section])
        if phase < depth and places.phases[section][phase][0] == "gather":
            start, rows = sum_range(section, phase)
            sum_in[row_span(places.inbox[section][phase] + line * rows, rows)] = grads_ref[row_span(start, rows)]
        for copy in sum_copies(section, phase):
            copy.start()

    def sum_start(section):
        if places.leader[section] == section:
            begun[section] = 0
            sum_send(section, 0)

    def sum_left(section):
        return len(places.phases[section]) + len(places.back[section]) - begun[section]

    def sum_step(section):
        if section not in begun or sum_left(section) == 0:
            return
        phase = begun[section]
        for copy in sum_copies(section, phase):
            copy.wait_recv()
        depth = len(places.phases[section])
        if phase < depth:
            start, rows = sum_range(section, phase + 1)
            target = grads_ref if phase < depth - 1 else sums_ref
            kind, _, members = places.phases[section][phase]
            whole = kind == "gather"
            add_up(start, rows, places.inbox[section][phase], members - (not whole), target, not whole)
        begun[section] = phase + 1
        if sum_left(section):
            sum_send(section, phase + 1)

    drained = {}

    def sum_drain(section):
        for phase in range(drained.get(section, 0), begun[section]):
            for copy in sum_copies(section, phase):
                copy.wait_send()
        drained[section] = begun[section]

    def halo(exchange, frame):
        return pltpu.make_async_remote_copy(
            src_ref=out_halo.at[exchange % 2, frame],
            dst_ref=in_halo.at[exchange % 2, frame],
            send_sem=send_sem.at[exchange, frame],
            recv_sem=recv_sem.at[exchange, frame],
            device_id={"lon": behind if exchange % 2 == 0 else ahead},
            device_id_type=MESH,
        )

    def send_halo(exchange, frame, value):
        if exchange >= 2:
            halo(exchange - 2, frame).wait_send()
        out_halo[exchange % 2, frame] = pack_half(value).astype(BF16)
        halo(exchange, frame).start()

    def take_halo(exchange, frame, own):
        halo(exchange, frame).wait_recv()
        return unpack_half(in_halo[exchange % 2, frame].astype(F32), own)

    tokens_in = [
        pltpu.make_async_copy(hbm, ref, token_sem.at[i])
        for i, (hbm, ref) in enumerate(
            ((frames_hbm, frames_ref), (latent_hbm, latent_ref), (cotangent_hbm, gm_ref))
        )
    ]

    def wide_in(which, kind, layer):
        at = 3 * which + kind if places.ahead else which
        return pltpu.make_async_copy(
            wide_hbm[3 * which + kind].at[layer], held[at].at[layer], weight_sem.at[3 * which + kind, layer]
        )

    small_in = [
        pltpu.make_async_copy(recurrent_hbm, recurrent_wide, token_sem.at[3]),
        pltpu.make_async_copy(readout_hbm, readout_wide, token_sem.at[4]),
    ]

    def weights_take(which, layer):
        wide_in(which, 0, layer).wait()
        low = (triple_low, output_low, expand_low, shrink_low)[which]
        wide = held[3 * which if places.ahead else which]
        step = 64

        def body(i, unused):
            at = pl.ds(pl.multiple_of(i * step, step), step)
            low[layer, at] = wide[layer, at].astype(BF16)

        lax.fori_loop(0, wide.shape[1] // step, body, None)

    tokens_in[0].start()
    wide_in(0, 0, 0).start()
    tokens_in[1].start()
    for copy in small_in:
        copy.start()
    for which in (1, 2, 3):
        wide_in(which, 0, 0).start()

    def make_bias(layer):
        table_pad[...] = jnp.zeros_like(table_pad)
        table_pad[:, :PAIRS] = table_ref[layer]
        gl_ref[...] = offset_onehot(layer % 2 == 1)
        bias_ref[layer] = bias_of_table(table_pad[...], gl_ref[...])

    make_bias(0)
    for copy in small_in:
        copy.wait()
    for layer in range(LAYERS):
        recurrent_low[layer] = recurrent_wide[layer].astype(BF16)
        readout_low[layer] = readout_wide[layer].astype(BF16)
    tokens_in[0].wait()
    tokens_in[1].wait()
    for which in range(4):
        weights_take(which, 0)
    for which in range(4):
        wide_in(which, 0, 1).start()
    tokens_in[2].start()
    gathered_ref[...] = jnp.zeros_like(gathered_ref)

    def span(frame):
        return pl.ds(pl.multiple_of(frame * tokens, tokens), tokens)

    def gain(layer, which):
        return gains_ref[which, layer : layer + 1, :]

    def attention_part(layer, frame, normed):
        at = span(frame)
        normed_ref[layer, at] = normed
        qkv = dot(normed, triple_low[layer]).astype(BF16)
        qkv_ref[layer, at] = qkv
        crop = (crop_ref[0, frame], crop_ref[1, frame])
        return attend_forward(qkv, bias_ref, layer, crop, probs_ref, frame, row_count)

    def middle(layer, at, stream, context, latent):
        context_ref[layer, at] = context
        one = stream + dot(context, output_low[layer])
        (stream_one, input_grad_ref)[layer][at] = one
        scaled, _ = norm_parts(one)
        cell = (scaled * gain(layer, 2)).astype(BF16)
        cell_ref[layer, at] = cell
        preact = dot_nt(cell, recurrent_low[layer, :, :WIDTH]) + dot_nt(latent, recurrent_low[layer, :, WIDTH:])
        tangent = jnp.tanh(preact)
        bend_ref[layer, at] = (1.0 - tangent * tangent).astype(BF16)
        state = tangent.astype(BF16)
        state_ref[layer, at] = state
        two = one + dot(state, readout_low[layer])
        (stream_two, g_ref)[layer][at] = two
        scaled, _ = norm_parts(two)
        hidden = (scaled * gain(layer, 1)).astype(BF16)
        hidden_ref[layer, at] = hidden
        for block in range(HIDDEN // WIDTH):
            cols = slice(block * WIDTH, (block + 1) * WIDTH)
            inner = dot(hidden, expand_low[layer, :, cols])
            square = inner * inner
            gate = 0.5 + 0.5 * jnp.tanh(inner * (GELU_C + (GELU_C * GELU_A) * square))
            active = inner * gate
            slope = gate + active * (1.0 - gate) * (2.0 * GELU_C + (6.0 * GELU_C * GELU_A) * square)
            active_ref[layer, at, cols] = active.astype(BF16)
            if layer == LAYERS - 1:
                slope = slope * slope_ref[layer, at, cols].astype(F32)
            slope_ref[layer, at, cols] = slope.astype(BF16)
        return two + dot(active_ref[layer, at], shrink_low[layer])

    def feed_back(layer, at, g):
        if layer < LAYERS - 1:
            gm_ref[at] = g.astype(BF16)
        gm = gm_ref[at]
        for block in range(HIDDEN // WIDTH):
            cols = slice(block * WIDTH, (block + 1) * WIDTH)
            dactive = dot_nt(gm, shrink_low[layer, cols])
            if layer < LAYERS - 1:
                dactive = dactive * slope_ref[layer, at, cols].astype(F32)
            slope_ref[layer, at, cols] = dactive.astype(BF16)

    def middle_back(layer, at, g, gstate):
        dhidden = dot_nt(slope_ref[layer, at], expand_low[layer])
        scaled, inverse = norm_parts((stream_two, g_ref)[layer][at])
        scaled_one, inverse_one = norm_parts((stream_one, input_grad_ref)[layer][at])
        g = g + norm_back(dhidden, gain(layer, 1), scaled, inverse)
        gl = g.astype(BF16)
        gl_ref[at] = gl
        dstate = dot_nt(gl, readout_low[layer])
        if gstate is not None:
            dstate = dstate + gstate.astype(F32)
        gpre = (dstate * bend_ref[layer, at].astype(F32)).astype(BF16)
        gpre_ref[at] = gpre
        if layer > 0:
            gstate_ref[at] = dot(gpre, recurrent_low[layer, :, WIDTH:]).astype(BF16)
        dcell = dot(gpre, recurrent_low[layer, :, :WIDTH])
        g = g + norm_back(dcell, gain(layer, 2), scaled_one, inverse_one)
        gc = g.astype(BF16)
        gc_ref[at] = gc
        g_ref[at] = g
        return dot_nt(gc, output_low[layer])

    def values_back(layer, frame, dcontext):
        dpacked_ref[span(frame), 2 * WIDTH :] = value_grads(dcontext, layer, probs_ref, frame, row_count)

    def attention_back(layer, frame, dcontext):
        at = span(frame)
        pieces = attend_backward(
            qkv_ref[layer, at], dcontext, layer, probs_ref, frame, gathered_ref, row_count
        )
        for which in range(2):
            dpacked_ref[at, which * WIDTH : (which + 1) * WIDTH] = pieces[which]

    def packed_back(layer, frame):
        return dot_nt(dpacked_ref[span(frame)], triple_low[layer])

    def stream_back(layer, frame, g, stream, dnormed):
        scaled, inverse = norm_parts(stream)
        return g + norm_back(dnormed, gain(layer, 0), scaled, inverse)

    def put_blocks(start, value):
        rows = value.shape[0]
        for block in range(value.shape[1] // LANES):
            grads_ref[start + block * rows : start + (block + 1) * rows] = value[
                :, half_lanes(block)
            ].astype(BF16)

    def put_rows(start, total_rows, row, value):
        rows = value.shape[0]
        for block in range(value.shape[1] // LANES):
            at = start + block * total_rows + row
            grads_ref[at : at + rows] = value[:, half_lanes(block)].astype(BF16)

    def shrink_grads(layer):
        for block in range(HIDDEN // WIDTH):
            cols = slice(block * WIDTH, (block + 1) * WIDTH)
            put_rows(
                places.shrink[layer], HIDDEN, block * WIDTH, dot_tn(active_ref[layer, :, cols], gm_ref[...])
            )

    def expand_grads(layer):
        for block in range(HIDDEN // WIDTH):
            cols = slice(block * WIDTH, (block + 1) * WIDTH)
            put_blocks(
                places.expand[layer] + 2 * block * WIDTH, dot_tn(hidden_ref[layer], slope_ref[layer, :, cols])
            )

    def small_grads(layer, latent):
        near = dot_tn(gpre_ref[...], cell_ref[layer])
        far = dot_tn(gpre_ref[...], latent)
        far = jnp.concatenate([far, jnp.zeros((LATENT, LANES - LATENT), F32)], axis=1)
        readout = dot_tn(state_ref[layer], gl_ref[...])
        return [near[:, :LANES], near[:, LANES:], far, readout[:, :LANES], readout[:, LANES:]]

    def table_pieces(layer):
        gl_ref[...] = offset_onehot(layer % 2 == 1)
        table = table_of_bias(gathered_ref[layer], gl_ref[...])
        return [table[:, :LANES], table[:, LANES:]]

    def put_pieces(start, pieces):
        used = sum(piece.shape[0] for piece in pieces)
        value = jnp.concatenate(pieces, axis=0).astype(BF16)
        grads_ref[start : start + used] = value
        return start + used

    def clear_spare(section):
        if section in places.spare:
            clear_rows(*places.spare[section])

    def clear_rows(start, stop):
        if stop > start:
            grads_ref[start:stop] = jnp.zeros((stop - start, LANES), BF16)

    def output_grads(layer):
        put_blocks(places.output[layer], dot_tn(context_ref[layer], gc_ref[...]))

    def triple_grads(layer, blocks):
        for block in blocks:
            cols = slice(block * WIDTH, (block + 1) * WIDTH)
            put_blocks(places.triple[layer][block], dot_tn(normed_ref[layer], dpacked_ref[:, cols]))

    def table_core():
        here = row_span(0, TABLE_ROWS)
        return pltpu.make_async_remote_copy(
            src_ref=table_own.at[here],
            dst_ref=table_in.at[row_span(members * TABLE_ROWS, TABLE_ROWS)],
            send_sem=table_send_sem.at[0],
            recv_sem=table_recv_sem.at[0],
            device_id=neighbours[0],
            device_id_type=MESH,
        )

    members = lon_count * line_count

    def table_copies():
        mine = row_span((me_lon * line_count + line) * TABLE_ROWS, TABLE_ROWS)
        return [
            pltpu.make_async_remote_copy(
                src_ref=table_in.at[mine],
                dst_ref=table_in.at[mine],
                send_sem=table_send_sem.at[1 + i],
                recv_sem=table_recv_sem.at[1 + i],
                device_id=device,
                device_id_type=MESH,
            )
            for i, (_, device) in enumerate(members_of("both", 0)[1])
        ]

    def table_start():
        table_own[...] = jnp.concatenate(table_pieces(0), axis=0).astype(BF16)
        table_core().start()

    def table_spread():
        table_core().wait_recv()
        other = table_in[members * TABLE_ROWS : (members + 1) * TABLE_ROWS].astype(F32)
        mine = row_span((me_lon * line_count + line) * TABLE_ROWS, TABLE_ROWS)
        table_in[mine] = (table_own[...].astype(F32) + other).astype(BF16)
        for copy in table_copies():
            copy.start()

    def table_take():
        for copy in table_copies():
            copy.wait_recv()
        total = table_in[:TABLE_ROWS].astype(F32)
        for i in range(1, members):
            total = total + table_in[i * TABLE_ROWS : (i + 1) * TABLE_ROWS].astype(F32)
        sums_ref[places.table[0] : places.table[0] + TABLE_ROWS] = total.astype(BF16)

    def loop(body, steps=(), count=frame_count):
        def whole(frame, unused):
            body(frame)
            for after in range(count):
                here = [section for when, section in steps if when == after]
                if here:

                    @pl.when(frame == after)
                    def _(here=here):
                        sum_steps(*here)

        lax.fori_loop(0, count, whole, None)

    def sum_steps(*sections):
        for section in sections:
            sum_step(section)

    paired = 2 - frame_count % 2
    pairs = frame_count // paired

    def pair_span(pair):
        return pl.ds(pl.multiple_of(pair * paired * tokens, paired * tokens), paired * tokens)

    def frames_of(pair):
        return [(pair * paired + i, slice(i * tokens, (i + 1) * tokens)) for i in range(paired)]

    def first_layer(pair):
        at = pair_span(pair)
        stream = frames_ref[at].astype(F32)
        scaled, _ = norm_parts(stream)
        normed = (scaled * gain(0, 0)).astype(BF16)
        context = jnp.concatenate(
            [attention_part(0, frame, normed[rows]).astype(BF16) for frame, rows in frames_of(pair)], axis=0
        )
        stream = middle(0, at, stream, context, latent_ref[at])
        stream_in[at] = stream
        scaled, _ = norm_parts(stream)
        normed = scaled * gain(1, 0)
        normed_ref[1, at] = normed.astype(BF16)

        @pl.when(pair == 0)
        def _():
            pl.semaphore_wait(barrier, len(neighbours))

        for frame, rows in frames_of(pair):
            send_halo(0, frame, normed[rows])

    loop(first_layer, count=pairs)
    make_bias(1)
    for which in range(4):
        weights_take(which, 1)
    tokens_in[2].wait()
    if places.ahead:
        for layer in (1, 0):
            for which in range(4):
                for kind in (1, 2):
                    wide_in(which, kind, layer).start()

    def second_attention(frame):
        at = span(frame)
        normed = take_halo(0, frame, normed_ref[1, at].astype(F32))
        context = attention_part(1, frame, rows_ahead(normed).astype(BF16))
        context = rows_behind(context)
        context_ref[1, at] = context.astype(BF16)
        send_halo(1, frame, context)

    loop(second_attention)

    def second_feed_back(pair):
        feed_back(1, pair_span(pair), None)

    loop(second_feed_back, count=pairs)

    def second_middle(pair):
        at = pair_span(pair)
        context = jnp.concatenate(
            [
                take_halo(1, frame, context_ref[1, span(frame)].astype(F32)).astype(BF16)
                for frame, _ in frames_of(pair)
            ],
            axis=0,
        )
        dpacked_ref[at, WIDTH : 2 * WIDTH] = middle(1, at, stream_in[at], context, state_ref[0, at]).astype(BF16)

    loop(second_middle, count=pairs)
    act_out = pltpu.make_async_copy(dpacked_ref.at[:, pl.ds(WIDTH, WIDTH)], act_out_hbm, result_sem.at[frame_count])
    act_out.start()

    def second_middle_back(pair):
        at = pair_span(pair)
        dcontext = middle_back(1, at, gm_ref[at].astype(F32), None)
        dpacked_ref[at, :WIDTH] = dcontext.astype(BF16)
        for frame, rows in frames_of(pair):
            send_halo(2, frame, dcontext[rows])

    loop(second_middle_back, STEPS["second_middle_back"], pairs)
    shrink_grads(1)
    sum_start(SHRINK_ONE)
    expand_grads(1)
    sum_start(EXPAND_ONE)
    output_grads(1)
    early_one = put_pieces(places.early[1], small_grads(1, state_ref[0]))
    sum_steps(*STEPS["before_second_back"])
    act_out.wait()

    def second_back(frame):
        at = span(frame)
        dcontext = take_halo(2, frame, dpacked_ref[at, :WIDTH].astype(F32))
        dcontext = rows_ahead(dcontext).astype(BF16)
        values_back(1, frame, dcontext)
        attention_back(1, frame, dcontext)
        dnormed = rows_behind(packed_back(1, frame))
        gc_ref[at] = dnormed.astype(BF16)
        send_halo(3, frame, dnormed)

    loop(second_back, STEPS["second_back"])
    triple_grads(1, (0, 1, 2))
    clear_spare(ATTEND_ONE)
    sum_start(ATTEND_ONE)
    clear_rows(put_pieces(early_one, table_pieces(1)), places.early[1] + SMALL_ROWS)
    sum_steps(*STEPS["before_first_feed_back"])

    def first_feed_back(frame):
        at = span(frame)
        dnormed = take_halo(3, frame, gc_ref[at].astype(F32))
        g = stream_back(1, frame, g_ref[at], stream_in[at], dnormed)
        g_ref[at] = g
        feed_back(0, at, g)

    loop(first_feed_back, STEPS["first_feed_back"])
    shrink_grads(0)
    sum_start(SHRINK_ZERO)
    sum_start(SHRINK_MORE)
    sum_steps(*STEPS["after_shrink"])
    expand_grads(0)
    sum_start(EXPAND_ZERO)
    sum_start(EXPAND_MORE)

    def first_middle_back(pair):
        at = pair_span(pair)
        dcontext = middle_back(0, at, g_ref[at], gstate_ref[at]).astype(BF16)
        dpacked_ref[at, :WIDTH] = dcontext
        for frame, rows in frames_of(pair):
            values_back(0, frame, dcontext[rows])

    loop(first_middle_back, STEPS["first_middle_back"], pairs)
    output_grads(0)
    triple_grads(0, (2,))
    clear_rows(put_pieces(places.early[0], small_grads(0, latent_ref[...])), places.early[1])
    clear_spare(OUTPUT_ZERO)
    sum_start(OUTPUT_ZERO)
    sum_steps(*STEPS["after_output"])

    def grad_out(frame):
        at = span(frame)
        return pltpu.make_async_copy(input_grad_ref.at[at], input_grad_hbm.at[at], result_sem.at[frame])

    def first_back(frame):
        attention_back(0, frame, dpacked_ref[span(frame), :WIDTH])

    loop(first_back, STEPS["first_back"])
    triple_grads(0, (0, 1))
    if not places.few:
        put_pieces(places.table[0], table_pieces(0))
        clear_spare(TRIPLE_ZERO)
    sum_start(TRIPLE_ZERO)
    if places.few:
        table_start()

    def last_back(frame):
        at = span(frame)
        stream = frames_ref[at].astype(F32)
        input_grad_ref[at] = stream_back(0, frame, g_ref[at], stream, packed_back(0, frame))
        grad_out(frame).start()

    loop(last_back, STEPS["last_back"])
    if places.few:
        table_spread()
    sum_steps(*STEPS["last"][:-LAST_STEPS])

    def drain(frame, unused):
        for exchange in (2, 3):
            halo(exchange, frame).wait_send()
        grad_out(frame).wait()

    lax.fori_loop(0, frame_count, drain, None)
    if places.few:
        table_take()
        table_core().wait_send()
        for copy in table_copies():
            copy.wait_send()
    if places.ahead:
        for layer in (1, 0):
            for which in range(4):
                for kind in (1, 2):
                    wide_in(which, kind, layer).wait()
    for section in begun:
        sum_drain(section)
    sum_steps(*STEPS["last"][-LAST_STEPS:])
    while any(sum_left(section) for section in begun):
        sum_steps(*begun)
    for section in begun:
        sum_drain(section)


def flat_tokens(array):
    return array.reshape(-1, array.shape[-1])


def in_hbm(array):
    return pltpu.with_memory_space_constraint(array, pltpu.HBM)


def layers_step(frames, latent, crop_band, cotangent, parameters, places):
    frame_count, row_count, col_count, features = frames.shape
    count = frame_count * row_count * col_count
    tokens = row_count * col_count
    vmem = pl.BlockSpec(memory_space=pltpu.VMEM)
    hbm = pl.BlockSpec(memory_space=pltpu.HBM)
    both = lambda *shape: pltpu.VMEM((LAYERS,) + shape, BF16)
    one = lambda *shape: pltpu.VMEM(shape, BF16)
    wide = lambda *shape: pltpu.VMEM(shape, F32)
    scratch = [
        one(count, WIDTH),
        one(count, LATENT),
        wide(count, WIDTH),
        wide(LAYERS, LATENT, WIDTH + LATENT),
        wide(LAYERS, LATENT, WIDTH),
        both(WIDTH, 3 * WIDTH),
        both(WIDTH, WIDTH),
        both(WIDTH, HIDDEN),
        both(HIDDEN, WIDTH),
        both(LATENT, WIDTH + LATENT),
        both(LATENT, WIDTH),
        wide(HEADS, WIDTH),
        wide(LAYERS, SPAN, HEADS * SPAN),
        wide(LAYERS, SPAN, HEADS * SPAN),
        wide(count, WIDTH),
        wide(count, WIDTH),
        wide(count, WIDTH),
        both(count, WIDTH),
        both(count, 3 * WIDTH),
        both(count, HEADS * SPAN),
        both(count, WIDTH),
        both(count, WIDTH),
        both(count, LATENT),
        both(count, LATENT),
        both(count, WIDTH),
        both(count, HIDDEN),
        both(count, HIDDEN),
        wide(count, WIDTH),
        one(count, WIDTH),
        one(count, WIDTH),
        one(count, WIDTH),
        one(count, LATENT),
        one(count, LATENT),
        one(count, 3 * WIDTH),
        one(2, frame_count, tokens // 2, WIDTH),
        one(2, frame_count, tokens // 2, WIDTH),
        one(places.total, LANES),
        one(places.inbox_rows, LANES),
        one(TABLE_ROWS, LANES),
        one((places.few_members + 1) * TABLE_ROWS, LANES),
        pltpu.SemaphoreType.DMA((4, frame_count)),
        pltpu.SemaphoreType.DMA((4, frame_count)),
        pltpu.SemaphoreType.DMA((len(SECTION_ROWS), places.most_sems)),
        pltpu.SemaphoreType.DMA((len(SECTION_ROWS), places.most_sems)),
        pltpu.SemaphoreType.DMA((places.few_members,)),
        pltpu.SemaphoreType.DMA((places.few_members,)),
        pltpu.SemaphoreType.DMA((12, LAYERS)),
        pltpu.SemaphoreType.DMA((5,)),
        pltpu.SemaphoreType.DMA((frame_count + 1,)),
    ]
    wide_parameters = parameters[:12]
    recurrent, readout, gains, table = parameters[12::3]
    held = [a for i, a in enumerate(wide_parameters) if places.ahead or i % 3 == 0]
    given = (frames, latent, cotangent)
    outs = pl.pallas_call(
        functools.partial(kernel, places),
        out_shape=(
            pltpu.HBM((count, WIDTH), BF16),
            pltpu.HBM((count, WIDTH), F32),
            pltpu.VMEM((places.sum_rows, LANES), BF16),
        )
        + tuple(pltpu.VMEM(a.shape, F32) for a in held),
        in_specs=[pl.BlockSpec(memory_space=pltpu.SMEM), vmem, vmem] + [hbm] * 17,
        out_specs=(hbm, hbm, vmem) + (vmem,) * len(held),
        scratch_shapes=scratch,
        compiler_params=pltpu.CompilerParams(
            collective_id=0, has_side_effects=True, vmem_limit_bytes=places.grant
        ),
        name="swin_step",
    )(
        crop_band.T,
        gains,
        table,
        *(in_hbm(flat_tokens(a)) for a in given),
        *(in_hbm(a) for a in wide_parameters),
        in_hbm(recurrent),
        in_hbm(readout),
    )
    return outs[0], outs[1], outs[2], outs[3:]


def update_kernel(scale, places, sums, result_hbm, grad_hbm, *refs):
    count = 24
    given, result_out, grad_out = refs[:count], refs[count], refs[count + 1]
    made, held = refs[count + 2 : 2 * count + 2], refs[2 * count + 2 : 3 * count + 2]
    result_held, products, pass_sem, in_sem, out_sem = refs[3 * count + 2 :]
    triple, output, expand, shrink, recurrent, readout, gains, table = range(8)
    grad_held = held[3 * shrink].at[0]

    passing_in = [
        pltpu.make_async_copy(result_hbm, result_held, pass_sem.at[0]),
        pltpu.make_async_copy(grad_hbm, grad_held, pass_sem.at[1]),
    ]
    passing_out = [
        pltpu.make_async_copy(result_held, result_out, pass_sem.at[2]),
        pltpu.make_async_copy(grad_held, grad_out, pass_sem.at[3]),
    ]
    units = [
        (shrink, 1),
        (expand, 1),
        (triple, 1),
        (output, 1),
        (shrink, 0),
        (expand, 0),
        (output, 0),
        (triple, 0),
        (recurrent, None),
        (readout, None),
        (table, None),
        (gains, None),
    ]

    def part(ref, layer):
        return ref if layer is None else ref.at[layer]

    def is_held(which, kind):
        return which < recurrent and (places.ahead or kind == 0)

    def coming(index):
        which, layer = units[index]
        return [
            pltpu.make_async_copy(
                part(given[3 * which + i], layer), part(held[3 * which + i], layer), in_sem.at[index, i]
            )
            for i in range(3)
            if not is_held(which, i)
        ]

    def going(index):
        which, layer = units[index]
        return [
            pltpu.make_async_copy(
                part(held[3 * which + i], layer), part(made[3 * which + i], layer), out_sem.at[index, i]
            )
            for i in range(3)
        ]

    for index in range(len(units)):
        for copy in coming(index):
            copy.start()
    for copy in passing_in:
        copy.start()

    def change(which, at, summed):
        old = [(given if is_held(which, i) else held)[3 * which + i][at] for i in range(3)]
        weight, moment, average = held[3 * which : 3 * which + 3]
        gradient = summed.astype(F32) * scale
        velocity = MOMENTUM_RATE * old[1] + gradient
        updated = old[0] - LEARN_RATE * (gradient + MOMENTUM_RATE * velocity)
        average[at] = AVERAGE_DECAY * old[2] + (1.0 - AVERAGE_DECAY) * updated
        weight[at] = updated
        moment[at] = velocity
        return old[0].astype(BF16).astype(F32) * gradient

    def change_blocks(which, layer, starts, rows, norm=None):
        step = 256 // len(starts)
        step = 32 if step < 64 else min(step, 128)

        def body(i, unused):
            row = pl.multiple_of(i * step, step)
            total = None
            for block, start in enumerate(starts):
                summed = sums[pl.ds(start + row, step)]
                product = change(which, (layer, pl.ds(row, step), half_lanes(block)), summed)
                total = product if total is None else total + product
            if norm is not None:
                products[layer, norm, pl.ds(row, step)] = total

        lax.fori_loop(0, rows // step, body, None)

    def sum_lanes(ones, value):
        rows = value.shape[0]
        parts = three_parts(value)
        sums_of = [dot_nt(ones, parts[i * rows : (i + 1) * rows])[:1] for i in range(3)]
        return sums_of[0] + (sums_of[1] + sums_of[2])

    cell_rows = []

    def blocks_at(start, rows, count):
        return [start + i * rows for i in range(count)]

    for index, (which, layer) in enumerate(units):
        for copy in coming(index):
            copy.wait()
        if which == expand:
            change_blocks(expand, layer, blocks_at(places.expand[layer], WIDTH, HIDDEN // LANES), WIDTH, 1)
        elif which == shrink:
            change_blocks(shrink, layer, blocks_at(places.shrink[layer], HIDDEN, 2), HIDDEN)
        elif which == output:
            change_blocks(output, layer, blocks_at(places.output[layer], WIDTH, 2), WIDTH)
        elif which == triple:
            starts = [at for start in places.triple[layer] for at in blocks_at(start, WIDTH, 2)]
            change_blocks(triple, layer, starts, WIDTH, 0)
        else:
            for each in range(LAYERS):
                at = places.early[each]
                if which == recurrent:
                    rows = []
                    for block in range(3):
                        lanes = slice(block * LANES, min((block + 1) * LANES, WIDTH + LATENT))
                        summed = sums[pl.ds(at + block * LATENT, LATENT)][:, : lanes.stop - lanes.start]
                        product = change(which, (each, slice(0, LATENT), lanes), summed)
                        rows.append(jnp.sum(product, axis=0, keepdims=True))
                    cell_rows.append(jnp.concatenate(rows[:2], axis=1))
                elif which == readout:
                    for block in range(2):
                        rows = sums[pl.ds(at + 96 + block * LATENT, LATENT)]
                        change(which, (each, slice(0, LATENT), half_lanes(block)), rows)
                elif which == table:
                    rows = sums[pl.ds(places.table[each], TABLE_ROWS)].astype(F32)
                    change(which, (each, slice(0, HEADS), slice(0, LANES)), rows[:8])
                    change(which, (each, slice(0, HEADS), slice(LANES, PAIRS)), rows[8:16, : PAIRS - LANES])
                else:
                    ones = jnp.ones((8, LANES), BF16)
                    for norm in range(3):
                        gain_row = held[3 * gains][norm, each : each + 1, :]
                        if norm == 2:
                            total = cell_rows[each]
                        else:
                            total = sum_lanes(ones, products[each, norm])
                        change(which, (norm, slice(each, each + 1)), total / (gain_row * scale))
        for copy in going(index):
            copy.start()
        if index == 1:
            for copy in passing_in:
                copy.wait()
            for copy in passing_out:
                copy.start()
        if index == 3:
            for copy in passing_out:
                copy.wait()
    for index in range(len(units)):
        for copy in going(index):
            copy.wait()


def update_step(sums, result, input_grad, held, parameters, scale, places):
    hbm = pl.BlockSpec(memory_space=pltpu.HBM)
    vmem = pl.BlockSpec(memory_space=pltpu.VMEM)
    in_vmem = lambda a: pltpu.with_memory_space_constraint(a, pltpu.VMEM)
    held = list(held)
    given, specs = [], []
    for i, a in enumerate(parameters):
        if i < 12 and (places.ahead or i % 3 == 0):
            given.append(in_vmem(held.pop(0)))
            specs.append(vmem)
        else:
            given.append(in_hbm(a))
            specs.append(hbm)
    like = lambda a: pltpu.HBM(a.shape, a.dtype)
    return pl.pallas_call(
        functools.partial(update_kernel, scale, places),
        out_shape=(like(result), like(input_grad)) + tuple(like(a) for a in parameters),
        in_specs=[vmem, hbm, hbm] + specs,
        out_specs=(hbm,) * (2 + len(parameters)),
        scratch_shapes=[pltpu.VMEM(a.shape, F32) for a in parameters]
        + [
            pltpu.VMEM(result.shape, result.dtype),
            pltpu.VMEM((LAYERS, 2, WIDTH, LANES), F32),
            pltpu.SemaphoreType.DMA((4,)),
            pltpu.SemaphoreType.DMA((12, 3)),
            pltpu.SemaphoreType.DMA((12, 3)),
        ],
        compiler_params=pltpu.CompilerParams(vmem_limit_bytes=20 * 2**20),
        name="nesterov_step",
    )(in_vmem(sums), in_hbm(result), in_hbm(input_grad), *given)


def per_device(frames, latent_init, crop_band, cotangent, *parameters):
    shape = frames.shape
    lon_count, batch_count = lax.axis_size("lon"), lax.axis_size("batch")
    places = Places(lon_count, batch_count)
    turned = {4: (0, 2, 1), 6: (1, 0, 2)}
    parameters = [
        a.transpose(turned[i // 3]) if i // 3 in turned else a for i, a in enumerate(parameters)
    ]
    result, input_grad, sums, held = layers_step(
        frames, latent_init, crop_band, cotangent, parameters, places
    )
    tokens = shape[0] * shape[1] * shape[2] * lon_count * batch_count
    result, input_grad, *updated = update_step(
        sums, result, input_grad, held, parameters, float(tokens) ** (-0.5), places
    )
    updated = [a.transpose(turned[i // 3]) if i // 3 in turned else a for i, a in enumerate(updated)]
    return (result.reshape(shape), input_grad.reshape(shape), *updated)


def solution(mesh):
    split = P("batch", None, "lon", None)
    return jax.shard_map(
        per_device,
        mesh=mesh,
        in_specs=(split, split, P("batch", None), split) + (P(),) * 24,
        out_specs=(split, split) + (P(),) * 24,
        check_vma=False,
    )
```
